256 devices in a mesh: grp: 2 (over core), row: 8 (over y_lo, x), tp: 16 (over z, y_hi).
Axes of the slice: x: 4, y: 4 (y_hi: 2, y_lo: 2; y = y_hi * 2 + y_lo), z: 8, core: 2. Of those that a mesh axis runs over, the one named last changes fastest.
Arguments:
- frame: bfloat16 [128, 16, 5120], P(('grp', 'row'), 'tp'), may hold values from -6 to 6
- cache: bfloat16 [128, 16, 512, 256], P(('grp', 'row'), 'tp'), may hold values from -6 to 6
- actions: int32 [128, 4], P(('grp', 'row')), may hold values from 0 to 17
- owners: int32 [128, 1], P(('grp', 'row')), may hold values from 0 to 7; in each aligned block of 8 rows (0 to 7, 8 to 15, ...) at most 2 rows name the same one
- attn_gain: float32 [5120], replicated, may hold values from 0.1 to 1.9
- w_query: bfloat16 [5120, 4096], P(None, 'tp'), may hold values from -1 to 1
- w_keyval: bfloat16 [5120, 2048], P(None, 'tp'), may hold values from -0.078125 to 0.078125
- w_out: bfloat16 [4096, 5120], P('tp'), may hold values from -0.09375 to 0.09375
- action_table: bfloat16 [18, 5120], replicated, may hold values from -6 to 6
- policy_in: bfloat16 [8, 5120, 2048], P('row', None, 'tp'), may hold values from -0.078125 to 0.078125
- policy_mid: bfloat16 [8, 2048, 2048], P('row', 'tp'), may hold values from -0.125 to 0.125
- policy_head: bfloat16 [8, 2048, 18], P('row'), may hold values from -0.25 to 0.25
- policy_value: bfloat16 [8, 2048], P('row'), may hold values from -0.125 to 0.125
Outputs:
- latents: bfloat16 [128, 16, 5120], P(('grp', 'row'), 'tp')
- log_probs: float32 [128, 4, 18], P(('grp', 'row'))
- values: float32 [128, 4], P(('grp', 'row'))
The draws below stay inside these ranges and needn't reach their ends.
Inputs may be any that keep to these rules, and one draw needn't show every extreme that they name: `owners`: among the 8 rollouts of one device (aligned blocks of 8 rows), no policy is named by more than 2.
All inputs are finite; a program needn't handle non-finite values.
Results may differ from the reference program's by a relative error of at most 0.018.
Values may be sent and summed in bfloat16 or wider, within the bound.
A program may use at most 128 MiB of HBM per device.

```python
import math
import jax
import jax.numpy as jnp
import numpy as np
from jax import lax

D = 5120
QH = 32
KVH = 8
HD = 128
PH = 2048
ACTIONS = 18
FRAME = 16
CACHE = 1024
STEPS = 4
R_DEV = 8
CAP = 2
SPLIT = 2
ROLLOUTS = 128
POLICIES = 8


ALIGN = 0.1


PEAK = 6.0


NEAR_PEAK = 5.9375


def planted(key):
    sign_u = jnp.where(jax.random.bernoulli(jax.random.fold_in(key, 101), 0.5, (D,)), 1.0, -1.0).astype(jnp.float32)
    sign_v = jnp.where(jax.random.bernoulli(jax.random.fold_in(key, 102), 0.5, (KVH, HD)), 1.0, -1.0).astype(jnp.float32)
    strength = jax.random.uniform(jax.random.fold_in(key, 103), (ROLLOUTS,), jnp.float32, 0.0, 1.0)
    return (sign_u, sign_v, strength)


def draw_frame(key, part):
    sign_u, sign_v, strength = planted(key)
    key = jax.random.fold_in(key, 1)
    full_shape = (ROLLOUTS, FRAME, D)
    rough_part = jax.random.truncated_normal(key, -5.0, 5.0, full_shape, jnp.float32)
    return (rough_part + strength[:, None, None] * sign_u[None, None, :]).astype(jnp.bfloat16)


def draw_cache(key, part):
    sign_u, sign_v, strength = planted(key)
    key = jax.random.fold_in(key, 4)
    full_shape = (ROLLOUTS, KVH, CACHE, 2 * HD)
    rough_part = jax.random.truncated_normal(key, -5.0, 5.0, full_shape, jnp.float32)
    spot_one = jax.random.randint(jax.random.fold_in(key, 5), (ROLLOUTS, KVH), 0, CACHE)
    spot_two = (spot_one + jax.random.randint(jax.random.fold_in(key, 6), (ROLLOUTS, KVH), 1, CACHE)) % CACHE
    position = jnp.arange(CACHE)
    hit_one = (position[None, None, :] == spot_one[..., None])[..., None]
    hit_two = (position[None, None, :] == spot_two[..., None])[..., None]
    aligned = sign_v[None, :, None, :]
    key_part = jnp.where(hit_one, PEAK * aligned, jnp.where(hit_two, NEAR_PEAK * aligned, rough_part[..., :HD]))
    whole = jnp.concatenate([key_part, rough_part[..., HD:]], axis=-1)
    return whole.reshape(ROLLOUTS, KVH * SPLIT, CACHE // SPLIT, 2 * HD).astype(jnp.bfloat16)


def draw_w_query(key, part):
    sign_u, sign_v, strength = planted(key)
    key = jax.random.fold_in(key, 7)
    full_shape = (D, QH * HD)
    rough_part = jax.random.truncated_normal(key, -4.0, 4.0, full_shape, jnp.float32)
    per_group = QH // KVH
    leading = (jnp.arange(QH) % per_group == 0).astype(jnp.float32)
    pattern = jnp.repeat(sign_v, per_group, axis=0) * leading[:, None]
    weights = (rough_part + ALIGN * sign_u[:, None] * pattern.reshape(1, QH * HD)) * D ** (-0.5)
    return weights.astype(jnp.bfloat16)


def place_ends(entries, key, least, top_value):
    longest = entries.shape.index(max(entries.shape))
    spots = []
    for shift in (0, 1):
        where = [jax.random.randint(jax.random.fold_in(key, axis), (), 0, length) for axis, length in enumerate(entries.shape)]
        where[longest] = (where[longest] + shift) % entries.shape[longest]
        spots.append(tuple(where))
    return entries.at[spots[0]].set(least).at[spots[1]].set(top_value)


def block_scale(key, dims, pieces, low, largest):
    loudness = 1.0
    for dim, shards_of in pieces:
        draws = jax.random.uniform(jax.random.fold_in(jax.random.fold_in(key, 6), dim), (shards_of,), jnp.float32, low / len(pieces), largest / len(pieces))
        loudness = loudness * jnp.repeat(jnp.exp(draws), dims[dim] // shards_of).reshape((-1,) + (1,) * (len(dims) - 1 - dim))
    return loudness


def assign_block(rng, own, number, rows, count, top, bound, skew):
    ranking = jax.random.permutation(rng, count)
    heavy_load, common = shares(count, rows * top, bound, skew, True), shares(count, rows * top, bound, skew, False)
    places = jnp.arange(count)

    def named(tallies, offset_by):
        used = int((tallies > 0).sum())
        fixed = max(1, used // 4)
        shifted = fixed + (places - fixed + offset_by * (used - fixed)) % max(1, count - fixed)
        return jnp.zeros((count,), jnp.int32).at[ranking[jnp.where(places < fixed, places, shifted)]].set(jnp.asarray(tallies, jnp.int32))

    tallies = jnp.where(number % 4 == 0, named(heavy_load, number // 4), named(common, number - number // 4 - 1))
    mixed = jax.random.permutation(jax.random.fold_in(own, 3), count)
    giver, sink = mixed[0:count // 2 * 2:2], mixed[1:count // 2 * 2:2]
    room = jnp.minimum(tallies[giver] - 1, bound - tallies[sink]) // 2
    room = jnp.where((giver == ranking[0]) | (sink == ranking[0]) | (tallies[sink] == 0), 0, jnp.maximum(room, 0))
    shifted = jax.random.randint(jax.random.fold_in(own, 4), (count // 2,), 0, 1 << 20) % (room + 1)
    tallies = tallies.at[giver].add(-shifted).at[sink].add(shifted)
    labels = jnp.searchsorted(jnp.cumsum(tallies), jnp.arange(rows * top), side="right").astype(jnp.int32)
    listing = labels.reshape(top, rows).T
    listing = listing[jax.random.permutation(jax.random.fold_in(own, 1), rows)]
    offset_by = jax.random.randint(jax.random.fold_in(own, 2), (rows, 1), 0, top)
    return jnp.take_along_axis(listing, (jnp.arange(top)[None, :] + offset_by) % top, axis=1)


def shares(count, total, bound, slope, full):
    loads = [(1 << 20) // math.isqrt(grade ** slope) + 1 for grade in range(1, count + 1)]
    largest = bound if full else min(bound, max(-(-total // count), total * loads[0] // sum(loads)))
    least = 1 if total - largest >= count - 1 else 0
    given, rest = [largest] + [least] * (count - 1), total - largest - least * (count - 1)
    while rest > 0:
        movable = [i for i in range(1, count) if given[i] < largest] or [i for i in range(1, count) if given[i] < bound]
        pool, remaining = sum([loads[i] for i in movable]), rest
        for i in movable:
            more = min(bound - given[i], max(1, remaining * loads[i] // pool), rest)
            given[i] = given[i] + more
            rest = rest - more
    return np.array(given)


def noise(own_key, extent, width, limit, shards=(), kind=jnp.bfloat16):
    entries = width * jax.random.normal(own_key, extent, jnp.float32)
    if shards:
        entries = entries * block_scale(own_key, extent, shards, -0.22, 0.18)
    return jnp.clip(entries, -limit, limit).astype(kind)


def setup_inputs(seed: int = 0) -> dict:
    seeds = jax.random.split(jax.random.key(seed), 14)
    frame = draw_frame(jax.random.fold_in(seeds[13], 71), 0)
    cache = draw_cache(jax.random.fold_in(seeds[13], 71), 0)
    actions = place_ends(jax.random.randint(seeds[2], (ROLLOUTS, STEPS), 0, ACTIONS), jax.random.fold_in(seeds[2], 1), 0, ACTIONS - 1).astype(jnp.int32)
    owners_keys = jax.random.split(jax.random.fold_in(seeds[3], 1), ROLLOUTS // R_DEV)
    owners_turns = jax.random.permutation(jax.random.fold_in(seeds[3], 3), ROLLOUTS // R_DEV)
    owners = jax.vmap(lambda own, number: assign_block(jax.random.fold_in(seeds[3], 2), own, number, R_DEV, POLICIES, 1, CAP, 1))(owners_keys, owners_turns).reshape((ROLLOUTS, 1))
    attn_gain = jnp.clip(1.0 + 0.18 * jax.random.normal(seeds[4], (D,), jnp.float32), 0.1, 1.9)
    w_query = draw_w_query(jax.random.fold_in(seeds[13], 71), 0)
    w_keyval = noise(seeds[6], (D, 2 * KVH * HD), D ** -0.5, 0.078125, ((1, 16),))
    w_out = noise(seeds[7], (QH * HD, D), (QH * HD) ** -0.5, 0.09375, ((0, 16),))
    action_table = noise(seeds[8], (ACTIONS, D), 1.0, 6.0)
    policy_in = noise(seeds[9], (POLICIES, D, PH), D ** -0.5, 0.078125, ((0, 8), (2, 16)))
    policy_mid = noise(seeds[10], (POLICIES, PH, PH), PH ** -0.5, 0.125, ((0, 8), (1, 16)))
    policy_head = noise(seeds[11], (POLICIES, PH, ACTIONS), (PH // 4) ** -0.5, 0.25, ((0, 8),))
    policy_value = noise(seeds[12], (POLICIES, PH), PH ** -0.5, 0.125, ((0, 8),))
    return {"frame": frame, "cache": cache, "actions": actions, "owners": owners, "attn_gain": attn_gain, "w_query": w_query, "w_keyval": w_keyval, "w_out": w_out, "action_table": action_table, "policy_in": policy_in, "policy_mid": policy_mid, "policy_head": policy_head, "policy_value": policy_value}


EPS = 1e-05

def rms_rows(values):
    return values * lax.rsqrt(lax.optimization_barrier(jnp.mean(values * values, axis=-1, keepdims=True)) + EPS)

def attend_rollout(args, step):
    query, cached, stash = args
    keys_cache = cached[..., :HD].astype(jnp.float32)
    values_cache = cached[..., HD:].astype(jnp.float32)
    keys_new = stash[..., :HD].astype(jnp.float32)
    values_new = stash[..., HD:].astype(jnp.float32)
    grouped = query.astype(jnp.float32)
    score_cache = jnp.einsum('fkgd,kcd->kgfc', grouped, keys_cache)
    score_new = jnp.einsum('fkgd,jkd->kgfj', grouped, keys_new)
    key_pos = jnp.arange(STEPS * FRAME).astype(jnp.int32)
    key_step = key_pos // FRAME
    key_slot = key_pos % FRAME
    query_pos = jnp.arange(FRAME).astype(jnp.int32)
    allowed = (key_step[None, :] < step) | (key_step[None, :] == step) & (key_slot[None, :] <= query_pos[:, None])
    score_new = jnp.where(allowed, score_new, -jnp.inf)
    top = jnp.maximum(lax.optimization_barrier(jnp.max(score_cache, axis=-1)), lax.optimization_barrier(jnp.max(score_new, axis=-1)))
    weight_cache = jnp.exp(score_cache - top[..., None])
    weight_new = jnp.exp(score_new - top[..., None])
    total = lax.optimization_barrier(jnp.sum(weight_cache, axis=-1)) + lax.optimization_barrier(jnp.sum(weight_new, axis=-1))
    summed = jnp.einsum('kgfc,kcd->kgfd', weight_cache.astype(jnp.bfloat16).astype(jnp.float32), values_cache)
    summed = summed + jnp.einsum('kgfj,jkd->kgfd', weight_new.astype(jnp.bfloat16).astype(jnp.float32), values_new)
    attended = summed / total[..., None]
    return jnp.transpose(attended, (2, 0, 1, 3)).reshape(FRAME, QH * HD).astype(jnp.bfloat16)

def policies_all(latent_vector, owners, policy_in, policy_mid, policy_head, policy_value):
    normed = rms_rows(latent_vector.astype(jnp.float32)).astype(jnp.bfloat16)

    def single(weights):
        first, second, actor, critic = weights
        inner = jax.nn.silu(jnp.dot(normed, first, preferred_element_type=jnp.float32)).astype(jnp.bfloat16)
        hidden = jax.nn.silu(jnp.dot(inner, second, preferred_element_type=jnp.float32)).astype(jnp.bfloat16)
        logits = jnp.dot(hidden, actor, preferred_element_type=jnp.float32)
        value = jnp.dot(hidden, critic, preferred_element_type=jnp.float32)
        return (logits - jax.nn.logsumexp(logits, axis=-1, keepdims=True), value)
    every_logp, every_value = lax.map(single, (policy_in, policy_mid, policy_head, policy_value))
    pick = (owners[:, 0][None, :] == jnp.arange(POLICIES).astype(jnp.int32)[:, None]).astype(jnp.float32)
    return (lax.optimization_barrier(jnp.sum(every_logp * pick[..., None], axis=0)), lax.optimization_barrier(jnp.sum(every_value * pick, axis=0)))

def reference(frame, cache, actions, owners, attn_gain, w_query, w_keyval, w_out, action_table, policy_in, policy_mid, policy_head, policy_value):
    repeat = QH // KVH
    whole_cache = cache.reshape(ROLLOUTS, KVH, CACHE, 2 * HD)
    stash = jnp.zeros((ROLLOUTS, STEPS * FRAME, KVH, 2 * HD), jnp.bfloat16)
    state = frame
    all_logp = []
    all_value = []
    for step in range(STEPS):
        code = (actions[:, step][:, None] == jnp.arange(ACTIONS).astype(jnp.int32)[None, :]).astype(jnp.bfloat16)
        embed = jnp.dot(code, action_table, preferred_element_type=jnp.float32)
        inputs = (state.astype(jnp.float32) + embed[:, None, :]).astype(jnp.bfloat16)
        flat = inputs.reshape(ROLLOUTS * FRAME, D)
        normed = (rms_rows(flat.astype(jnp.float32)) * attn_gain).astype(jnp.bfloat16)
        query = (jnp.dot(normed, w_query, preferred_element_type=jnp.float32) * HD ** (-0.5)).astype(jnp.bfloat16)
        query = query.reshape(ROLLOUTS, FRAME, KVH, repeat, HD)
        keyval = jnp.dot(normed, w_keyval, preferred_element_type=jnp.float32).astype(jnp.bfloat16)
        keyval = keyval.reshape(ROLLOUTS, FRAME, KVH, 2 * HD)
        stash = stash.at[:, step * FRAME:(step + 1) * FRAME].set(keyval)
        attended = lax.map(partial_attend(step), (query, whole_cache, stash))
        projected = jnp.dot(attended.reshape(ROLLOUTS * FRAME, QH * HD), w_out, preferred_element_type=jnp.float32)
        state = (flat.astype(jnp.float32) + projected).astype(jnp.bfloat16).reshape(ROLLOUTS, FRAME, D)
        logp, value = policies_all(state[:, FRAME - 1], owners, policy_in, policy_mid, policy_head, policy_value)
        all_logp.append(logp)
        all_value.append(value)
    return (state, jnp.stack(all_logp, axis=1), jnp.stack(all_value, axis=1))

def partial_attend(step):

    def inner_attend(args):
        return attend_rollout(args, step)
    return inner_attend
```

```python
import functools

import jax
import jax.numpy as jnp
from jax import lax
from jax.experimental import pallas as pl
from jax.experimental.pallas import tpu as pltpu
from jax.sharding import PartitionSpec as P

HD = 128
STEPS = 4
CAP = 2
EPS = 1e-05
MESH = pl.DeviceIdType.MESH
F32 = jnp.float32
BF16 = jnp.bfloat16
VMEM_LIMIT = 56 << 20


def rms_rows(values):
    return values * lax.rsqrt(jnp.mean(values * values, axis=-1, keepdims=True) + EPS)


def folded(rows):
    half = rows.shape[1] // 2
    return jnp.concatenate([rows[:, :half], rows[:, half:]], axis=0)


def halves(product, half, width):
    return product.reshape(-1, 2, 8, width)[:, half].reshape(-1, width)


def fold_dot(chunks, weight):
    half = weight.shape[0] // 2
    columns = weight.shape[1]
    left = jnp.dot(chunks, weight[:half], preferred_element_type=F32)
    right = jnp.dot(chunks, weight[half:], preferred_element_type=F32)
    return halves(left, 0, columns) + halves(right, 1, columns)


def world_kernel(
    n_z,
    frame_ref,
    actions_ref,
    gain_ref,
    table_ref,
    cache_ref,
    wq_ref,
    wkv_ref,
    wo_ref,
    latents_ref,
    rows_ref,
    state,
    gath,
    qkv,
    qkv_in,
    keys,
    vals,
    scores,
    weights,
    own_o,
    out_o,
    in_o,
    terms,
    pair_in,
    zsum,
    zsum_in,
    ag_send,
    ag_recv,
    fw_send,
    fw_recv,
    z_send,
    z_recv,
    q_send,
    q_recv,
    o_send,
    o_recv,
    p_send,
    p_recv,
    s_send,
    s_recv,
):
    tensor = lax.axis_index("tp")
    z = tensor // 2
    yh = lax.rem(tensor, 2)
    partner = tensor + 1 - 2 * yh
    rollouts, width = state.shape
    tokens = 2 * n_z
    n_rows = tokens * rollouts
    cached = cache_ref.shape[2]
    last = tokens - 1
    order = [k for d in range(1, n_z // 2 + 1) for k in dict.fromkeys((d, n_z - d))]

    def plane(k):
        return lax.rem(z + k, n_z)

    def to_plane(k):
        return {"tp": plane(k) * 2 + yh}

    barrier = pltpu.get_barrier_semaphore()
    for k in order:
        pl.semaphore_signal(barrier, inc=1, device_id=to_plane(k), device_id_type=MESH)
    pl.semaphore_signal(barrier, inc=1, device_id={"tp": partner}, device_id_type=MESH)

    def copy(src, dst, send, recv, target):
        return pltpu.make_async_remote_copy(
            src_ref=src, dst_ref=dst, send_sem=send, recv_sem=recv, device_id=target, device_id_type=MESH
        )

    state[...] = frame_ref[...].astype(F32)
    keys[...] = jnp.zeros_like(keys)
    vals[...] = jnp.zeros_like(vals)
    iota_r = lax.broadcasted_iota(jnp.int32, (n_rows, n_rows), 0)
    iota_c = lax.broadcasted_iota(jnp.int32, (n_rows, n_rows), 1)
    by_rollout = (lax.rem(iota_r, tokens) * rollouts + iota_r // tokens == iota_c).astype(F32).astype(BF16)
    by_token = (lax.rem(iota_c, tokens) * rollouts + iota_c // tokens == iota_r).astype(F32).astype(BF16)
    pl.semaphore_wait(barrier, len(order) + 1)

    def spread_rows(s):
        source = rows_ref.at[s]

        def across(k):
            return copy(source, source, z_send.at[s, k], z_recv.at[s, 0], to_plane(k))

        pair = copy(source, source, z_send.at[s, 0], z_recv.at[s, 1], {"tp": partner})

        def start():
            @pl.when(tensor == last)
            def _():
                for k in order:
                    across(k).start()
                pair.start()

        def finish():
            @pl.when((yh == 1) & (tensor != last))
            def _():
                across(1).wait_recv()
                pair.start()

            @pl.when(yh == 0)
            def _():
                pair.wait_recv()

            @pl.when(yh == 1)
            def _():
                pair.wait_send()

            @pl.when(tensor == last)
            def _():
                for k in order:
                    across(k).wait_send()

        return start, finish

    def step(s, carry):
        picked = jnp.sum(
            jnp.where(lax.broadcasted_iota(jnp.int32, actions_ref.shape, 1) == s, actions_ref[...], 0),
            axis=1,
            keepdims=True,
        )
        code = (lax.broadcasted_iota(jnp.int32, (rollouts, table_ref.shape[0]), 1) == picked).astype(F32).astype(BF16)
        embed = jnp.dot(code, table_ref[...], preferred_element_type=F32)
        inputs = (state[...] + embed).astype(BF16).astype(F32)
        state[...] = inputs
        normed = rms_rows(inputs) * gain_ref[...]
        gath[s, tensor] = folded(normed).astype(BF16)

        mine = gath.at[s, tensor]
        for k in order:
            copy(mine, mine, ag_send.at[s, k], ag_recv.at[s, k], to_plane(k)).start()
        forward = {}
        for k in [0] + order:
            slot = gath.at[s, plane(k) * 2 + yh]
            if k:
                copy(slot, slot, ag_send.at[s, n_z - k], ag_recv.at[s, n_z - k], to_plane(k)).wait_recv()
            forward[k] = copy(slot, slot, fw_send.at[s, k], fw_recv.at[s, k], {"tp": partner})
            forward[k].start()
        for k in [0] + order:
            slot = gath.at[s, plane(k) * 2 + 1 - yh]
            copy(slot, slot, fw_send.at[s, k], fw_recv.at[s, k], {"tp": partner}).wait_recv()

        chunks = gath[s].reshape(tokens * 16, width // 2)
        query = (fold_dot(chunks, wq_ref) * HD ** (-0.5)).astype(BF16)
        keyval = fold_dot(chunks, wkv_ref).astype(BF16)
        n_query = query.shape[1]
        qkv[s, :, :n_query] = jnp.dot(by_rollout, query, preferred_element_type=F32).astype(BF16)
        qkv[s, :, n_query:] = jnp.dot(by_rollout, keyval, preferred_element_type=F32).astype(BF16)
        swap = copy(qkv.at[s], qkv_in.at[s], q_send.at[s], q_recv.at[s], {"tp": partner})
        swap.start()
        for k in order:
            copy(mine, mine, ag_send.at[s, k], ag_recv.at[s, k], to_plane(k)).wait_send()
        for k in [0] + order:
            forward[k].wait_send()
        swap.wait()

        own_kv = qkv[s, :, n_query:].astype(F32)
        other_kv = qkv_in[s, :, n_query:].astype(F32)
        new_key = jnp.where(yh == 0, own_kv, other_kv).astype(BF16)
        new_val = jnp.where(yh == 0, other_kv, own_kv).astype(BF16)
        place = pl.ds(pl.multiple_of(s * tokens, tokens), tokens)
        heads = n_query // HD
        per = 2 * heads * tokens
        nt = (((1,), (1,)), ((), ()))
        for r in range(rollouts):
            rows = slice(r * tokens, (r + 1) * tokens)
            keys[r, place, :] = new_key[rows]
            vals[r, place, :] = new_val[rows]
            parts = [qkv[s, rows, h * HD : (h + 1) * HD] for h in range(heads)]
            parts += [qkv_in[s, rows, h * HD : (h + 1) * HD] for h in range(heads)]
            grouped = jnp.concatenate(parts, axis=0)
            band = slice(r * per, (r + 1) * per)
            scores[band, :cached] = lax.dot_general(
                grouped, cache_ref[r, 0, :, :HD], nt, preferred_element_type=F32
            )
            scores[band, cached:] = lax.dot_general(grouped, keys[r], nt, preferred_element_type=F32)
        fresh = scores[:, cached:]
        key_pos = lax.broadcasted_iota(jnp.int32, fresh.shape, 1)
        query_pos = lax.rem(lax.broadcasted_iota(jnp.int32, fresh.shape, 0), tokens)
        allowed = (key_pos <= s * tokens + query_pos) & (yh == 0)
        fresh = jnp.where(allowed, fresh, -jnp.inf)
        old = scores[:, :cached]
        top = jnp.maximum(jnp.max(old, axis=1, keepdims=True), jnp.max(fresh, axis=1, keepdims=True))
        old = jnp.exp(old - top)
        fresh = jnp.exp(fresh - top)
        total = jnp.sum(old, axis=1, keepdims=True) + jnp.sum(fresh, axis=1, keepdims=True)
        weights[:, :cached] = old.astype(BF16)
        weights[:, cached:] = fresh.astype(BF16)
        inverse = 1.0 / total
        lane = lax.broadcasted_iota(jnp.int32, (tokens, HD), 1)
        for r in range(rollouts):
            rows = slice(r * tokens, (r + 1) * tokens)
            band = slice(r * per, (r + 1) * per)
            summed = jnp.dot(weights[band, :cached], cache_ref[r, 0, :, HD:], preferred_element_type=F32)
            summed = summed + jnp.dot(weights[band, cached:], vals[r], preferred_element_type=F32)
            summed = summed * inverse[band]
            stats = jnp.zeros((tokens, HD), F32)
            for h in range(heads):
                own_o[rows, h * HD : (h + 1) * HD] = summed[h * tokens : (h + 1) * tokens]
                far = slice((heads + h) * tokens, (heads + h + 1) * tokens)
                out_o[s, rows, h * HD : (h + 1) * HD] = summed[far].astype(BF16)
                left = top[band][far]
                for piece in range(3):
                    term = left.astype(BF16).astype(F32)
                    left = left - term
                    stats = jnp.where(lane == 8 * h + piece, term, stats)
                left = total[band][far]
                for piece in range(3):
                    term = left.astype(BF16).astype(F32)
                    left = left - term
                    stats = jnp.where(lane == 8 * h + 3 + piece, term, stats)
            out_o[s, rows, n_query:] = stats.astype(BF16)
        swap = copy(out_o.at[s], in_o.at[s], o_send.at[s], o_recv.at[s], {"tp": partner})
        swap.start()
        swap.wait()

        stats = in_o[s, :, n_query:].astype(F32)
        top4 = top.reshape(rollouts, 2 * heads, tokens, 1)
        total4 = total.reshape(rollouts, 2 * heads, tokens, 1)
        joined = []
        for h in range(heads):
            pick = [stats[:, 8 * h + i : 8 * h + i + 1] for i in range(6)]
            far_top = pick[0] + pick[1] + pick[2]
            far_total = pick[3] + pick[4] + pick[5]
            near_top = top4[:, h].reshape(n_rows, 1)
            near_total = total4[:, h].reshape(n_rows, 1)
            peak = jnp.maximum(near_top, far_top)
            near = near_total * jnp.exp(near_top - peak)
            far = far_total * jnp.exp(far_top - peak)
            both = 1.0 / (near + far)
            cols = slice(h * HD, (h + 1) * HD)
            joined.append(own_o[:, cols] * (near * both) + in_o[s, :, cols].astype(F32) * (far * both))
        attended = jnp.concatenate(joined, axis=1).astype(BF16)
        attended = jnp.dot(by_token, attended, preferred_element_type=F32).astype(BF16)

        tile = 512 if (width // 2) % 512 == 0 else HD
        for j in range(width // 2 // tile):
            at = slice(j * tile, (j + 1) * tile)
            also = slice(width // 2 + j * tile, width // 2 + (j + 1) * tile)
            left = jnp.dot(attended, wo_ref[:, at], preferred_element_type=F32).reshape(tokens, rollouts, tile)
            right = jnp.dot(attended, wo_ref[:, also], preferred_element_type=F32).reshape(tokens, rollouts, tile)
            terms[:, :, at] = jnp.concatenate([left, right], axis=1).astype(BF16)

        def to_pair(k):
            return copy(
                terms.at[plane(k) * 2 + 1 - yh], pair_in.at[s, k], p_send.at[s, k], p_recv.at[s, k], {"tp": partner}
            )

        def across(k):
            return copy(zsum.at[k], zsum_in.at[s, k], s_send.at[s, k], s_recv.at[s, k], to_plane(k))

        outward = order[::-1]
        for k in outward + [0]:
            to_pair(k).start()
        for k in outward:
            to_pair(k).wait_recv()
            zsum[k] = (terms[plane(k) * 2 + yh].astype(F32) + pair_in[s, k].astype(F32)).astype(BF16)
            across(k).start()
        to_pair(0).wait_recv()
        reduced = terms[tensor].astype(F32) + pair_in[s, 0].astype(F32)
        for k in order:
            across(n_z - k).wait_recv()
            reduced = reduced + zsum_in[s, n_z - k].astype(F32)
        reduced = jnp.concatenate([reduced[:rollouts], reduced[rollouts:]], axis=1)
        updated = (state[...] + reduced).astype(BF16).astype(F32)
        state[...] = updated

        @pl.when(tensor == last)
        def _():
            rows_ref[s] = folded(rms_rows(updated)).astype(BF16)

        start, finish = spread_rows(s)
        start()
        for k in outward:
            to_pair(k).wait_send()
            across(k).wait_send()
        to_pair(0).wait_send()
        finish()
        return carry

    lax.fori_loop(0, STEPS, step, 0)
    latents_ref[...] = state[...].astype(BF16)


def policy_kernel(
    peers,
    n_tensor,
    rows_ref,
    owners_ref,
    pin_ref,
    pmid_ref,
    head_ref,
    critic_ref,
    logp_ref,
    value_ref,
    outgoing,
    arrived,
    partial,
    partial_in,
    hidden,
    answers,
    returned,
    a_send,
    a_recv,
    h_send,
    h_recv,
    g_send,
    g_recv,
    b_send,
    b_recv,
):
    tensor = lax.axis_index("tp")
    row = lax.axis_index("row")
    rollouts = owners_ref.shape[0]
    actions = head_ref.shape[1]
    per = STEPS * CAP

    def to_row(k):
        return {"row": lax.rem(row + k, peers)}

    def to_tensor(k):
        return {"tp": lax.rem(tensor + k, n_tensor)}

    barrier = pltpu.get_barrier_semaphore()
    for k in range(1, peers):
        pl.semaphore_signal(barrier, inc=1, device_id=to_row(k), device_id_type=MESH)
    for k in range(1, n_tensor):
        pl.semaphore_signal(barrier, inc=1, device_id=to_tensor(k), device_id_type=MESH)

    def copy(src, dst, send, recv, target):
        return pltpu.make_async_remote_copy(
            src_ref=src, dst_ref=dst, send_sem=send, recv_sem=recv, device_id=target, device_id_type=MESH
        )

    owner_col = owners_ref[...]
    hit = (lax.broadcasted_iota(jnp.int32, (rollouts, 128), 1) == owner_col).astype(F32)
    lower = (
        lax.broadcasted_iota(jnp.int32, (rollouts, rollouts), 0)
        > lax.broadcasted_iota(jnp.int32, (rollouts, rollouts), 1)
    ).astype(F32)
    before = jnp.zeros((rollouts, 128), F32)
    for r in range(rollouts):
        before = before + lower[:, r : r + 1] * hit[r : r + 1, :]
    slot = jnp.sum(before * hit, axis=1, keepdims=True)
    places = peers * per
    col = lax.broadcasted_iota(jnp.int32, (rollouts, places), 1)
    owner_hit = (col // per == owner_col) & (lax.rem(col, CAP).astype(F32) == slot)
    step_of = lax.rem(col, per) // CAP
    hot = jnp.concatenate([(owner_hit & (step_of == s)).astype(F32) for s in range(STEPS)], axis=0)
    hot16 = hot.astype(BF16)
    tn = (((0,), (0,)), ((), ()))
    sources = rows_ref[...].astype(F32).reshape(STEPS, 2, rollouts, -1)
    half = sources.shape[-1]
    left = lax.dot_general(
        hot16, sources[:, 0].reshape(STEPS * rollouts, half).astype(BF16), tn, preferred_element_type=F32
    )
    right = lax.dot_general(
        hot16, sources[:, 1].reshape(STEPS * rollouts, half).astype(BF16), tn, preferred_element_type=F32
    )
    outgoing[...] = jnp.concatenate(
        [left.reshape(peers, per, half), right.reshape(peers, per, half)], axis=1
    ).astype(BF16)
    arrived[row] = outgoing[row]
    pl.semaphore_wait(barrier, peers + n_tensor - 2)

    def route(k):
        return copy(outgoing.at[lax.rem(row + k, peers)], arrived.at[row], a_send.at[k], a_recv.at[k], to_row(k))

    for k in range(1, peers):
        route(k).start()
    for k in range(1, peers):
        origin = lax.rem(row + peers - k, peers)
        copy(arrived.at[origin], arrived.at[origin], a_send.at[k], a_recv.at[k], to_row(k)).wait_recv()
    chunks = arrived[...].reshape(peers * 16, half)
    inner = jax.nn.silu(fold_dot(chunks, pin_ref.at[0])).astype(BF16)
    units = pmid_ref.shape[2] // n_tensor
    for j in range(n_tensor):
        partial[j] = jnp.dot(
            inner, pmid_ref[0, :, j * units : (j + 1) * units], preferred_element_type=F32
        ).astype(BF16)

    def to_units(k):
        return copy(
            partial.at[lax.rem(tensor + k, n_tensor)], partial_in.at[k], h_send.at[k], h_recv.at[k], to_tensor(k)
        )

    for k in range(1, n_tensor):
        to_units(k).start()
    summed = partial[tensor].astype(F32)
    for k in range(1, n_tensor):
        to_units(k).wait_recv()
        summed = summed + partial_in[k].astype(F32)
    hidden[tensor] = jax.nn.silu(summed).astype(BF16)

    def share(k):
        return copy(hidden.at[tensor], hidden.at[tensor], g_send.at[k], g_recv.at[k], to_tensor(k))

    for k in range(1, n_tensor):
        share(k).start()
    for k in range(1, n_tensor):
        origin = lax.rem(tensor + n_tensor - k, n_tensor)
        copy(hidden.at[origin], hidden.at[origin], g_send.at[k], g_recv.at[k], to_tensor(k)).wait_recv()
    logits = jnp.zeros((places, actions), F32)
    value = jnp.zeros((places, 1), F32)
    for j in range(n_tensor):
        part = hidden[j]
        at = slice(j * units, (j + 1) * units)
        logits = logits + jnp.dot(part, head_ref[at, :], preferred_element_type=F32)
        value = value + jnp.sum(part.astype(F32) * critic_ref[:, at].astype(F32), axis=1, keepdims=True)
    peak = jnp.max(logits, axis=1, keepdims=True)
    logp = logits - (peak + jnp.log(jnp.sum(jnp.exp(logits - peak), axis=1, keepdims=True)))
    packed = jnp.concatenate([logp, value, jnp.zeros((places, 128 - actions - 1), F32)], axis=1)
    answers[...] = packed.reshape(peers, per, 128)
    returned[row] = answers[row]

    def reply(k):
        return copy(answers.at[lax.rem(row + k, peers)], returned.at[row], b_send.at[k], b_recv.at[k], to_row(k))

    for k in range(1, peers):
        reply(k).start()
    for k in range(1, peers):
        origin = lax.rem(row + peers - k, peers)
        copy(returned.at[origin], returned.at[origin], b_send.at[k], b_recv.at[k], to_row(k)).wait_recv()
    result = jnp.dot(
        hot, returned[...].reshape(places, 128), preferred_element_type=F32, precision=lax.Precision.HIGHEST
    )
    lane = lax.broadcasted_iota(jnp.int32, (rollouts, STEPS), 1)
    all_values = jnp.zeros((rollouts, STEPS), F32)
    for s in range(STEPS):
        now = result[s * rollouts : (s + 1) * rollouts]
        logp_ref[:, s, :] = now[:, :actions]
        all_values = jnp.where(lane == s, now[:, actions : actions + 1], all_values)
    value_ref[...] = all_values
    for k in range(1, peers):
        route(k).wait_send()
        reply(k).wait_send()
    for k in range(1, n_tensor):
        to_units(k).wait_send()
        share(k).wait_send()


def shards(
    frame,
    cache,
    actions,
    owners,
    attn_gain,
    w_query,
    w_keyval,
    w_out,
    action_table,
    policy_in,
    policy_mid,
    policy_head,
    policy_value,
):
    n_tensor = lax.axis_size("tp")
    peers = lax.axis_size("row")
    n_z = n_tensor // 2
    rollouts, _, width = frame.shape
    half = width // 2
    n_rows = n_tensor * rollouts
    n_query = w_query.shape[1]
    n_fresh = w_keyval.shape[1]
    wide = n_query + n_fresh
    cached = cache.shape[2]
    bands = n_rows * 2 * (n_query // HD)
    vmem = pl.BlockSpec(memory_space=pltpu.VMEM)
    dma = pltpu.SemaphoreType.DMA
    latents, rows = pl.pallas_call(
        functools.partial(world_kernel, n_z),
        out_shape=(
            jax.ShapeDtypeStruct((rollouts, width), BF16),
            jax.ShapeDtypeStruct((STEPS, 2 * rollouts, half), BF16),
        ),
        in_specs=[vmem] * 8,
        out_specs=(vmem, vmem),
        scratch_shapes=[
            pltpu.VMEM((rollouts, width), F32),
            pltpu.VMEM((STEPS, n_tensor, 16, half), BF16),
            pltpu.VMEM((STEPS, n_rows, wide), BF16),
            pltpu.VMEM((STEPS, n_rows, wide), BF16),
            pltpu.VMEM((rollouts, 128, HD), BF16),
            pltpu.VMEM((rollouts, 128, HD), BF16),
            pltpu.VMEM((bands, cached + 128), F32),
            pltpu.VMEM((bands, cached + 128), BF16),
            pltpu.VMEM((n_rows, n_query), F32),
            pltpu.VMEM((STEPS, n_rows, wide), BF16),
            pltpu.VMEM((STEPS, n_rows, wide), BF16),
            pltpu.VMEM((n_tensor, 16, half), BF16),
            pltpu.VMEM((STEPS, n_z, 16, half), BF16),
            pltpu.VMEM((n_z, 16, half), BF16),
            pltpu.VMEM((STEPS, n_z, 16, half), BF16),
        ]
        + [dma((STEPS, n_z))] * 5
        + [dma((STEPS, 2))]
        + [dma((STEPS,))] * 4
        + [dma((STEPS, n_z))] * 4,
        compiler_params=pltpu.CompilerParams(
            collective_id=0, has_side_effects=True, vmem_limit_bytes=VMEM_LIMIT
        ),
        name="world",
    )(
        frame.reshape(rollouts, width),
        actions,
        attn_gain.reshape(1, width),
        action_table,
        cache,
        w_query,
        w_keyval,
        w_out,
    )
    n_actions = policy_head.shape[2]
    units = policy_mid.shape[2] // n_tensor
    places = peers * STEPS * CAP
    log_probs, values = pl.pallas_call(
        functools.partial(policy_kernel, peers, n_tensor),
        out_shape=(
            jax.ShapeDtypeStruct((rollouts, STEPS, n_actions), F32),
            jax.ShapeDtypeStruct((rollouts, STEPS), F32),
        ),
        in_specs=[vmem] * 6,
        out_specs=(vmem, vmem),
        scratch_shapes=[
            pltpu.VMEM((peers, 16, half), BF16),
            pltpu.VMEM((peers, 16, half), BF16),
            pltpu.VMEM((n_tensor, places, units), BF16),
            pltpu.VMEM((n_tensor, places, units), BF16),
            pltpu.VMEM((n_tensor, places, units), BF16),
            pltpu.VMEM((peers, STEPS * CAP, 128), F32),
            pltpu.VMEM((peers, STEPS * CAP, 128), F32),
        ]
        + [dma((peers,))] * 2
        + [dma((n_tensor,))] * 4
        + [dma((peers,))] * 2,
        compiler_params=pltpu.CompilerParams(
            collective_id=1, has_side_effects=True, vmem_limit_bytes=VMEM_LIMIT
        ),
        name="policies",
    )(rows, owners, policy_in, policy_mid, policy_head.reshape(policy_head.shape[1:]), policy_value)
    return (latents.reshape(frame.shape), log_probs, values)


def solution(mesh):
    placed = (
        P(("grp", "row"), "tp", None),
        P(("grp", "row"), "tp", None, None),
        P(("grp", "row"), None),
        P(("grp", "row"), None),
        P(),
        P(None, "tp"),
        P(None, "tp"),
        P("tp", None),
        P(),
        P("row", None, "tp"),
        P("row", "tp", None),
        P("row", None, None),
        P("row", None),
    )
    return jax.shard_map(
        shards,
        mesh=mesh,
        in_specs=placed,
        out_specs=(
            P(("grp", "row"), "tp", None),
            P(("grp", "row"), None, None),
            P(("grp", "row"), None),
        ),
        check_vma=False,
    )
```

```python
import functools

import jax
import jax.numpy as jnp
from jax import lax
from jax.experimental import pallas as pl
from jax.experimental.pallas import tpu as pltpu
from jax.sharding import PartitionSpec as P

HD = 128
STEPS = 4
CAP = 2
EPS = 1e-05
MESH = pl.DeviceIdType.MESH
F32 = jnp.float32
BF16 = jnp.bfloat16
VMEM_LIMIT = 56 << 20


def rms_rows(values):
    return values * lax.rsqrt(jnp.mean(values * values, axis=-1, keepdims=True) + EPS)


def folded(rows):
    half = rows.shape[1] // 2
    return jnp.concatenate([rows[:, :half], rows[:, half:]], axis=0)


PAIR_COLUMNS = 512
FAR = {False: {1: 0, -1: 0, 2: 0, -2: 0, 3: 2, -3: -2, 4: 2}, True: {1: 0, -1: 0, 2: 0, -2: 0, 3: 2, -3: -2, -4: -2}}


def due(tree, k):
    return 0.0 if k == 0 else due(tree, tree[k]) + 2.0 + 0.8 * abs(k - tree[k])


def below(tree, k):
    return sorted([c for c in tree if tree[c] == k], key=lambda c: abs(c - k))


def halves(product, half, width):
    return product.reshape(-1, 2, 8, width)[:, half].reshape(-1, width)


def fold_dot(first, second, weight):
    half = weight.shape[0] // 2
    columns = weight.shape[1]
    cut = first.shape[1]
    left = jnp.dot(first, weight[:cut], preferred_element_type=F32)
    left = left + jnp.dot(second, weight[cut:half], preferred_element_type=F32)
    right = jnp.dot(first, weight[half : half + cut], preferred_element_type=F32)
    right = right + jnp.dot(second, weight[half + cut :], preferred_element_type=F32)
    return halves(left, 0, columns) + halves(right, 1, columns)


def silu(values):
    return values / (1.0 + jnp.exp(-values))


def kernel(
    n_z,
    peers,
    frame_ref,
    actions_ref,
    owners_ref,
    gain_ref,
    table_ref,
    cache_ref,
    wq_ref,
    wkv_ref,
    wo_ref,
    pin_ref,
    pmid_ref,
    head_ref,
    critic_ref,
    latents_ref,
    logp_ref,
    value_ref,
    state,
    gath_p,
    gath_q,
    qkv,
    qkv_in,
    keys,
    vals,
    scores,
    weights,
    own_o,
    out_o,
    in_o,
    terms_p,
    terms_q,
    tree_p,
    tree_q,
    pair_p,
    pair_q,
    latent_rows,
    outgoing,
    arrived,
    partial,
    partial_in,
    hidden,
    answers,
    returned,
    ag_zs,
    ag_zr,
    ag_ys,
    ag_yr,
    rs_zs,
    rs_zr,
    rs_ys,
    rs_yr,
    q_send,
    q_recv,
    o_send,
    o_recv,
    l_send,
    l_recv,
    a_send,
    a_recv,
    h_send,
    h_recv,
    g_send,
    g_recv,
    b_send,
    b_recv,
):
    tensor = lax.axis_index("tp")
    row = lax.axis_index("row")
    z = tensor // 2
    yh = lax.rem(tensor, 2)
    pair = {"tp": tensor + 1 - 2 * yh}
    rollouts, width = state.shape
    n_tensor = 2 * n_z
    tokens = n_tensor
    n_rows = tokens * rollouts
    cached = cache_ref.shape[2]
    last = n_tensor - 1
    cut = gath_p.shape[3]
    half = width // 2

    def plane(k):
        return lax.rem(z + k + 2 * n_z, n_z)

    def to_plane(k):
        return {"tp": plane(k) * 2 + yh}

    def slot_of(k, other):
        return plane(k) * 2 + (1 - yh if other else yh)

    def to_row(k):
        return {"row": lax.rem(row + k, peers)}

    def to_tensor(k):
        return {"tp": lax.rem(tensor + k, n_tensor)}

    barrier = pltpu.get_barrier_semaphore()
    for k in range(1, n_tensor):
        pl.semaphore_signal(barrier, inc=1, device_id=to_tensor(k), device_id_type=MESH)
    for k in range(1, peers):
        pl.semaphore_signal(barrier, inc=1, device_id=to_row(k), device_id_type=MESH)

    def copy(src, dst, send, recv, target):
        return pltpu.make_async_remote_copy(
            src_ref=src, dst_ref=dst, send_sem=send, recv_sem=recv, device_id=target, device_id_type=MESH
        )

    state[...] = frame_ref[...].astype(F32)
    keys[...] = jnp.zeros_like(keys)
    vals[...] = jnp.zeros_like(vals)
    iota_r = lax.broadcasted_iota(jnp.int32, (n_rows, n_rows), 0)
    iota_c = lax.broadcasted_iota(jnp.int32, (n_rows, n_rows), 1)
    by_rollout = (lax.rem(iota_r, tokens) * rollouts + iota_r // tokens == iota_c).astype(F32).astype(BF16)
    by_token = (lax.rem(iota_c, tokens) * rollouts + iota_c // tokens == iota_r).astype(F32).astype(BF16)

    owner = owners_ref[...]
    hit = (lax.broadcasted_iota(jnp.int32, (rollouts, 128), 1) == owner).astype(F32)
    later = (
        lax.broadcasted_iota(jnp.int32, (rollouts, rollouts), 0)
        > lax.broadcasted_iota(jnp.int32, (rollouts, rollouts), 1)
    ).astype(F32)
    before = jnp.zeros((rollouts, 128), F32)
    for r in range(rollouts):
        before = before + later[:, r : r + 1] * hit[r : r + 1, :]
    place_of = jnp.sum(before * hit, axis=1, keepdims=True)
    eighths = 16 // CAP
    spots = peers * 16
    tn = (((0,), (0,)), ((), ()))
    pl.semaphore_wait(barrier, peers + n_tensor - 2)

    def spread_out(q, k):
        mine = latent_rows.at[q]
        for c in below(FAR[False], k):
            copy(mine, mine, l_send.at[q, c % n_z], l_recv.at[q, 0], to_plane(c - k)).start()
        copy(mine, mine, l_send.at[q, 0], l_recv.at[q, 1], pair).start()

    def spread_sent(q, k):
        mine = latent_rows.at[q]
        for c in below(FAR[False], k):
            copy(mine, mine, l_send.at[q, c % n_z], l_recv.at[q, 0], to_plane(c - k)).wait_send()
        copy(mine, mine, l_send.at[q, 0], l_recv.at[q, 1], pair).wait_send()

    def spread_start(q):
        @pl.when(tensor == last)
        def _():
            spread_out(q, 0)

    def spread_on(q):
        mine = latent_rows.at[q]
        for k in FAR[False]:

            @pl.when(tensor == (last + 2 * k) % n_tensor)
            def _():
                copy(mine, mine, l_send.at[q, 0], l_recv.at[q, 0], pair).wait_recv()
                spread_out(q, k)

        @pl.when(yh == 0)
        def _():
            copy(mine, mine, l_send.at[q, 0], l_recv.at[q, 1], pair).wait_recv()

    def spread_end(q):
        for k in [0] + list(FAR[False]):

            @pl.when(tensor == (last + 2 * k) % n_tensor)
            def _():
                spread_sent(q, k)

    def route(q, k):
        return copy(
            outgoing.at[q, lax.rem(row + k, peers)], arrived.at[q, row], a_send.at[q, k], a_recv.at[q, k], to_row(k)
        )

    def route_start(q):
        wide = half // 4
        i = lax.broadcasted_iota(jnp.int32, (16, spots), 1)
        j = lax.broadcasted_iota(jnp.int32, (16, spots), 0)
        owner2 = jnp.concatenate([owner, owner], axis=0)
        place2 = jnp.concatenate([place_of, place_of], axis=0)
        chosen = (i // 16 == owner2) & (lax.rem(i, CAP).astype(F32) == place2)
        eighth = lax.rem(i // CAP, eighths)
        built = jnp.zeros((spots, wide), F32)
        for quarter in range(4):
            hot = (chosen & (eighth == (j // rollouts) * 4 + quarter)).astype(F32).astype(BF16)
            built = built + lax.dot_general(
                hot, latent_rows[q, :, quarter * wide : (quarter + 1) * wide], tn, preferred_element_type=F32
            )
        outgoing[q] = built.astype(BF16).reshape(peers, 16, wide)
        arrived[q, row] = outgoing[q, row]
        for k in range(1, peers):
            route(q, k).start()

    def to_units(q, k):
        return copy(
            partial.at[q, lax.rem(tensor + k, n_tensor)],
            partial_in.at[q, k],
            h_send.at[q, k],
            h_recv.at[q, k],
            to_tensor(k),
        )

    def inner_start(q):
        for k in range(1, peers):
            origin = arrived.at[q, lax.rem(row + peers - k, peers)]
            copy(origin, origin, a_send.at[q, k], a_recv.at[q, k], to_row(k)).wait_recv()
        wide = half // 4
        rows = arrived[q].reshape(spots, wide)
        n_inner = pin_ref.shape[2]
        at_row = lax.rem(lax.broadcasted_iota(jnp.int32, (spots, n_inner), 0) // CAP, eighths)
        picked = jnp.zeros((spots, n_inner), F32)
        for e in range(eighths):
            product = jnp.dot(rows, pin_ref[0, e * wide : (e + 1) * wide, :], preferred_element_type=F32)
            picked = picked + jnp.where(at_row == e, product, 0.0)
        i = lax.broadcasted_iota(jnp.int32, (16, spots), 1)
        j = lax.broadcasted_iota(jnp.int32, (16, spots), 0)
        gather = ((i // 16 == j // CAP) & (lax.rem(i, CAP) == lax.rem(j, CAP))).astype(F32)
        before_silu = jnp.dot(gather, picked, preferred_element_type=F32, precision=lax.Precision.HIGHEST)
        inner = silu(before_silu).astype(BF16)
        units = partial.shape[3]
        product = jnp.dot(inner, pmid_ref[0], preferred_element_type=F32).astype(BF16)
        for t in range(n_tensor):
            partial[q, t] = product[:, t * units : (t + 1) * units]
        for k in range(1, n_tensor):
            to_units(q, k).start()

    def share(q, k):
        mine = hidden.at[q, tensor]
        return copy(mine, mine, g_send.at[q, k], g_recv.at[q, k], to_tensor(k))

    def hidden_start(q):
        summed = partial[q, tensor].astype(F32)
        for k in range(1, n_tensor):
            to_units(q, k).wait_recv()
            summed = summed + partial_in[q, k].astype(F32)
        hidden[q, tensor] = silu(summed).astype(BF16)
        for k in range(1, n_tensor):
            share(q, k).start()

    def reply(q, k):
        return copy(answers.at[q], returned.at[q, row], b_send.at[q, k], b_recv.at[q, k], to_row(k))

    def heads_start(q):
        for k in range(1, n_tensor):
            origin = hidden.at[q, lax.rem(tensor + n_tensor - k, n_tensor)]
            copy(origin, origin, g_send.at[q, k], g_recv.at[q, k], to_tensor(k)).wait_recv()
        whole = jnp.concatenate([hidden[q, t] for t in range(n_tensor)], axis=1)
        logits = jnp.dot(whole, head_ref[...], preferred_element_type=F32)
        value = jnp.sum(whole.astype(F32) * critic_ref[...].astype(F32), axis=1, keepdims=True)
        peak = jnp.max(logits, axis=1, keepdims=True)
        logp = logits - (peak + jnp.log(jnp.sum(jnp.exp(logits - peak), axis=1, keepdims=True)))
        blank = jnp.zeros((16, 128 - logits.shape[1] - 1), F32)
        answers[q] = jnp.concatenate([logp, value, blank], axis=1)
        returned[q, row] = answers[q]
        for k in range(1, peers):
            reply(q, k).start()

    def policy_end(q):
        for k in range(1, peers):
            origin = returned.at[q, lax.rem(row + peers - k, peers)]
            copy(origin, origin, b_send.at[q, k], b_recv.at[q, k], to_row(k)).wait_recv()
        spread_end(q)
        for k in range(1, peers):
            route(q, k).wait_send()
            reply(q, k).wait_send()
        for k in range(1, n_tensor):
            to_units(q, k).wait_send()
            share(q, k).wait_send()

    def gather(s):
        own, other, front = FAR[False], FAR[True], FAR[False]
        sent = []

        def block(stream, k):
            return (gath_q if stream == 2 else gath_p).at[s, slot_of(-k, stream == 1)]

        def go(ref, send, recv, target):
            moved = copy(ref, ref, send, recv, target)
            moved.start()
            sent.append(moved)

        def spread(stream, tree, k):
            for c in below(tree, k):
                go(block(stream, k), ag_zs.at[s, stream, c % n_z], ag_zr.at[s, stream, c % n_z], to_plane(c - k))

        def pass_on(k):
            go(block(2, k), ag_ys.at[s, k % n_z], ag_yr.at[s, k % n_z], pair)

        go(block(0, 0), ag_ys.at[s, n_z], ag_yr.at[s, n_z], pair)
        spread(2, front, 0)
        pass_on(0)
        spread(0, own, 0)
        events = [(due(front, k), 2, k) for k in front] + [(due(own, k), 0, k) for k in own]
        events += [(3.0 + due(other, k), 1, k) for k in [0] + list(other)]
        for _, stream, k in sorted(events):
            ref = block(stream, k)
            if k == 0:
                copy(ref, ref, ag_ys.at[s, n_z], ag_yr.at[s, n_z], pair).wait_recv()
            else:
                copy(ref, ref, ag_zs.at[s, stream, k % n_z], ag_zr.at[s, stream, k % n_z], pair).wait_recv()
            spread(stream, (own, other, front)[stream], k)
            if stream == 2:
                pass_on(k)
        for k in [0] + list(front):
            ref = gath_q.at[s, slot_of(-k, True)]
            copy(ref, ref, ag_ys.at[s, k % n_z], ag_yr.at[s, k % n_z], pair).wait_recv()
        return sent

    def scatter(s, meanwhile):
        trees = (FAR[False], FAR[True], FAR[False])
        sent = []

        def go(src, dst, send, recv, target):
            moved = copy(src, dst, send, recv, target)
            moved.start()
            sent.append(moved)

        for k in sorted(trees[2], key=lambda k: -due(trees[2], k)) + [0]:
            go(
                terms_q.at[slot_of(-k, True)],
                pair_q.at[s, k % n_z],
                rs_ys.at[s, k % n_z],
                rs_yr.at[s, k % n_z],
                pair,
            )
        deepest = max(due(trees[0], k) for k in trees[0])
        events = []
        for stream, offset in ((0, 1.0), (1, -0.1), (2, 3.0)):
            events += [(offset + deepest - due(trees[stream], k), stream, k) for k in [0] + list(trees[stream])]
        ends = {}
        for number, (_, stream, k) in enumerate(sorted(events)):
            if number == len(events) // 2:
                meanwhile()
            tree = trees[stream]
            terms = terms_q if stream == 2 else terms_p
            slot = slot_of(-k, stream == 1)

            def landing(c):
                return tree_q.at[s, c % n_z] if stream == 2 else tree_p.at[s, stream, c % n_z]

            total = None
            children = below(tree, k)
            if stream == 2 or children or k == 0:
                total = terms[slot].astype(F32)
            if stream == 2:
                ref = pair_q.at[s, k % n_z]
                copy(ref, ref, rs_ys.at[s, k % n_z], rs_yr.at[s, k % n_z], pair).wait_recv()
                total = total + pair_q[s, k % n_z].astype(F32)
            for c in children:
                ref = landing(c)
                copy(ref, ref, rs_zs.at[s, stream, c % n_z], rs_zr.at[s, stream, c % n_z], pair).wait_recv()
                total = total + ref[...].astype(F32)
            if k:
                if total is not None:
                    terms[slot] = total.astype(BF16)
                go(
                    terms.at[slot],
                    landing(k),
                    rs_zs.at[s, stream, k % n_z],
                    rs_zr.at[s, stream, k % n_z],
                    to_plane(tree[k] - k),
                )
            elif stream == 1:
                terms[slot] = total.astype(BF16)
                go(terms.at[slot], pair_p.at[s], rs_ys.at[s, n_z], rs_yr.at[s, n_z], pair)
            else:
                ends[stream] = total
        ref = pair_p.at[s]
        copy(ref, ref, rs_ys.at[s, n_z], rs_yr.at[s, n_z], pair).wait_recv()
        first = ends[0] + pair_p[s].astype(F32)
        both = jnp.concatenate([first, ends[2]], axis=1)
        return jnp.concatenate([both[:rollouts], both[rollouts:]], axis=1), sent

    def step(s, carry):
        picked = jnp.sum(
            jnp.where(lax.broadcasted_iota(jnp.int32, actions_ref.shape, 1) == s, actions_ref[...], 0),
            axis=1,
            keepdims=True,
        )
        code = (lax.broadcasted_iota(jnp.int32, (rollouts, table_ref.shape[0]), 1) == picked).astype(F32).astype(BF16)
        embed = jnp.dot(code, table_ref[...], preferred_element_type=F32)
        inputs = (state[...] + embed).astype(BF16).astype(F32)
        state[...] = inputs
        normed = folded(rms_rows(inputs) * gain_ref[...]).astype(BF16)
        gath_p[s, tensor] = normed[:, :cut]
        gath_q[s, tensor] = normed[:, cut:]
        gathered = gather(s)

        first = gath_p[s].reshape(n_tensor * 16, cut)
        second = gath_q[s].reshape(n_tensor * 16, half - cut)
        query = (fold_dot(first, second, wq_ref) * HD ** (-0.5)).astype(BF16)
        keyval = fold_dot(first, second, wkv_ref).astype(BF16)
        n_query = query.shape[1]
        qkv[s, :, :n_query] = jnp.dot(by_rollout, query, preferred_element_type=F32).astype(BF16)
        qkv[s, :, n_query:] = jnp.dot(by_rollout, keyval, preferred_element_type=F32).astype(BF16)
        swap = copy(qkv.at[s], qkv_in.at[s], q_send.at[s], q_recv.at[s], pair)
        swap.start()

        @pl.when(s > 0)
        def _():
            spread_on(s - 1)
            route_start(s - 1)

        for moved in gathered:
            moved.wait_send()
        swap.wait()

        own_kv = qkv[s, :, n_query:].astype(F32)
        other_kv = qkv_in[s, :, n_query:].astype(F32)
        new_key = jnp.where(yh == 0, own_kv, other_kv).astype(BF16)
        new_val = jnp.where(yh == 0, other_kv, own_kv).astype(BF16)
        place = pl.ds(pl.multiple_of(s * tokens, tokens), tokens)
        heads = n_query // HD
        per = 2 * heads * tokens
        nt = (((1,), (1,)), ((), ()))
        for r in range(rollouts):
            rows = slice(r * tokens, (r + 1) * tokens)
            keys[r, place, :] = new_key[rows]
            vals[r, place, :] = new_val[rows]
            parts = [qkv[s, rows, h * HD : (h + 1) * HD] for h in range(heads)]
            parts += [qkv_in[s, rows, h * HD : (h + 1) * HD] for h in range(heads)]
            grouped = jnp.concatenate(parts, axis=0)
            band = slice(r * per, (r + 1) * per)
            scores[band, :cached] = lax.dot_general(
                grouped, cache_ref[r, 0, :, :HD], nt, preferred_element_type=F32
            )
            scores[band, cached:] = lax.dot_general(grouped, keys[r], nt, preferred_element_type=F32)
        fresh = scores[:, cached:]
        key_pos = lax.broadcasted_iota(jnp.int32, fresh.shape, 1)
        query_pos = lax.rem(lax.broadcasted_iota(jnp.int32, fresh.shape, 0), tokens)
        allowed = (key_pos <= s * tokens + query_pos) & (yh == 0)
        fresh = jnp.where(allowed, fresh, -jnp.inf)
        old = scores[:, :cached]
        top = jnp.maximum(jnp.max(old, axis=1, keepdims=True), jnp.max(fresh, axis=1, keepdims=True))
        old = jnp.exp(old - top)
        fresh = jnp.exp(fresh - top)
        total = jnp.sum(old, axis=1, keepdims=True) + jnp.sum(fresh, axis=1, keepdims=True)
        weights[:, :cached] = old.astype(BF16)
        weights[:, cached:] = fresh.astype(BF16)
        inverse = 1.0 / total
        lane = lax.broadcasted_iota(jnp.int32, (tokens, HD), 1)
        for r in range(rollouts):
            rows = slice(r * tokens, (r + 1) * tokens)
            band = slice(r * per, (r + 1) * per)
            summed = jnp.dot(weights[band, :cached], cache_ref[r, 0, :, HD:], preferred_element_type=F32)
            summed = summed + jnp.dot(weights[band, cached:], vals[r], preferred_element_type=F32)
            summed = summed * inverse[band]
            stats = jnp.zeros((tokens, HD), F32)
            for h in range(heads):
                own_o[rows, h * HD : (h + 1) * HD] = summed[h * tokens : (h + 1) * tokens]
                far = slice((heads + h) * tokens, (heads + h + 1) * tokens)
                out_o[s, rows, h * HD : (h + 1) * HD] = summed[far].astype(BF16)
                left = top[band][far]
                for piece in range(3):
                    term = left.astype(BF16).astype(F32)
                    left = left - term
                    stats = jnp.where(lane == 8 * h + piece, term, stats)
                left = total[band][far]
                for piece in range(3):
                    term = left.astype(BF16).astype(F32)
                    left = left - term
                    stats = jnp.where(lane == 8 * h + 3 + piece, term, stats)
            out_o[s, rows, n_query:] = stats.astype(BF16)
        swap = copy(out_o.at[s], in_o.at[s], o_send.at[s], o_recv.at[s], pair)
        swap.start()

        @pl.when(s > 0)
        def _():
            inner_start(s - 1)

        swap.wait()

        stats = in_o[s, :, n_query:].astype(F32)
        top4 = top.reshape(rollouts, 2 * heads, tokens, 1)
        total4 = total.reshape(rollouts, 2 * heads, tokens, 1)
        joined = []
        for h in range(heads):
            pick = [stats[:, 8 * h + i : 8 * h + i + 1] for i in range(6)]
            far_top = pick[0] + pick[1] + pick[2]
            far_total = pick[3] + pick[4] + pick[5]
            near_top = top4[:, h].reshape(n_rows, 1)
            near_total = total4[:, h].reshape(n_rows, 1)
            peak = jnp.maximum(near_top, far_top)
            near = near_total * jnp.exp(near_top - peak)
            far = far_total * jnp.exp(far_top - peak)
            both = 1.0 / (near + far)
            cols = slice(h * HD, (h + 1) * HD)
            joined.append(own_o[:, cols] * (near * both) + in_o[s, :, cols].astype(F32) * (far * both))
        attended = jnp.concatenate(joined, axis=1).astype(BF16)
        attended = jnp.dot(by_token, attended, preferred_element_type=F32).astype(BF16)

        tile = 512 if half % 512 == 0 else HD
        for j in range(half // tile):
            at = slice(j * tile, (j + 1) * tile)
            also = slice(half + j * tile, half + (j + 1) * tile)
            left = jnp.dot(attended, wo_ref[:, at], preferred_element_type=F32).reshape(tokens, rollouts, tile)
            right = jnp.dot(attended, wo_ref[:, also], preferred_element_type=F32).reshape(tokens, rollouts, tile)
            part = jnp.concatenate([left, right], axis=1).astype(BF16)
            if j * tile < cut:
                terms_p[:, :, at] = part
            else:
                terms_q[:, :, j * tile - cut : (j + 1) * tile - cut] = part

        def meanwhile():
            @pl.when(s > 0)
            def _():
                hidden_start(s - 1)

        reduced, sent = scatter(s, meanwhile)
        updated = (state[...] + reduced).astype(BF16).astype(F32)
        state[...] = updated

        @pl.when(tensor == last)
        def _():
            latent_rows[s] = folded(rms_rows(updated)).astype(BF16)

        spread_start(s)
        for moved in sent:
            moved.wait_send()

        @pl.when(s > 0)
        def _():
            heads_start(s - 1)

        return carry

    lax.fori_loop(0, STEPS, step, 0)
    latents_ref[...] = state[...].astype(BF16)
    final = STEPS - 1
    spread_on(final)
    route_start(final)
    inner_start(final)
    hidden_start(final)
    heads_start(final)
    i = lax.broadcasted_iota(jnp.int32, (rollouts, spots), 1)
    mine = (i // 16 == owner) & (lax.rem(i, CAP).astype(F32) == place_of) & (lax.rem(i // CAP, eighths) == row)
    mine = mine.astype(F32)
    lane = lax.broadcasted_iota(jnp.int32, (rollouts, STEPS), 1)
    all_values = jnp.zeros((rollouts, STEPS), F32)
    n_actions = head_ref.shape[1]
    for q in range(STEPS):
        policy_end(q)
        now = jnp.dot(
            mine, returned[q].reshape(spots, 128), preferred_element_type=F32, precision=lax.Precision.HIGHEST
        )
        logp_ref[:, q, :] = now[:, :n_actions]
        all_values = jnp.where(lane == q, now[:, n_actions : n_actions + 1], all_values)
    value_ref[...] = all_values


def shards(
    frame,
    cache,
    actions,
    owners,
    attn_gain,
    w_query,
    w_keyval,
    w_out,
    action_table,
    policy_in,
    policy_mid,
    policy_head,
    policy_value,
):
    n_tensor = lax.axis_size("tp")
    peers = lax.axis_size("row")
    n_z = n_tensor // 2
    rollouts, _, width = frame.shape
    half = width // 2
    n_rows = n_tensor * rollouts
    n_query = w_query.shape[1]
    wide = n_query + w_keyval.shape[1]
    cached = cache.shape[2]
    bands = n_rows * 2 * (n_query // HD)
    units = policy_mid.shape[2] // n_tensor
    cut = PAIR_COLUMNS
    vmem = pl.BlockSpec(memory_space=pltpu.VMEM)
    dma = pltpu.SemaphoreType.DMA
    latents, log_probs, values = pl.pallas_call(
        functools.partial(kernel, n_z, peers),
        out_shape=(
            jax.ShapeDtypeStruct((rollouts, width), BF16),
            jax.ShapeDtypeStruct((rollouts, STEPS, policy_head.shape[2]), F32),
            jax.ShapeDtypeStruct((rollouts, STEPS), F32),
        ),
        in_specs=[vmem] * 13,
        out_specs=(vmem,) * 3,
        scratch_shapes=[
            pltpu.VMEM((rollouts, width), F32),
            pltpu.VMEM((STEPS, n_tensor, 16, cut), BF16),
            pltpu.VMEM((STEPS, n_tensor, 16, half - cut), BF16),
            pltpu.VMEM((STEPS, n_rows, wide), BF16),
            pltpu.VMEM((STEPS, n_rows, wide), BF16),
            pltpu.VMEM((rollouts, 128, HD), BF16),
            pltpu.VMEM((rollouts, 128, HD), BF16),
            pltpu.VMEM((bands, cached + 128), F32),
            pltpu.VMEM((bands, cached + 128), BF16),
            pltpu.VMEM((n_rows, n_query), F32),
            pltpu.VMEM((STEPS, n_rows, wide), BF16),
            pltpu.VMEM((STEPS, n_rows, wide), BF16),
            pltpu.VMEM((n_tensor, 16, cut), BF16),
            pltpu.VMEM((n_tensor, 16, half - cut), BF16),
            pltpu.VMEM((STEPS, 2, n_z, 16, cut), BF16),
            pltpu.VMEM((STEPS, n_z, 16, half - cut), BF16),
            pltpu.VMEM((STEPS, 16, cut), BF16),
            pltpu.VMEM((STEPS, n_z, 16, half - cut), BF16),
            pltpu.VMEM((STEPS, 16, half), BF16),
            pltpu.VMEM((STEPS, peers, 16, half // 4), BF16),
            pltpu.VMEM((STEPS, peers, 16, half // 4), BF16),
            pltpu.VMEM((STEPS, n_tensor, 16, units), BF16),
            pltpu.VMEM((STEPS, n_tensor, 16, units), BF16),
            pltpu.VMEM((STEPS, n_tensor, 16, units), BF16),
            pltpu.VMEM((STEPS, 16, 128), F32),
            pltpu.VMEM((STEPS, peers, 16, 128), F32),
        ]
        + [dma((STEPS, 3, n_z))] * 2
        + [dma((STEPS, n_z + 1))] * 2
        + [dma((STEPS, 3, n_z))] * 2
        + [dma((STEPS, n_z + 1))] * 2
        + [dma((STEPS,))] * 4
        + [dma((STEPS, n_z)), dma((STEPS, 2))]
        + [dma((STEPS, peers))] * 2
        + [dma((STEPS, n_tensor))] * 4
        + [dma((STEPS, peers))] * 2,
        compiler_params=pltpu.CompilerParams(
            collective_id=0, has_side_effects=True, vmem_limit_bytes=VMEM_LIMIT
        ),
        name="imagine",
    )(
        frame.reshape(rollouts, width),
        actions,
        owners,
        attn_gain.reshape(1, width),
        action_table,
        cache,
        w_query,
        w_keyval,
        w_out,
        policy_in,
        policy_mid,
        policy_head.reshape(policy_head.shape[1:]),
        policy_value,
    )
    return (latents.reshape(frame.shape), log_probs, values)


def solution(mesh):
    placed = (
        P(("grp", "row"), "tp", None),
        P(("grp", "row"), "tp", None, None),
        P(("grp", "row"), None),
        P(("grp", "row"), None),
        P(),
        P(None, "tp"),
        P(None, "tp"),
        P("tp", None),
        P(),
        P("row", None, "tp"),
        P("row", "tp", None),
        P("row", None, None),
        P("row", None),
    )
    return jax.shard_map(
        shards,
        mesh=mesh,
        in_specs=placed,
        out_specs=(
            P(("grp", "row"), "tp", None),
            P(("grp", "row"), None, None),
            P(("grp", "row"), None),
        ),
        check_vma=False,
    )
```

```python
import functools

import jax
import jax.numpy as jnp
from jax import lax
from jax.experimental import pallas as pl
from jax.experimental.pallas import tpu as pltpu
from jax.sharding import PartitionSpec as P

HD = 128
STEPS = 4
CAP = 2
EPS = 1e-05
MESH = pl.DeviceIdType.MESH
F32 = jnp.float32
BF16 = jnp.bfloat16
VMEM_LIMIT = 56 << 20


def rms_rows(values):
    return values * lax.rsqrt(jnp.mean(values * values, axis=-1, keepdims=True) + EPS)


def folded(rows):
    half = rows.shape[1] // 2
    return jnp.concatenate([rows[:, :half], rows[:, half:]], axis=0)


PAIR_COLUMNS = 512
FAR = {False: {1: 0, -1: 0, 2: 0, -2: 0, 3: 2, -3: -2, 4: 2}, True: {1: 0, -1: 0, 2: 0, -2: 0, 3: 2, -3: -2, -4: -2}}


def due(tree, k):
    return 0.0 if k == 0 else due(tree, tree[k]) + 2.0 + 0.8 * abs(k - tree[k])


def below(tree, k):
    return sorted([c for c in tree if tree[c] == k], key=lambda c: abs(c - k))


def halves(product, half, width):
    return product.reshape(-1, 2, 8, width)[:, half].reshape(-1, width)


def fold_dot(first, second, weight):
    half = weight.shape[0] // 2
    columns = weight.shape[1]
    cut = first.shape[1]
    left = jnp.dot(first, weight[:cut], preferred_element_type=F32)
    left = left + jnp.dot(second, weight[cut:half], preferred_element_type=F32)
    right = jnp.dot(first, weight[half : half + cut], preferred_element_type=F32)
    right = right + jnp.dot(second, weight[half + cut :], preferred_element_type=F32)
    return halves(left, 0, columns) + halves(right, 1, columns)


def silu(values):
    return values / (1.0 + jnp.exp(-values))


def kernel(
    n_z,
    peers,
    frame_ref,
    actions_ref,
    owners_ref,
    gain_ref,
    table_ref,
    cache_hbm,
    wq_hbm,
    wkv_hbm,
    wo_hbm,
    pin_hbm,
    pmid_hbm,
    head_ref,
    critic_ref,
    latents_ref,
    logp_ref,
    value_ref,
    cache_ref,
    wq_ref,
    wkv_ref,
    wo_ref,
    pin_ref,
    pmid_ref,
    embed,
    state,
    gath_p,
    gath_q,
    qkv,
    qkv_in,
    keys,
    vals,
    scores,
    weights,
    own_o,
    out_o,
    in_o,
    terms_p,
    terms_q,
    tree_p,
    tree_q,
    pair_p,
    pair_q,
    latent_rows,
    outgoing,
    arrived,
    partial,
    partial_in,
    hidden,
    answers,
    returned,
    ag_zs,
    ag_zr,
    ag_ys,
    ag_yr,
    rs_zs,
    rs_zr,
    rs_ys,
    rs_yr,
    q_send,
    q_recv,
    o_send,
    o_recv,
    l_send,
    l_recv,
    a_send,
    a_recv,
    h_send,
    h_recv,
    g_send,
    g_recv,
    b_send,
    b_recv,
    loaded,
):
    loads = [
        pltpu.make_async_copy(src, dst, loaded.at[i])
        for i, (src, dst) in enumerate(
            (
                (wq_hbm, wq_ref),
                (wkv_hbm, wkv_ref),
                (cache_hbm, cache_ref),
                (wo_hbm, wo_ref),
                (pin_hbm, pin_ref),
                (pmid_hbm, pmid_ref),
            )
        )
    ]
    for load in loads:
        load.start()
    tensor = lax.axis_index("tp")
    row = lax.axis_index("row")
    z = tensor // 2
    yh = lax.rem(tensor, 2)
    pair = {"tp": tensor + 1 - 2 * yh}
    rollouts, width = state.shape
    n_tensor = 2 * n_z
    tokens = n_tensor
    n_rows = tokens * rollouts
    cached = cache_ref.shape[2]
    last = n_tensor - 1
    cut = gath_p.shape[3]
    half = width // 2

    def plane(k):
        return lax.rem(z + k + 2 * n_z, n_z)

    def to_plane(k):
        return {"tp": plane(k) * 2 + yh}

    def slot_of(k, other):
        return plane(k) * 2 + (1 - yh if other else yh)

    def to_row(k):
        return {"row": lax.rem(row + k, peers)}

    def to_tensor(k):
        return {"tp": lax.rem(tensor + k, n_tensor)}

    barrier = pltpu.get_barrier_semaphore()
    for k in range(1, n_tensor):
        pl.semaphore_signal(barrier, inc=1, device_id=to_tensor(k), device_id_type=MESH)
    for k in range(1, peers):
        pl.semaphore_signal(barrier, inc=1, device_id=to_row(k), device_id_type=MESH)

    def copy(src, dst, send, recv, target):
        return pltpu.make_async_remote_copy(
            src_ref=src, dst_ref=dst, send_sem=send, recv_sem=recv, device_id=target, device_id_type=MESH
        )

    state[...] = frame_ref[...].astype(F32)
    keys[...] = jnp.zeros_like(keys)
    vals[...] = jnp.zeros_like(vals)
    iota_r = lax.broadcasted_iota(jnp.int32, (n_rows, n_rows), 0)
    iota_c = lax.broadcasted_iota(jnp.int32, (n_rows, n_rows), 1)
    by_rollout = (lax.rem(iota_r, tokens) * rollouts + iota_r // tokens == iota_c).astype(F32).astype(BF16)
    by_token = (lax.rem(iota_c, tokens) * rollouts + iota_c // tokens == iota_r).astype(F32).astype(BF16)

    eye = lax.broadcasted_iota(jnp.int32, (rollouts, rollouts), 0) == lax.broadcasted_iota(
        jnp.int32, (rollouts, rollouts), 1
    )
    owner = jnp.sum(jnp.where(eye, owners_ref[...], 0), axis=1, keepdims=True)
    hit = (lax.broadcasted_iota(jnp.int32, (rollouts, 128), 1) == owner).astype(F32)
    later = (
        lax.broadcasted_iota(jnp.int32, (rollouts, rollouts), 0)
        > lax.broadcasted_iota(jnp.int32, (rollouts, rollouts), 1)
    ).astype(F32)
    before = jnp.zeros((rollouts, 128), F32)
    for r in range(rollouts):
        before = before + later[:, r : r + 1] * hit[r : r + 1, :]
    place_of = jnp.sum(before * hit, axis=1, keepdims=True)
    eighths = 16 // CAP
    spots = peers * 16
    tn = (((0,), (0,)), ((), ()))
    nt = (((1,), (1,)), ((), ()))
    pl.semaphore_wait(barrier, peers + n_tensor - 2)

    def spread_out(q, k):
        mine = latent_rows.at[q]
        for c in below(FAR[False], k):
            copy(mine, mine, l_send.at[q, c % n_z], l_recv.at[q, 0], to_plane(c - k)).start()
        copy(mine, mine, l_send.at[q, 0], l_recv.at[q, 1], pair).start()

    def spread_sent(q, k):
        mine = latent_rows.at[q]
        for c in below(FAR[False], k):
            copy(mine, mine, l_send.at[q, c % n_z], l_recv.at[q, 0], to_plane(c - k)).wait_send()
        copy(mine, mine, l_send.at[q, 0], l_recv.at[q, 1], pair).wait_send()

    def spread_start(q):
        @pl.when(tensor == last)
        def _():
            spread_out(q, 0)

    def spread_on(q):
        mine = latent_rows.at[q]
        for k in FAR[False]:

            @pl.when(tensor == (last + 2 * k) % n_tensor)
            def _():
                copy(mine, mine, l_send.at[q, 0], l_recv.at[q, 0], pair).wait_recv()
                spread_out(q, k)

        @pl.when(yh == 0)
        def _():
            copy(mine, mine, l_send.at[q, 0], l_recv.at[q, 1], pair).wait_recv()

    def spread_end(q):
        for k in [0] + list(FAR[False]):

            @pl.when(tensor == (last + 2 * k) % n_tensor)
            def _():
                spread_sent(q, k)

    def route(q, k):
        return copy(
            outgoing.at[q, lax.rem(row + k, peers)], arrived.at[q, row], a_send.at[q, k], a_recv.at[q, k], to_row(k)
        )

    def route_start(q):
        wide = half // 4
        i = lax.broadcasted_iota(jnp.int32, (16, spots), 1)
        j = lax.broadcasted_iota(jnp.int32, (16, spots), 0)
        owner2 = jnp.concatenate([owner, owner], axis=0)
        place2 = jnp.concatenate([place_of, place_of], axis=0)
        chosen = (i // 16 == owner2) & (lax.rem(i, CAP).astype(F32) == place2)
        eighth = lax.rem(i // CAP, eighths)
        built = jnp.zeros((spots, wide), F32)
        for quarter in range(4):
            hot = (chosen & (eighth == (j // rollouts) * 4 + quarter)).astype(F32).astype(BF16)
            built = built + lax.dot_general(
                hot, latent_rows[q, :, quarter * wide : (quarter + 1) * wide], tn, preferred_element_type=F32
            )
        outgoing[q] = built.astype(BF16).reshape(peers, 16, wide)
        arrived[q, row] = outgoing[q, row]
        for k in range(1, peers):
            route(q, k).start()

    def to_units(q, k):
        return copy(
            partial.at[q, lax.rem(tensor + k, n_tensor)],
            partial_in.at[q, k],
            h_send.at[q, k],
            h_recv.at[q, k],
            to_tensor(k),
        )

    def inner_start(q):
        for k in range(1, peers):
            origin = arrived.at[q, lax.rem(row + peers - k, peers)]
            copy(origin, origin, a_send.at[q, k], a_recv.at[q, k], to_row(k)).wait_recv()
        wide = half // 4
        rows = arrived[q].reshape(spots, wide)
        n_inner = pin_ref.shape[2]
        at_row = lax.rem(lax.broadcasted_iota(jnp.int32, (spots, n_inner), 0) // CAP, eighths)
        picked = jnp.zeros((spots, n_inner), F32)
        for e in range(eighths):
            product = jnp.dot(rows, pin_ref[0, e * wide : (e + 1) * wide, :], preferred_element_type=F32)
            picked = picked + jnp.where(at_row == e, product, 0.0)
        i = lax.broadcasted_iota(jnp.int32, (16, spots), 1)
        j = lax.broadcasted_iota(jnp.int32, (16, spots), 0)
        gather = ((i // 16 == j // CAP) & (lax.rem(i, CAP) == lax.rem(j, CAP))).astype(F32)
        before_silu = jnp.dot(gather, picked, preferred_element_type=F32, precision=lax.Precision.HIGHEST)
        inner = silu(before_silu).astype(BF16)
        units = partial.shape[3]
        product = jnp.dot(inner, pmid_ref[0], preferred_element_type=F32).astype(BF16)
        for t in range(n_tensor):
            partial[q, t] = product[:, t * units : (t + 1) * units]
        for k in range(1, n_tensor):
            to_units(q, k).start()

    def share(q, k):
        mine = hidden.at[q, tensor]
        return copy(mine, mine, g_send.at[q, k], g_recv.at[q, k], to_tensor(k))

    def hidden_start(q):
        summed = partial[q, tensor].astype(F32)
        for k in range(1, n_tensor):
            to_units(q, k).wait_recv()
            summed = summed + partial_in[q, k].astype(F32)
        hidden[q, tensor] = silu(summed).astype(BF16)
        for k in range(1, n_tensor):
            share(q, k).start()

    def reply(q, k):
        return copy(answers.at[q], returned.at[q, row], b_send.at[q, k], b_recv.at[q, k], to_row(k))

    def heads_start(q):
        for k in range(1, n_tensor):
            origin = hidden.at[q, lax.rem(tensor + n_tensor - k, n_tensor)]
            copy(origin, origin, g_send.at[q, k], g_recv.at[q, k], to_tensor(k)).wait_recv()
        whole = jnp.concatenate([hidden[q, t] for t in range(n_tensor)], axis=1)
        logits = lax.dot_general(whole, head_ref[...], nt, preferred_element_type=F32)
        value = jnp.sum(whole.astype(F32) * critic_ref[...].astype(F32), axis=1, keepdims=True)
        peak = jnp.max(logits, axis=1, keepdims=True)
        logp = logits - (peak + jnp.log(jnp.sum(jnp.exp(logits - peak), axis=1, keepdims=True)))
        blank = jnp.zeros((16, 128 - logits.shape[1] - 1), F32)
        answers[q] = jnp.concatenate([logp, value, blank], axis=1)
        returned[q, row] = answers[q]
        for k in range(1, peers):
            reply(q, k).start()

    def policy_end(q):
        for k in range(1, peers):
            origin = returned.at[q, lax.rem(row + peers - k, peers)]
            copy(origin, origin, b_send.at[q, k], b_recv.at[q, k], to_row(k)).wait_recv()
        spread_end(q)
        for k in range(1, peers):
            route(q, k).wait_send()
            reply(q, k).wait_send()
        for k in range(1, n_tensor):
            to_units(q, k).wait_send()
            share(q, k).wait_send()

    def gather(s):
        own, other, front = FAR[False], FAR[True], FAR[False]
        sent = []

        def block(stream, k):
            return (gath_q if stream == 2 else gath_p).at[s, slot_of(-k, stream == 1)]

        def go(ref, send, recv, target):
            moved = copy(ref, ref, send, recv, target)
            moved.start()
            sent.append(moved)

        def spread(stream, tree, k):
            for c in below(tree, k):
                go(block(stream, k), ag_zs.at[s, stream, c % n_z], ag_zr.at[s, stream, c % n_z], to_plane(c - k))

        def pass_on(k):
            go(block(2, k), ag_ys.at[s, k % n_z], ag_yr.at[s, k % n_z], pair)

        go(block(0, 0), ag_ys.at[s, n_z], ag_yr.at[s, n_z], pair)
        spread(2, front, 0)
        pass_on(0)
        spread(0, own, 0)
        events = [(due(front, k), 2, k) for k in front] + [(due(own, k), 0, k) for k in own]
        events += [(3.0 + due(other, k), 1, k) for k in [0] + list(other)]
        for _, stream, k in sorted(events):
            ref = block(stream, k)
            if k == 0:
                copy(ref, ref, ag_ys.at[s, n_z], ag_yr.at[s, n_z], pair).wait_recv()
            else:
                copy(ref, ref, ag_zs.at[s, stream, k % n_z], ag_zr.at[s, stream, k % n_z], pair).wait_recv()
            spread(stream, (own, other, front)[stream], k)
            if stream == 2:
                pass_on(k)
        for k in [0] + list(front):
            ref = gath_q.at[s, slot_of(-k, True)]
            copy(ref, ref, ag_ys.at[s, k % n_z], ag_yr.at[s, k % n_z], pair).wait_recv()
        return sent

    def scatter(s, hooks):
        trees = (FAR[False], FAR[True], FAR[False])
        sent = []

        def go(src, dst, send, recv, target):
            moved = copy(src, dst, send, recv, target)
            moved.start()
            sent.append(moved)

        for k in sorted(trees[2], key=lambda k: -due(trees[2], k)) + [0]:
            go(
                terms_q.at[slot_of(-k, True)],
                pair_q.at[s, k % n_z],
                rs_ys.at[s, k % n_z],
                rs_yr.at[s, k % n_z],
                pair,
            )
        deepest = max(due(trees[0], k) for k in trees[0])
        events = []
        for stream, offset in ((0, 1.0), (1, -0.1), (2, 3.0)):
            events += [(offset + deepest - due(trees[stream], k), stream, k) for k in [0] + list(trees[stream])]
        ends = {}
        for number, (_, stream, k) in enumerate(sorted(events)):
            if number in (len(events) // 2, len(events) * 7 // 8):
                hooks.pop(0)()
            tree = trees[stream]
            terms = terms_q if stream == 2 else terms_p
            slot = slot_of(-k, stream == 1)

            def landing(c):
                return tree_q.at[s, c % n_z] if stream == 2 else tree_p.at[s, stream, c % n_z]

            total = None
            children = below(tree, k)
            if stream == 2 or children or k == 0:
                total = terms[slot].astype(F32)
            if stream == 2:
                ref = pair_q.at[s, k % n_z]
                copy(ref, ref, rs_ys.at[s, k % n_z], rs_yr.at[s, k % n_z], pair).wait_recv()
                total = total + pair_q[s, k % n_z].astype(F32)
            for c in children:
                ref = landing(c)
                copy(ref, ref, rs_zs.at[s, stream, c % n_z], rs_zr.at[s, stream, c % n_z], pair).wait_recv()
                total = total + ref[...].astype(F32)
            if k:
                if total is not None:
                    terms[slot] = total.astype(BF16)
                go(
                    terms.at[slot],
                    landing(k),
                    rs_zs.at[s, stream, k % n_z],
                    rs_zr.at[s, stream, k % n_z],
                    to_plane(tree[k] - k),
                )
            elif stream == 1:
                terms[slot] = total.astype(BF16)
                go(terms.at[slot], pair_p.at[s], rs_ys.at[s, n_z], rs_yr.at[s, n_z], pair)
            else:
                ends[stream] = total
        ref = pair_p.at[s]
        copy(ref, ref, rs_ys.at[s, n_z], rs_yr.at[s, n_z], pair).wait_recv()
        first = ends[0] + pair_p[s].astype(F32)
        both = jnp.concatenate([first, ends[2]], axis=1)
        return jnp.concatenate([both[:rollouts], both[rollouts:]], axis=1), sent

    def embed_actions(s):
        at_step = lax.broadcasted_iota(jnp.int32, actions_ref.shape, 0) == s
        picked = jnp.sum(jnp.where(at_step, actions_ref[...], 0), axis=0, keepdims=True)
        code = lax.broadcasted_iota(jnp.int32, (table_ref.shape[0], rollouts), 0) == picked
        embed[...] = lax.dot_general(
            code.astype(F32).astype(BF16), table_ref[...], tn, preferred_element_type=F32
        )

    def step(s, carry):
        inputs = (state[...] + embed[...]).astype(BF16).astype(F32)
        state[...] = inputs
        normed = folded(rms_rows(inputs) * gain_ref[...]).astype(BF16)
        gath_p[s, tensor] = normed[:, :cut]
        gath_q[s, tensor] = normed[:, cut:]
        gathered = gather(s)

        @pl.when(s == 0)
        def _():
            for load in loads:
                load.wait()

        first = gath_p[s].reshape(n_tensor * 16, cut)
        second = gath_q[s].reshape(n_tensor * 16, half - cut)
        query = (fold_dot(first, second, wq_ref) * HD ** (-0.5)).astype(BF16)
        keyval = fold_dot(first, second, wkv_ref).astype(BF16)
        n_query = query.shape[1]
        qkv[s, :, :n_query] = jnp.dot(by_rollout, query, preferred_element_type=F32).astype(BF16)
        qkv[s, :, n_query:] = jnp.dot(by_rollout, keyval, preferred_element_type=F32).astype(BF16)
        swap = copy(qkv.at[s], qkv_in.at[s], q_send.at[s], q_recv.at[s], pair)
        swap.start()

        heads = n_query // HD
        per = heads * tokens

        def grouped(source, r):
            rows = slice(r * tokens, (r + 1) * tokens)
            return jnp.concatenate([source[s, rows, h * HD : (h + 1) * HD] for h in range(heads)], axis=0)

        def band(r):
            return slice(r * per, (r + 1) * per)

        def score_cached(group, source, r):
            scores[group, band(r), :cached] = lax.dot_general(
                grouped(source, r), cache_ref[r, 0, :, :HD], nt, preferred_element_type=F32
            )

        def score_new(group, source, r):
            scores[group, band(r), cached:] = lax.dot_general(
                grouped(source, r), keys[r], nt, preferred_element_type=F32
            )

        for r in range(rollouts):
            score_cached(0, qkv, r)

        @pl.when(s > 0)
        def _():
            spread_on(s - 1)
            route_start(s - 1)

        for moved in gathered:
            moved.wait_send()
        swap.wait()

        own_kv = qkv[s, :, n_query:].astype(F32)
        other_kv = qkv_in[s, :, n_query:].astype(F32)
        new_key = jnp.where(yh == 0, own_kv, other_kv).astype(BF16)
        new_val = jnp.where(yh == 0, other_kv, own_kv).astype(BF16)
        place = pl.ds(pl.multiple_of(s * tokens, tokens), tokens)
        for r in range(rollouts):
            rows = slice(r * tokens, (r + 1) * tokens)
            keys[r, place, :] = new_key[rows]
            vals[r, place, :] = new_val[rows]
            score_cached(1, qkv_in, r)
            score_new(1, qkv_in, r)
            score_new(0, qkv, r)

        def soften(group):
            fresh = scores[group, :, cached:]
            key_pos = lax.broadcasted_iota(jnp.int32, fresh.shape, 1)
            query_pos = lax.rem(lax.broadcasted_iota(jnp.int32, fresh.shape, 0), tokens)
            allowed = (key_pos <= s * tokens + query_pos) & (yh == 0)
            fresh = jnp.where(allowed, fresh, -jnp.inf)
            old = scores[group, :, :cached]
            top = jnp.maximum(jnp.max(old, axis=1, keepdims=True), jnp.max(fresh, axis=1, keepdims=True))
            old = jnp.exp(old - top)
            fresh = jnp.exp(fresh - top)
            total = jnp.sum(old, axis=1, keepdims=True) + jnp.sum(fresh, axis=1, keepdims=True)
            weights[group, :, :cached] = old.astype(BF16)
            weights[group, :, cached:] = fresh.astype(BF16)
            return top, total, 1.0 / total

        def attend(group, r, inverse):
            summed = jnp.dot(weights[group, band(r), :cached], cache_ref[r, 0, :, HD:], preferred_element_type=F32)
            summed = summed + jnp.dot(weights[group, band(r), cached:], vals[r], preferred_element_type=F32)
            return summed * inverse[band(r)]

        far_top, far_total, inverse = soften(1)
        lane = lax.broadcasted_iota(jnp.int32, (tokens, HD), 1)
        for r in range(rollouts):
            rows = slice(r * tokens, (r + 1) * tokens)
            summed = attend(1, r, inverse)
            stats = jnp.zeros((tokens, HD), F32)
            for h in range(heads):
                at = slice(h * tokens, (h + 1) * tokens)
                out_o[s, rows, h * HD : (h + 1) * HD] = summed[at].astype(BF16)
                for first, column in ((8 * h, far_top), (8 * h + 3, far_total)):
                    left = column[band(r)][at]
                    for piece in range(3):
                        term = left.astype(BF16).astype(F32)
                        left = left - term
                        stats = jnp.where(lane == first + piece, term, stats)
            out_o[s, rows, n_query:] = stats.astype(BF16)
        swap = copy(out_o.at[s], in_o.at[s], o_send.at[s], o_recv.at[s], pair)
        swap.start()

        top, total, inverse = soften(0)
        for r in range(rollouts):
            rows = slice(r * tokens, (r + 1) * tokens)
            summed = attend(0, r, inverse)
            for h in range(heads):
                own_o[rows, h * HD : (h + 1) * HD] = summed[h * tokens : (h + 1) * tokens]

        @pl.when(s > 0)
        def _():
            inner_start(s - 1)

        embed_actions(s + 1)
        swap.wait()

        stats = in_o[s, :, n_query:].astype(F32)
        top4 = top.reshape(rollouts, heads, tokens, 1)
        total4 = total.reshape(rollouts, heads, tokens, 1)
        joined = []
        for h in range(heads):
            pick = [stats[:, 8 * h + i : 8 * h + i + 1] for i in range(6)]
            far_top = pick[0] + pick[1] + pick[2]
            far_total = pick[3] + pick[4] + pick[5]
            near_top = top4[:, h].reshape(n_rows, 1)
            near_total = total4[:, h].reshape(n_rows, 1)
            peak = jnp.maximum(near_top, far_top)
            near = near_total * jnp.exp(near_top - peak)
            far = far_total * jnp.exp(far_top - peak)
            both = 1.0 / (near + far)
            cols = slice(h * HD, (h + 1) * HD)
            joined.append(own_o[:, cols] * (near * both) + in_o[s, :, cols].astype(F32) * (far * both))
        attended = jnp.concatenate(joined, axis=1).astype(BF16)
        attended = jnp.dot(by_token, attended, preferred_element_type=F32).astype(BF16)

        tile = 512 if half % 512 == 0 else HD
        for j in range(half // tile):
            at = slice(j * tile, (j + 1) * tile)
            also = slice(half + j * tile, half + (j + 1) * tile)
            left = jnp.dot(attended, wo_ref[:, at], preferred_element_type=F32).reshape(tokens, rollouts, tile)
            right = jnp.dot(attended, wo_ref[:, also], preferred_element_type=F32).reshape(tokens, rollouts, tile)
            part = jnp.concatenate([left, right], axis=1).astype(BF16)
            if j * tile < cut:
                terms_p[:, :, at] = part
            else:
                terms_q[:, :, j * tile - cut : (j + 1) * tile - cut] = part

        def hidden_hook():
            @pl.when(s > 0)
            def _():
                hidden_start(s - 1)

        def heads_hook():
            @pl.when(s > 0)
            def _():
                heads_start(s - 1)

        reduced, sent = scatter(s, [hidden_hook, heads_hook])
        updated = (state[...] + reduced).astype(BF16).astype(F32)
        state[...] = updated

        @pl.when(tensor == last)
        def _():
            latent_rows[s] = folded(rms_rows(updated)).astype(BF16)

        spread_start(s)
        for moved in sent:
            moved.wait_send()
        return carry

    embed_actions(0)
    lax.fori_loop(0, STEPS, step, 0)
    latents_ref[...] = state[...].astype(BF16)
    final = STEPS - 1
    spread_on(final)
    route_start(final)
    inner_start(final)
    hidden_start(final)
    heads_start(final)
    i = lax.broadcasted_iota(jnp.int32, (rollouts, spots), 1)
    mine = (i // 16 == owner) & (lax.rem(i, CAP).astype(F32) == place_of) & (lax.rem(i // CAP, eighths) == row)
    mine = mine.astype(F32)
    lane = lax.broadcasted_iota(jnp.int32, (rollouts, STEPS), 1)
    all_values = jnp.zeros((rollouts, STEPS), F32)
    n_actions = head_ref.shape[0]
    for q in range(STEPS):
        policy_end(q)
        now = jnp.dot(
            mine, returned[q].reshape(spots, 128), preferred_element_type=F32, precision=lax.Precision.HIGHEST
        )
        logp_ref[:, q, :] = now[:, :n_actions]
        all_values = jnp.where(lane == q, now[:, n_actions : n_actions + 1], all_values)
    value_ref[...] = all_values


def shards(
    frame,
    cache,
    actions,
    owners,
    attn_gain,
    w_query,
    w_keyval,
    w_out,
    action_table,
    policy_in,
    policy_mid,
    policy_head,
    policy_value,
):
    n_tensor = lax.axis_size("tp")
    peers = lax.axis_size("row")
    n_z = n_tensor // 2
    rollouts, _, width = frame.shape
    half = width // 2
    n_rows = n_tensor * rollouts
    n_query = w_query.shape[1]
    wide = n_query + w_keyval.shape[1]
    cached = cache.shape[2]
    bands = n_rows * (n_query // HD)
    units = policy_mid.shape[2] // n_tensor
    cut = PAIR_COLUMNS
    vmem = pl.BlockSpec(memory_space=pltpu.VMEM)
    dma = pltpu.SemaphoreType.DMA
    latents, log_probs, values = pl.pallas_call(
        functools.partial(kernel, n_z, peers),
        out_shape=(
            jax.ShapeDtypeStruct((rollouts, width), BF16),
            jax.ShapeDtypeStruct((rollouts, STEPS, policy_head.shape[2]), F32),
            jax.ShapeDtypeStruct((rollouts, STEPS), F32),
        ),
        in_specs=[vmem] * 5 + [pl.BlockSpec(memory_space=pl.ANY)] * 6 + [vmem] * 2,
        out_specs=(vmem,) * 3,
        scratch_shapes=[
            pltpu.VMEM(big.shape, BF16)
            for big in (cache, w_query, w_keyval, w_out, policy_in, policy_mid)
        ]
        + [
            pltpu.VMEM((rollouts, width), F32),
            pltpu.VMEM((rollouts, width), F32),
            pltpu.VMEM((STEPS, n_tensor, 16, cut), BF16),
            pltpu.VMEM((STEPS, n_tensor, 16, half - cut), BF16),
            pltpu.VMEM((STEPS, n_rows, wide), BF16),
            pltpu.VMEM((STEPS, n_rows, wide), BF16),
            pltpu.VMEM((rollouts, 128, HD), BF16),
            pltpu.VMEM((rollouts, 128, HD), BF16),
            pltpu.VMEM((2, bands, cached + 128), F32),
            pltpu.VMEM((2, bands, cached + 128), BF16),
            pltpu.VMEM((n_rows, n_query), F32),
            pltpu.VMEM((STEPS, n_rows, wide), BF16),
            pltpu.VMEM((STEPS, n_rows, wide), BF16),
            pltpu.VMEM((n_tensor, 16, cut), BF16),
            pltpu.VMEM((n_tensor, 16, half - cut), BF16),
            pltpu.VMEM((STEPS, 2, n_z, 16, cut), BF16),
            pltpu.VMEM((STEPS, n_z, 16, half - cut), BF16),
            pltpu.VMEM((STEPS, 16, cut), BF16),
            pltpu.VMEM((STEPS, n_z, 16, half - cut), BF16),
            pltpu.VMEM((STEPS, 16, half), BF16),
            pltpu.VMEM((STEPS, peers, 16, half // 4), BF16),
            pltpu.VMEM((STEPS, peers, 16, half // 4), BF16),
            pltpu.VMEM((STEPS, n_tensor, 16, units), BF16),
            pltpu.VMEM((STEPS, n_tensor, 16, units), BF16),
            pltpu.VMEM((STEPS, n_tensor, 16, units), BF16),
            pltpu.VMEM((STEPS, 16, 128), F32),
            pltpu.VMEM((STEPS, peers, 16, 128), F32),
        ]
        + [dma((STEPS, 3, n_z))] * 2
        + [dma((STEPS, n_z + 1))] * 2
        + [dma((STEPS, 3, n_z))] * 2
        + [dma((STEPS, n_z + 1))] * 2
        + [dma((STEPS,))] * 4
        + [dma((STEPS, n_z)), dma((STEPS, 2))]
        + [dma((STEPS, peers))] * 2
        + [dma((STEPS, n_tensor))] * 4
        + [dma((STEPS, peers))] * 2
        + [dma((6,))],
        compiler_params=pltpu.CompilerParams(
            collective_id=0, has_side_effects=True, vmem_limit_bytes=VMEM_LIMIT
        ),
        name="imagine",
    )(
        frame.reshape(rollouts, width),
        actions.T,
        owners.T,
        attn_gain.reshape(1, width),
        action_table,
        cache,
        w_query,
        w_keyval,
        w_out,
        policy_in,
        policy_mid,
        policy_head.reshape(policy_head.shape[1:]).T,
        policy_value,
    )
    return (latents.reshape(frame.shape), log_probs, values)


def solution(mesh):
    placed = (
        P(("grp", "row"), "tp", None),
        P(("grp", "row"), "tp", None, None),
        P(("grp", "row"), None),
        P(("grp", "row"), None),
        P(),
        P(None, "tp"),
        P(None, "tp"),
        P("tp", None),
        P(),
        P("row", None, "tp"),
        P("row", "tp", None),
        P("row", None, None),
        P("row", None),
    )
    return jax.shard_map(
        shards,
        mesh=mesh,
        in_specs=placed,
        out_specs=(
            P(("grp", "row"), "tp", None),
            P(("grp", "row"), None, None),
            P(("grp", "row"), None),
        ),
        check_vma=False,
    )
```

```python
import functools
import typing

import jax
import jax.numpy as jnp
from jax import lax
from jax.experimental import pallas as pl
from jax.experimental.pallas import tpu as pltpu
from jax.sharding import PartitionSpec as P

HD = 128
STEPS = 4
CAP = 2
EPS = 1e-05
MESH = pl.DeviceIdType.MESH
F32 = jnp.float32
BF16 = jnp.bfloat16
VMEM_LIMIT = 56 << 20


def rms_rows(values):
    return values * lax.rsqrt(jnp.mean(values * values, axis=-1, keepdims=True) + EPS)


def folded(rows):
    half = rows.shape[1] // 2
    return jnp.concatenate([rows[:, :half], rows[:, half:]], axis=0)


PAIR_COLUMNS = 512
FAR = {False: {1: 0, -1: 0, 2: 0, -2: 0, 3: 2, -3: -2, 4: 2}, True: {1: 0, -1: 0, 2: 0, -2: 0, 3: 2, -3: -2, -4: -2}}


BATCHES = ((0, 1, 2), (3,))


class Batch(typing.NamedTuple):
    steps: tuple
    outgoing: typing.Any
    arrived: typing.Any
    partial: typing.Any
    partial_in: typing.Any
    hidden: typing.Any
    answers: typing.Any
    returned: typing.Any
    a_send: typing.Any
    a_recv: typing.Any
    h_send: typing.Any
    h_recv: typing.Any
    g_send: typing.Any
    g_recv: typing.Any
    b_send: typing.Any
    b_recv: typing.Any


def due(tree, k):
    return 0.0 if k == 0 else due(tree, tree[k]) + 2.0 + 0.8 * abs(k - tree[k])


def below(tree, k):
    return sorted([c for c in tree if tree[c] == k], key=lambda c: abs(c - k))


def halves(product, half, width):
    return product.reshape(-1, 2, 8, width)[:, half].reshape(-1, width)


def fold_dot(first, second, weight):
    half = weight.shape[0] // 2
    columns = weight.shape[1]
    cut = first.shape[1]
    left = jnp.dot(first, weight[:cut], preferred_element_type=F32)
    left = left + jnp.dot(second, weight[cut:half], preferred_element_type=F32)
    right = jnp.dot(first, weight[half : half + cut], preferred_element_type=F32)
    right = right + jnp.dot(second, weight[half + cut :], preferred_element_type=F32)
    return halves(left, 0, columns) + halves(right, 1, columns)


def silu(values):
    return values / (1.0 + jnp.exp(-values))


def kernel(
    n_z,
    peers,
    frame_ref,
    actions_ref,
    owners_ref,
    gain_ref,
    table_ref,
    cache_hbm,
    wq_hbm,
    wkv_hbm,
    wo_hbm,
    pin_hbm,
    pmid_hbm,
    head_ref,
    critic_ref,
    latents_ref,
    logp_ref,
    value_ref,
    cache_ref,
    wq_ref,
    wkv_ref,
    wo_ref,
    pin_ref,
    pmid_ref,
    embed,
    state,
    gath_p,
    gath_q,
    qkv,
    qkv_in,
    keys,
    vals,
    scores,
    weights,
    own_o,
    out_o,
    in_o,
    terms_p,
    terms_q,
    tree_p,
    tree_q,
    pair_p,
    pair_q,
    latent_rows,
    ag_zs,
    ag_zr,
    ag_ys,
    ag_yr,
    rs_zs,
    rs_zr,
    rs_ys,
    rs_yr,
    q_send,
    q_recv,
    o_send,
    o_recv,
    l_send,
    l_recv,
    loaded,
    *batch_refs,
):
    batches = [Batch(steps, *batch_refs[i * 15 : (i + 1) * 15]) for i, steps in enumerate(BATCHES)]
    loads = [
        pltpu.make_async_copy(src, dst, loaded.at[i])
        for i, (src, dst) in enumerate(
            (
                (wq_hbm, wq_ref),
                (wkv_hbm, wkv_ref),
                (cache_hbm, cache_ref),
                (wo_hbm, wo_ref),
                (pin_hbm, pin_ref),
                (pmid_hbm, pmid_ref),
            )
        )
    ]
    for load in loads:
        load.start()
    tensor = lax.axis_index("tp")
    row = lax.axis_index("row")
    z = tensor // 2
    yh = lax.rem(tensor, 2)
    pair = {"tp": tensor + 1 - 2 * yh}
    rollouts, width = state.shape
    n_tensor = 2 * n_z
    tokens = n_tensor
    n_rows = tokens * rollouts
    cached = cache_ref.shape[2]
    last = n_tensor - 1
    cut = gath_p.shape[3]
    half = width // 2

    def plane(k):
        return lax.rem(z + k + 2 * n_z, n_z)

    def to_plane(k):
        return {"tp": plane(k) * 2 + yh}

    def slot_of(k, other):
        return plane(k) * 2 + (1 - yh if other else yh)

    def to_row(k):
        return {"row": lax.rem(row + k, peers)}

    def to_tensor(k):
        return {"tp": lax.rem(tensor + k, n_tensor)}

    barrier = pltpu.get_barrier_semaphore()
    for k in range(1, n_tensor):
        pl.semaphore_signal(barrier, inc=1, device_id=to_tensor(k), device_id_type=MESH)
    for k in range(1, peers):
        pl.semaphore_signal(barrier, inc=1, device_id=to_row(k), device_id_type=MESH)

    def copy(src, dst, send, recv, target):
        return pltpu.make_async_remote_copy(
            src_ref=src, dst_ref=dst, send_sem=send, recv_sem=recv, device_id=target, device_id_type=MESH
        )

    state[...] = frame_ref[...].astype(F32)
    keys[...] = jnp.zeros_like(keys)
    vals[...] = jnp.zeros_like(vals)
    iota_r = lax.broadcasted_iota(jnp.int32, (n_rows, n_rows), 0)
    iota_c = lax.broadcasted_iota(jnp.int32, (n_rows, n_rows), 1)
    by_rollout = (lax.rem(iota_r, tokens) * rollouts + iota_r // tokens == iota_c).astype(F32).astype(BF16)
    by_token = (lax.rem(iota_c, tokens) * rollouts + iota_c // tokens == iota_r).astype(F32).astype(BF16)

    eye = lax.broadcasted_iota(jnp.int32, (rollouts, rollouts), 0) == lax.broadcasted_iota(
        jnp.int32, (rollouts, rollouts), 1
    )
    owner = jnp.sum(jnp.where(eye, owners_ref[...], 0), axis=1, keepdims=True)
    hit = (lax.broadcasted_iota(jnp.int32, (rollouts, 128), 1) == owner).astype(F32)
    later = (
        lax.broadcasted_iota(jnp.int32, (rollouts, rollouts), 0)
        > lax.broadcasted_iota(jnp.int32, (rollouts, rollouts), 1)
    ).astype(F32)
    before = jnp.zeros((rollouts, 128), F32)
    for r in range(rollouts):
        before = before + later[:, r : r + 1] * hit[r : r + 1, :]
    place_of = jnp.sum(before * hit, axis=1, keepdims=True)
    eighths = 16 // CAP
    spots = peers * 16
    tn = (((0,), (0,)), ((), ()))
    nt = (((1,), (1,)), ((), ()))
    pl.semaphore_wait(barrier, peers + n_tensor - 2)

    def spread_across(q, k):
        mine = latent_rows.at[q]
        return copy(mine, mine, l_send.at[q, k], l_recv.at[q, 0], to_plane(k))

    def spread_pair(q):
        mine = latent_rows.at[q]
        return copy(mine, mine, l_send.at[q, 0], l_recv.at[q, 1], pair)

    far_first = sorted(range(1, n_z), key=lambda k: -min(k, n_z - k))

    def spread_start(q):
        @pl.when(tensor == last)
        def _():
            for k in far_first:
                spread_across(q, k).start()
            spread_pair(q).start()

    def spread_on(q):
        @pl.when((yh == 1) & (tensor != last))
        def _():
            spread_across(q, 1).wait_recv()
            spread_pair(q).start()

    def spread_end(q):
        @pl.when(yh == 0)
        def _():
            spread_pair(q).wait_recv()

    def spread_sent(q):
        @pl.when(yh == 1)
        def _():
            spread_pair(q).wait_send()

        @pl.when(tensor == last)
        def _():
            for k in far_first:
                spread_across(q, k).wait_send()

    def route(b, k):
        return copy(b.outgoing.at[lax.rem(row + k, peers)], b.arrived.at[row], b.a_send.at[k], b.a_recv.at[k], to_row(k))

    def route_start(b):
        wide = half // 4
        i = lax.broadcasted_iota(jnp.int32, (16, spots), 1)
        j = lax.broadcasted_iota(jnp.int32, (16, spots), 0)
        owner2 = jnp.concatenate([owner, owner], axis=0)
        place2 = jnp.concatenate([place_of, place_of], axis=0)
        chosen = (i // 16 == owner2) & (lax.rem(i, CAP).astype(F32) == place2)
        eighth = lax.rem(i // CAP, eighths)
        hots = [
            (chosen & (eighth == (j // rollouts) * 4 + quarter)).astype(F32).astype(BF16) for quarter in range(4)
        ]
        for n, q in enumerate(b.steps):
            built = jnp.zeros((spots, wide), F32)
            for quarter in range(4):
                built = built + lax.dot_general(
                    hots[quarter],
                    latent_rows[q, :, quarter * wide : (quarter + 1) * wide],
                    tn,
                    preferred_element_type=F32,
                )
            b.outgoing[:, n * 16 : (n + 1) * 16, :] = built.astype(BF16).reshape(peers, 16, wide)
        for k in range(1, peers):
            route(b, k).start()
        b.arrived[row] = b.outgoing[row]

    def to_units(b, k):
        return copy(
            b.partial.at[lax.rem(tensor + k, n_tensor)], b.partial_in.at[k], b.h_send.at[k], b.h_recv.at[k], to_tensor(k)
        )

    def inner_start(b):
        for k in range(1, peers):
            origin = b.arrived.at[lax.rem(row + peers - k, peers)]
            copy(origin, origin, b.a_send.at[k], b.a_recv.at[k], to_row(k)).wait_recv()
        wide = half // 4
        tall = len(b.steps) * 16
        rows = b.arrived[...].reshape(peers * tall, wide)
        n_inner = pin_ref.shape[2]
        at_row = lax.rem(lax.broadcasted_iota(jnp.int32, (peers * tall, n_inner), 0) // CAP, eighths)
        picked = jnp.zeros((peers * tall, n_inner), F32)
        for e in range(eighths):
            product = jnp.dot(rows, pin_ref[0, e * wide : (e + 1) * wide, :], preferred_element_type=F32)
            picked = picked + jnp.where(at_row == e, product, 0.0)
        i = lax.broadcasted_iota(jnp.int32, (tall, peers * tall), 1)
        j = lax.broadcasted_iota(jnp.int32, (tall, peers * tall), 0)
        collect = (i // tall == lax.rem(j, 16) // CAP) & (lax.rem(i, tall) // 16 == j // 16)
        collect = (collect & (lax.rem(i, CAP) == lax.rem(j, CAP))).astype(F32)
        before_silu = jnp.dot(collect, picked, preferred_element_type=F32, precision=lax.Precision.HIGHEST)
        inner = silu(before_silu).astype(BF16)
        units = b.partial.shape[2]
        product = jnp.dot(inner, pmid_ref[0], preferred_element_type=F32).astype(BF16)
        for t in range(n_tensor):
            b.partial[t] = product[:, t * units : (t + 1) * units]
        for k in range(1, n_tensor):
            to_units(b, k).start()

    def share(b, k):
        mine = b.hidden.at[tensor]
        return copy(mine, mine, b.g_send.at[k], b.g_recv.at[k], to_tensor(k))

    def hidden_start(b):
        summed = b.partial[tensor].astype(F32)
        for k in range(1, n_tensor):
            to_units(b, k).wait_recv()
            summed = summed + b.partial_in[k].astype(F32)
        b.hidden[tensor] = silu(summed).astype(BF16)
        for k in range(1, n_tensor):
            share(b, k).start()

    def reply(b, k):
        return copy(b.answers, b.returned.at[row], b.b_send.at[k], b.b_recv.at[k], to_row(k))

    def heads_start(b):
        for k in range(1, n_tensor):
            origin = b.hidden.at[lax.rem(tensor + n_tensor - k, n_tensor)]
            copy(origin, origin, b.g_send.at[k], b.g_recv.at[k], to_tensor(k)).wait_recv()
        whole = jnp.concatenate([b.hidden[t] for t in range(n_tensor)], axis=1)
        logits = lax.dot_general(whole, head_ref[...], nt, preferred_element_type=F32)
        value = jnp.sum(whole.astype(F32) * critic_ref[...].astype(F32), axis=1, keepdims=True)
        peak = jnp.max(logits, axis=1, keepdims=True)
        logp = logits - (peak + jnp.log(jnp.sum(jnp.exp(logits - peak), axis=1, keepdims=True)))
        blank = jnp.zeros((logits.shape[0], 128 - logits.shape[1] - 1), F32)
        b.answers[...] = jnp.concatenate([logp, value, blank], axis=1)
        for k in range(1, peers):
            reply(b, k).start()
        b.returned[row] = b.answers[...]

    def replies_wait(b):
        for k in range(1, peers):
            origin = b.returned.at[lax.rem(row + peers - k, peers)]
            copy(origin, origin, b.b_send.at[k], b.b_recv.at[k], to_row(k)).wait_recv()

    def batch_sent(b):
        for k in range(1, peers):
            route(b, k).wait_send()
            reply(b, k).wait_send()
        for k in range(1, n_tensor):
            to_units(b, k).wait_send()
            share(b, k).wait_send()

    def gather(s):
        own, other, front = FAR[False], FAR[True], FAR[False]
        sent = []

        def block(stream, k):
            return (gath_q if stream == 2 else gath_p).at[s, slot_of(-k, stream == 1)]

        def go(ref, send, recv, target):
            moved = copy(ref, ref, send, recv, target)
            moved.start()
            sent.append(moved)

        def spread(stream, tree, k):
            for c in below(tree, k):
                go(block(stream, k), ag_zs.at[s, stream, c % n_z], ag_zr.at[s, stream, c % n_z], to_plane(c - k))

        def pass_on(k):
            go(block(2, k), ag_ys.at[s, k % n_z], ag_yr.at[s, k % n_z], pair)

        go(block(0, 0), ag_ys.at[s, n_z], ag_yr.at[s, n_z], pair)
        spread(2, front, 0)
        pass_on(0)
        spread(0, own, 0)
        events = [(due(front, k), 2, k) for k in front] + [(due(own, k), 0, k) for k in own]
        events += [(3.0 + due(other, k), 1, k) for k in [0] + list(other)]
        for _, stream, k in sorted(events):
            ref = block(stream, k)
            if k == 0:
                copy(ref, ref, ag_ys.at[s, n_z], ag_yr.at[s, n_z], pair).wait_recv()
            else:
                copy(ref, ref, ag_zs.at[s, stream, k % n_z], ag_zr.at[s, stream, k % n_z], pair).wait_recv()
            spread(stream, (own, other, front)[stream], k)
            if stream == 2:
                pass_on(k)
        for k in [0] + list(front):
            ref = gath_q.at[s, slot_of(-k, True)]
            copy(ref, ref, ag_ys.at[s, k % n_z], ag_yr.at[s, k % n_z], pair).wait_recv()
        return sent

    def scatter(s, hooks):
        trees = (FAR[False], FAR[True], FAR[False])
        sent = []

        def go(src, dst, send, recv, target):
            moved = copy(src, dst, send, recv, target)
            moved.start()
            sent.append(moved)

        for k in sorted(trees[2], key=lambda k: -due(trees[2], k)) + [0]:
            go(
                terms_q.at[slot_of(-k, True)],
                pair_q.at[s, k % n_z],
                rs_ys.at[s, k % n_z],
                rs_yr.at[s, k % n_z],
                pair,
            )
        deepest = max(due(trees[0], k) for k in trees[0])
        events = []
        for stream, offset in ((0, 1.0), (1, -0.1), (2, 3.0)):
            events += [(offset + deepest - due(trees[stream], k), stream, k) for k in [0] + list(trees[stream])]
        ends = {}
        for number, (_, stream, k) in enumerate(sorted(events)):
            if number in (0, len(events) // 2):
                hooks.pop(0)()
            tree = trees[stream]
            terms = terms_q if stream == 2 else terms_p
            slot = slot_of(-k, stream == 1)

            def landing(c):
                return tree_q.at[s, c % n_z] if stream == 2 else tree_p.at[s, stream, c % n_z]

            total = None
            children = below(tree, k)
            if stream == 2 or children or k == 0:
                total = terms[slot].astype(F32)
            if stream == 2:
                ref = pair_q.at[s, k % n_z]
                copy(ref, ref, rs_ys.at[s, k % n_z], rs_yr.at[s, k % n_z], pair).wait_recv()
                total = total + pair_q[s, k % n_z].astype(F32)
            for c in children:
                ref = landing(c)
                copy(ref, ref, rs_zs.at[s, stream, c % n_z], rs_zr.at[s, stream, c % n_z], pair).wait_recv()
                total = total + ref[...].astype(F32)
            if k:
                if total is not None:
                    terms[slot] = total.astype(BF16)
                go(
                    terms.at[slot],
                    landing(k),
                    rs_zs.at[s, stream, k % n_z],
                    rs_zr.at[s, stream, k % n_z],
                    to_plane(tree[k] - k),
                )
            elif stream == 1:
                terms[slot] = total.astype(BF16)
                go(terms.at[slot], pair_p.at[s], rs_ys.at[s, n_z], rs_yr.at[s, n_z], pair)
            else:
                ends[stream] = total
        ref = pair_p.at[s]
        copy(ref, ref, rs_ys.at[s, n_z], rs_yr.at[s, n_z], pair).wait_recv()
        first = ends[0] + pair_p[s].astype(F32)
        both = jnp.concatenate([first, ends[2]], axis=1)
        return jnp.concatenate([both[:rollouts], both[rollouts:]], axis=1), sent

    def embed_actions(s):
        at_step = lax.broadcasted_iota(jnp.int32, actions_ref.shape, 0) == s
        picked = jnp.sum(jnp.where(at_step, actions_ref[...], 0), axis=0, keepdims=True)
        code = lax.broadcasted_iota(jnp.int32, (table_ref.shape[0], rollouts), 0) == picked
        embed[...] = lax.dot_general(
            code.astype(F32).astype(BF16), table_ref[...], tn, preferred_element_type=F32
        )

    def step(s, carry):
        inputs = (state[...] + embed[...]).astype(BF16).astype(F32)
        state[...] = inputs
        normed = folded(rms_rows(inputs) * gain_ref[...]).astype(BF16)
        gath_p[s, tensor] = normed[:, :cut]
        gath_q[s, tensor] = normed[:, cut:]
        gathered = gather(s)

        @pl.when(s == 0)
        def _():
            for load in loads:
                load.wait()

        first = gath_p[s].reshape(n_tensor * 16, cut)
        second = gath_q[s].reshape(n_tensor * 16, half - cut)
        query = (fold_dot(first, second, wq_ref) * HD ** (-0.5)).astype(BF16)
        keyval = fold_dot(first, second, wkv_ref).astype(BF16)
        n_query = query.shape[1]
        qkv[s, :, :n_query] = jnp.dot(by_rollout, query, preferred_element_type=F32).astype(BF16)
        qkv[s, :, n_query:] = jnp.dot(by_rollout, keyval, preferred_element_type=F32).astype(BF16)
        swap = copy(qkv.at[s], qkv_in.at[s], q_send.at[s], q_recv.at[s], pair)
        swap.start()

        heads = n_query // HD
        per = heads * tokens

        def grouped(source, r):
            rows = slice(r * tokens, (r + 1) * tokens)
            return jnp.concatenate([source[s, rows, h * HD : (h + 1) * HD] for h in range(heads)], axis=0)

        def band(r):
            return slice(r * per, (r + 1) * per)

        def score_cached(group, source, r):
            scores[group, band(r), :cached] = lax.dot_general(
                grouped(source, r), cache_ref[r, 0, :, :HD], nt, preferred_element_type=F32
            )

        def score_new(group, source, r):
            scores[group, band(r), cached:] = lax.dot_general(
                grouped(source, r), keys[r], nt, preferred_element_type=F32
            )

        for r in range(rollouts):
            score_cached(0, qkv, r)

        @pl.when(s > 0)
        def _():
            spread_start(s - 1)

        for moved in gathered:
            moved.wait_send()
        swap.wait()

        own_kv = qkv[s, :, n_query:].astype(F32)
        other_kv = qkv_in[s, :, n_query:].astype(F32)
        new_key = jnp.where(yh == 0, own_kv, other_kv).astype(BF16)
        new_val = jnp.where(yh == 0, other_kv, own_kv).astype(BF16)
        place = pl.ds(pl.multiple_of(s * tokens, tokens), tokens)
        for r in range(rollouts):
            rows = slice(r * tokens, (r + 1) * tokens)
            keys[r, place, :] = new_key[rows]
            vals[r, place, :] = new_val[rows]
            score_cached(1, qkv_in, r)
            score_new(1, qkv_in, r)
            score_new(0, qkv, r)

        def soften(group):
            fresh = scores[group, :, cached:]
            key_pos = lax.broadcasted_iota(jnp.int32, fresh.shape, 1)
            query_pos = lax.rem(lax.broadcasted_iota(jnp.int32, fresh.shape, 0), tokens)
            allowed = (key_pos <= s * tokens + query_pos) & (yh == 0)
            fresh = jnp.where(allowed, fresh, -jnp.inf)
            old = scores[group, :, :cached]
            top = jnp.maximum(jnp.max(old, axis=1, keepdims=True), jnp.max(fresh, axis=1, keepdims=True))
            old = jnp.exp(old - top)
            fresh = jnp.exp(fresh - top)
            total = jnp.sum(old, axis=1, keepdims=True) + jnp.sum(fresh, axis=1, keepdims=True)
            weights[group, :, :cached] = old.astype(BF16)
            weights[group, :, cached:] = fresh.astype(BF16)
            return top, total, 1.0 / total

        def attend(group, r, inverse):
            summed = jnp.dot(weights[group, band(r), :cached], cache_ref[r, 0, :, HD:], preferred_element_type=F32)
            summed = summed + jnp.dot(weights[group, band(r), cached:], vals[r], preferred_element_type=F32)
            return summed * inverse[band(r)]

        far_top, far_total, inverse = soften(1)
        lane = lax.broadcasted_iota(jnp.int32, (tokens, HD), 1)
        for r in range(rollouts):
            rows = slice(r * tokens, (r + 1) * tokens)
            summed = attend(1, r, inverse)
            stats = jnp.zeros((tokens, HD), F32)
            for h in range(heads):
                at = slice(h * tokens, (h + 1) * tokens)
                out_o[s, rows, h * HD : (h + 1) * HD] = summed[at].astype(BF16)
                for first, column in ((8 * h, far_top), (8 * h + 3, far_total)):
                    left = column[band(r)][at]
                    for piece in range(3):
                        term = left.astype(BF16).astype(F32)
                        left = left - term
                        stats = jnp.where(lane == first + piece, term, stats)
            out_o[s, rows, n_query:] = stats.astype(BF16)
        swap = copy(out_o.at[s], in_o.at[s], o_send.at[s], o_recv.at[s], pair)
        swap.start()

        top, total, inverse = soften(0)
        for r in range(rollouts):
            rows = slice(r * tokens, (r + 1) * tokens)
            summed = attend(0, r, inverse)
            for h in range(heads):
                own_o[rows, h * HD : (h + 1) * HD] = summed[h * tokens : (h + 1) * tokens]

        embed_actions(s + 1)
        swap.wait()

        stats = in_o[s, :, n_query:].astype(F32)
        top4 = top.reshape(rollouts, heads, tokens, 1)
        total4 = total.reshape(rollouts, heads, tokens, 1)
        joined = []
        for h in range(heads):
            pick = [stats[:, 8 * h + i : 8 * h + i + 1] for i in range(6)]
            far_top = pick[0] + pick[1] + pick[2]
            far_total = pick[3] + pick[4] + pick[5]
            near_top = top4[:, h].reshape(n_rows, 1)
            near_total = total4[:, h].reshape(n_rows, 1)
            peak = jnp.maximum(near_top, far_top)
            near = near_total * jnp.exp(near_top - peak)
            far = far_total * jnp.exp(far_top - peak)
            both = 1.0 / (near + far)
            cols = slice(h * HD, (h + 1) * HD)
            joined.append(own_o[:, cols] * (near * both) + in_o[s, :, cols].astype(F32) * (far * both))
        attended = jnp.concatenate(joined, axis=1).astype(BF16)
        attended = jnp.dot(by_token, attended, preferred_element_type=F32).astype(BF16)

        tile = 512 if half % 512 == 0 else HD
        for j in range(half // tile):
            at = slice(j * tile, (j + 1) * tile)
            also = slice(half + j * tile, half + (j + 1) * tile)
            left = jnp.dot(attended, wo_ref[:, at], preferred_element_type=F32).reshape(tokens, rollouts, tile)
            right = jnp.dot(attended, wo_ref[:, also], preferred_element_type=F32).reshape(tokens, rollouts, tile)
            part = jnp.concatenate([left, right], axis=1).astype(BF16)
            if j * tile < cut:
                terms_p[:, :, at] = part
            else:
                terms_q[:, :, j * tile - cut : (j + 1) * tile - cut] = part

        def spread_hook():
            @pl.when(s > 0)
            def _():
                spread_on(s - 1)

        def route_hook():
            @pl.when(s > 0)
            def _():
                spread_end(s - 1)

            @pl.when(s == STEPS - 1)
            def _():
                route_start(batches[0])

        reduced, sent = scatter(s, [spread_hook, route_hook])
        updated = (state[...] + reduced).astype(BF16).astype(F32)
        state[...] = updated

        @pl.when(tensor == last)
        def _():
            latent_rows[s] = folded(rms_rows(updated)).astype(BF16)

        for moved in sent:
            moved.wait_send()
        return carry

    embed_actions(0)
    lax.fori_loop(0, STEPS, step, 0)
    final = STEPS - 1
    spread_start(final)
    inner_start(batches[0])
    spread_on(final)
    hidden_start(batches[0])
    spread_end(final)
    route_start(batches[1])
    heads_start(batches[0])
    latents_ref[...] = state[...].astype(BF16)
    inner_start(batches[1])
    for q in range(STEPS):
        spread_sent(q)
    hidden_start(batches[1])
    replies_wait(batches[0])
    heads_start(batches[1])
    for b in batches:
        batch_sent(b)
    replies_wait(batches[1])
    i = lax.broadcasted_iota(jnp.int32, (rollouts, spots), 1)
    mine = (i // 16 == owner) & (lax.rem(i, CAP).astype(F32) == place_of) & (lax.rem(i // CAP, eighths) == row)
    mine = mine.astype(F32)
    lane = lax.broadcasted_iota(jnp.int32, (rollouts, STEPS), 1)
    all_values = jnp.zeros((rollouts, STEPS), F32)
    n_actions = head_ref.shape[0]
    for q, b, n in [(q, b, n) for b in batches for n, q in enumerate(b.steps)]:
        now = jnp.dot(
            mine,
            b.returned[:, n * 16 : (n + 1) * 16, :].reshape(spots, 128),
            preferred_element_type=F32,
            precision=lax.Precision.HIGHEST,
        )
        logp_ref[:, q, :] = now[:, :n_actions]
        all_values = jnp.where(lane == q, now[:, n_actions : n_actions + 1], all_values)
    value_ref[...] = all_values


def shards(
    frame,
    cache,
    actions,
    owners,
    attn_gain,
    w_query,
    w_keyval,
    w_out,
    action_table,
    policy_in,
    policy_mid,
    policy_head,
    policy_value,
):
    n_tensor = lax.axis_size("tp")
    peers = lax.axis_size("row")
    n_z = n_tensor // 2
    rollouts, _, width = frame.shape
    half = width // 2
    n_rows = n_tensor * rollouts
    n_query = w_query.shape[1]
    wide = n_query + w_keyval.shape[1]
    cached = cache.shape[2]
    bands = n_rows * (n_query // HD)
    units = policy_mid.shape[2] // n_tensor
    cut = PAIR_COLUMNS
    vmem = pl.BlockSpec(memory_space=pltpu.VMEM)
    dma = pltpu.SemaphoreType.DMA

    def batch_scratch(count):
        tall = count * 16
        return (
            [pltpu.VMEM((peers, tall, half // 4), BF16)] * 2
            + [pltpu.VMEM((n_tensor, tall, units), BF16)] * 3
            + [pltpu.VMEM((tall, 128), F32), pltpu.VMEM((peers, tall, 128), F32)]
            + [dma((peers,))] * 2
            + [dma((n_tensor,))] * 4
            + [dma((peers,))] * 2
        )

    latents, log_probs, values = pl.pallas_call(
        functools.partial(kernel, n_z, peers),
        out_shape=(
            jax.ShapeDtypeStruct((rollouts, width), BF16),
            jax.ShapeDtypeStruct((rollouts, STEPS, policy_head.shape[2]), F32),
            jax.ShapeDtypeStruct((rollouts, STEPS), F32),
        ),
        in_specs=[vmem] * 5 + [pl.BlockSpec(memory_space=pl.ANY)] * 6 + [vmem] * 2,
        out_specs=(vmem,) * 3,
        scratch_shapes=[
            pltpu.VMEM(big.shape, BF16)
            for big in (cache, w_query, w_keyval, w_out, policy_in, policy_mid)
        ]
        + [
            pltpu.VMEM((rollouts, width), F32),
            pltpu.VMEM((rollouts, width), F32),
            pltpu.VMEM((STEPS, n_tensor, 16, cut), BF16),
            pltpu.VMEM((STEPS, n_tensor, 16, half - cut), BF16),
            pltpu.VMEM((STEPS, n_rows, wide), BF16),
            pltpu.VMEM((STEPS, n_rows, wide), BF16),
            pltpu.VMEM((rollouts, 128, HD), BF16),
            pltpu.VMEM((rollouts, 128, HD), BF16),
            pltpu.VMEM((2, bands, cached + 128), F32),
            pltpu.VMEM((2, bands, cached + 128), BF16),
            pltpu.VMEM((n_rows, n_query), F32),
            pltpu.VMEM((STEPS, n_rows, wide), BF16),
            pltpu.VMEM((STEPS, n_rows, wide), BF16),
            pltpu.VMEM((n_tensor, 16, cut), BF16),
            pltpu.VMEM((n_tensor, 16, half - cut), BF16),
            pltpu.VMEM((STEPS, 2, n_z, 16, cut), BF16),
            pltpu.VMEM((STEPS, n_z, 16, half - cut), BF16),
            pltpu.VMEM((STEPS, 16, cut), BF16),
            pltpu.VMEM((STEPS, n_z, 16, half - cut), BF16),
            pltpu.VMEM((STEPS, 16, half), BF16),
        ]
        + [dma((STEPS, 3, n_z))] * 2
        + [dma((STEPS, n_z + 1))] * 2
        + [dma((STEPS, 3, n_z))] * 2
        + [dma((STEPS, n_z + 1))] * 2
        + [dma((STEPS,))] * 4
        + [dma((STEPS, n_z)), dma((STEPS, 2))]
        + [dma((6,))]
        + [ref for steps in BATCHES for ref in batch_scratch(len(steps))],
        compiler_params=pltpu.CompilerParams(
            collective_id=0, has_side_effects=True, vmem_limit_bytes=VMEM_LIMIT
        ),
        name="imagine",
    )(
        frame.reshape(rollouts, width),
        actions.T,
        owners.T,
        attn_gain.reshape(1, width),
        action_table,
        cache,
        w_query,
        w_keyval,
        w_out,
        policy_in,
        policy_mid,
        policy_head.reshape(policy_head.shape[1:]).T,
        policy_value,
    )
    return (latents.reshape(frame.shape), log_probs, values)


def solution(mesh):
    placed = (
        P(("grp", "row"), "tp", None),
        P(("grp", "row"), "tp", None, None),
        P(("grp", "row"), None),
        P(("grp", "row"), None),
        P(),
        P(None, "tp"),
        P(None, "tp"),
        P("tp", None),
        P(),
        P("row", None, "tp"),
        P("row", "tp", None),
        P("row", None, None),
        P("row", None),
    )
    return jax.shard_map(
        shards,
        mesh=mesh,
        in_specs=placed,
        out_specs=(
            P(("grp", "row"), "tp", None),
            P(("grp", "row"), None, None),
            P(("grp", "row"), None),
        ),
        check_vma=False,
    )
```

```python
import functools
import typing

import jax
import jax.numpy as jnp
from jax import lax
from jax.experimental import pallas as pl
from jax.experimental.pallas import tpu as pltpu
from jax.sharding import PartitionSpec as P

HD = 128
STEPS = 4
CAP = 2
EPS = 1e-05
MESH = pl.DeviceIdType.MESH
F32 = jnp.float32
BF16 = jnp.bfloat16
VMEM_LIMIT = 56 << 20


def rms_rows(values):
    return values * lax.rsqrt(jnp.mean(values * values, axis=-1, keepdims=True) + EPS)


def folded(rows):
    half = rows.shape[1] // 2
    return jnp.concatenate([rows[:, :half], rows[:, half:]], axis=0)


PAIR_COLUMNS = 512
PARTS = 2
FAR = {False: {1: 0, -1: 0, 2: 0, -2: 0, 3: 2, -3: -2, 4: 2}, True: {1: 0, -1: 0, 2: 0, -2: 0, 3: 2, -3: -2, -4: -2}}


BATCHES = ((0, 1, 2), (3,))


class Batch(typing.NamedTuple):
    steps: tuple
    outgoing: typing.Any
    arrived: typing.Any
    partial: typing.Any
    partial_in: typing.Any
    hidden: typing.Any
    answers: typing.Any
    returned: typing.Any
    a_send: typing.Any
    a_recv: typing.Any
    h_send: typing.Any
    h_recv: typing.Any
    g_send: typing.Any
    g_recv: typing.Any
    b_send: typing.Any
    b_recv: typing.Any


def due(tree, k):
    return 0.0 if k == 0 else due(tree, tree[k]) + 2.0 + 0.8 * abs(k - tree[k])


def below(tree, k):
    return sorted([c for c in tree if tree[c] == k], key=lambda c: abs(c - k))


def halves(product, half, width):
    return product.reshape(-1, 2, 8, width)[:, half].reshape(-1, width)


def fold_dot(first, second, weight):
    half = weight.shape[0] // 2
    columns = weight.shape[1]
    cut = first.shape[1]
    left = jnp.dot(first, weight[:cut], preferred_element_type=F32)
    left = left + jnp.dot(second, weight[cut:half], preferred_element_type=F32)
    right = jnp.dot(first, weight[half : half + cut], preferred_element_type=F32)
    right = right + jnp.dot(second, weight[half + cut :], preferred_element_type=F32)
    return halves(left, 0, columns) + halves(right, 1, columns)


def silu(values):
    return values / (1.0 + jnp.exp(-values))


def kernel(
    n_z,
    peers,
    frame_ref,
    actions_ref,
    owners_ref,
    gain_ref,
    table_ref,
    cache_hbm,
    wq_hbm,
    wkv_hbm,
    wo_hbm,
    pin_hbm,
    pmid_hbm,
    head_ref,
    critic_ref,
    latents_ref,
    logp_ref,
    value_ref,
    cache_ref,
    wq_ref,
    wkv_ref,
    wo_ref,
    pin_ref,
    pmid_ref,
    embed,
    state,
    gath_p,
    gath_q,
    qkv,
    qkv_in,
    keys,
    vals,
    scores,
    weights,
    own_o,
    out_o,
    in_o,
    terms_p,
    terms_q,
    tree_p,
    tree_q,
    pair_p,
    pair_q,
    latent_rows,
    ag_zs,
    ag_zr,
    ag_ys,
    ag_yr,
    rs_zs,
    rs_zr,
    rs_ys,
    rs_yr,
    q_send,
    q_recv,
    o_send,
    o_recv,
    l_send,
    l_recv,
    loaded,
    *batch_refs,
):
    batches = [Batch(steps, *batch_refs[i * 15 : (i + 1) * 15]) for i, steps in enumerate(BATCHES)]
    loads = [
        pltpu.make_async_copy(src, dst, loaded.at[i])
        for i, (src, dst) in enumerate(
            (
                (wq_hbm, wq_ref),
                (wkv_hbm, wkv_ref),
                (cache_hbm, cache_ref),
                (wo_hbm, wo_ref),
                (pin_hbm, pin_ref),
                (pmid_hbm, pmid_ref),
            )
        )
    ]
    for load in loads:
        load.start()
    tensor = lax.axis_index("tp")
    row = lax.axis_index("row")
    z = tensor // 2
    yh = lax.rem(tensor, 2)
    pair = {"tp": tensor + 1 - 2 * yh}
    rollouts, width = state.shape
    n_tensor = 2 * n_z
    tokens = n_tensor
    n_rows = tokens * rollouts
    cached = cache_ref.shape[2]
    last = n_tensor - 1
    cut = gath_p.shape[3]
    half = width // 2

    def plane(k):
        return lax.rem(z + k + 2 * n_z, n_z)

    def to_plane(k):
        return {"tp": plane(k) * 2 + yh}

    def slot_of(k, other):
        return plane(k) * 2 + (1 - yh if other else yh)

    def to_row(k):
        return {"row": lax.rem(row + k, peers)}

    def to_tensor(k):
        return {"tp": lax.rem(tensor + k, n_tensor)}

    barrier = pltpu.get_barrier_semaphore()
    for k in range(1, n_tensor):
        pl.semaphore_signal(barrier, inc=1, device_id=to_tensor(k), device_id_type=MESH)
    for k in range(1, peers):
        pl.semaphore_signal(barrier, inc=1, device_id=to_row(k), device_id_type=MESH)

    def copy(src, dst, send, recv, target):
        return pltpu.make_async_remote_copy(
            src_ref=src, dst_ref=dst, send_sem=send, recv_sem=recv, device_id=target, device_id_type=MESH
        )

    state[...] = frame_ref[...].astype(F32)
    keys[...] = jnp.zeros_like(keys)
    vals[...] = jnp.zeros_like(vals)
    iota_r = lax.broadcasted_iota(jnp.int32, (n_rows, n_rows), 0)
    iota_c = lax.broadcasted_iota(jnp.int32, (n_rows, n_rows), 1)
    by_rollout = (lax.rem(iota_r, tokens) * rollouts + iota_r // tokens == iota_c).astype(F32).astype(BF16)
    by_token = (lax.rem(iota_c, tokens) * rollouts + iota_c // tokens == iota_r).astype(F32).astype(BF16)

    eye = lax.broadcasted_iota(jnp.int32, (rollouts, rollouts), 0) == lax.broadcasted_iota(
        jnp.int32, (rollouts, rollouts), 1
    )
    owner = jnp.sum(jnp.where(eye, owners_ref[...], 0), axis=1, keepdims=True)
    hit = (lax.broadcasted_iota(jnp.int32, (rollouts, 128), 1) == owner).astype(F32)
    later = (
        lax.broadcasted_iota(jnp.int32, (rollouts, rollouts), 0)
        > lax.broadcasted_iota(jnp.int32, (rollouts, rollouts), 1)
    ).astype(F32)
    before = jnp.zeros((rollouts, 128), F32)
    for r in range(rollouts):
        before = before + later[:, r : r + 1] * hit[r : r + 1, :]
    place_of = jnp.sum(before * hit, axis=1, keepdims=True)
    eighths = 16 // CAP
    spots = peers * 16
    tn = (((0,), (0,)), ((), ()))
    nt = (((1,), (1,)), ((), ()))
    pl.semaphore_wait(barrier, peers + n_tensor - 2)

    def spread_across(q, k):
        mine = latent_rows.at[q]
        return copy(mine, mine, l_send.at[q, k], l_recv.at[q, 0], to_plane(k))

    def spread_pair(q):
        mine = latent_rows.at[q]
        return copy(mine, mine, l_send.at[q, 0], l_recv.at[q, 1], pair)

    far_first = sorted(range(1, n_z), key=lambda k: -min(k, n_z - k))

    def spread_start(q):
        @pl.when(tensor == last)
        def _():
            for k in far_first:
                spread_across(q, k).start()
            spread_pair(q).start()

    def spread_on(q):
        @pl.when((yh == 1) & (tensor != last))
        def _():
            spread_across(q, 1).wait_recv()
            spread_pair(q).start()

    def spread_end(q):
        @pl.when(yh == 0)
        def _():
            spread_pair(q).wait_recv()

    def spread_sent(q):
        @pl.when(yh == 1)
        def _():
            spread_pair(q).wait_send()

        @pl.when(tensor == last)
        def _():
            for k in far_first:
                spread_across(q, k).wait_send()

    def route(b, k):
        return copy(b.outgoing.at[lax.rem(row + k, peers)], b.arrived.at[row], b.a_send.at[k], b.a_recv.at[k], to_row(k))

    def route_start(b):
        wide = half // 4
        i = lax.broadcasted_iota(jnp.int32, (16, spots), 1)
        j = lax.broadcasted_iota(jnp.int32, (16, spots), 0)
        owner2 = jnp.concatenate([owner, owner], axis=0)
        place2 = jnp.concatenate([place_of, place_of], axis=0)
        chosen = (i // 16 == owner2) & (lax.rem(i, CAP).astype(F32) == place2)
        eighth = lax.rem(i // CAP, eighths)
        hots = [
            (chosen & (eighth == (j // rollouts) * 4 + quarter)).astype(F32).astype(BF16) for quarter in range(4)
        ]
        for n, q in enumerate(b.steps):
            built = jnp.zeros((spots, wide), F32)
            for quarter in range(4):
                built = built + lax.dot_general(
                    hots[quarter],
                    latent_rows[q, :, quarter * wide : (quarter + 1) * wide],
                    tn,
                    preferred_element_type=F32,
                )
            b.outgoing[:, n * 16 : (n + 1) * 16, :] = built.astype(BF16).reshape(peers, 16, wide)
        for k in range(1, peers):
            route(b, k).start()
        b.arrived[row] = b.outgoing[row]

    def to_units(b, k):
        return copy(
            b.partial.at[lax.rem(tensor + k, n_tensor)], b.partial_in.at[k], b.h_send.at[k], b.h_recv.at[k], to_tensor(k)
        )

    def inner_start(b):
        for k in range(1, peers):
            origin = b.arrived.at[lax.rem(row + peers - k, peers)]
            copy(origin, origin, b.a_send.at[k], b.a_recv.at[k], to_row(k)).wait_recv()
        wide = half // 4
        tall = len(b.steps) * 16
        rows = b.arrived[...].reshape(peers * tall, wide)
        n_inner = pin_ref.shape[2]
        at_row = lax.rem(lax.broadcasted_iota(jnp.int32, (peers * tall, n_inner), 0) // CAP, eighths)
        picked = jnp.zeros((peers * tall, n_inner), F32)
        for e in range(eighths):
            product = jnp.dot(rows, pin_ref[0, e * wide : (e + 1) * wide, :], preferred_element_type=F32)
            picked = picked + jnp.where(at_row == e, product, 0.0)
        i = lax.broadcasted_iota(jnp.int32, (tall, peers * tall), 1)
        j = lax.broadcasted_iota(jnp.int32, (tall, peers * tall), 0)
        collect = (i // tall == lax.rem(j, 16) // CAP) & (lax.rem(i, tall) // 16 == j // 16)
        collect = (collect & (lax.rem(i, CAP) == lax.rem(j, CAP))).astype(F32)
        before_silu = jnp.dot(collect, picked, preferred_element_type=F32, precision=lax.Precision.HIGHEST)
        inner = silu(before_silu).astype(BF16)
        units = b.partial.shape[2]
        product = jnp.dot(inner, pmid_ref[0], preferred_element_type=F32).astype(BF16)
        for t in range(n_tensor):
            b.partial[t] = product[:, t * units : (t + 1) * units]
        for k in range(1, n_tensor):
            to_units(b, k).start()

    def share(b, k):
        mine = b.hidden.at[tensor]
        return copy(mine, mine, b.g_send.at[k], b.g_recv.at[k], to_tensor(k))

    def hidden_start(b):
        summed = b.partial[tensor].astype(F32)
        for k in range(1, n_tensor):
            to_units(b, k).wait_recv()
            summed = summed + b.partial_in[k].astype(F32)
        b.hidden[tensor] = silu(summed).astype(BF16)
        for k in range(1, n_tensor):
            share(b, k).start()

    def reply(b, k):
        return copy(b.answers, b.returned.at[row], b.b_send.at[k], b.b_recv.at[k], to_row(k))

    def heads_start(b):
        for k in range(1, n_tensor):
            origin = b.hidden.at[lax.rem(tensor + n_tensor - k, n_tensor)]
            copy(origin, origin, b.g_send.at[k], b.g_recv.at[k], to_tensor(k)).wait_recv()
        whole = jnp.concatenate([b.hidden[t] for t in range(n_tensor)], axis=1)
        logits = lax.dot_general(whole, head_ref[...], nt, preferred_element_type=F32)
        value = jnp.sum(whole.astype(F32) * critic_ref[...].astype(F32), axis=1, keepdims=True)
        peak = jnp.max(logits, axis=1, keepdims=True)
        logp = logits - (peak + jnp.log(jnp.sum(jnp.exp(logits - peak), axis=1, keepdims=True)))
        blank = jnp.zeros((logits.shape[0], 128 - logits.shape[1] - 1), F32)
        b.answers[...] = jnp.concatenate([logp, value, blank], axis=1)
        for k in range(1, peers):
            reply(b, k).start()
        b.returned[row] = b.answers[...]

    def replies_wait(b):
        for k in range(1, peers):
            origin = b.returned.at[lax.rem(row + peers - k, peers)]
            copy(origin, origin, b.b_send.at[k], b.b_recv.at[k], to_row(k)).wait_recv()

    def batch_sent(b):
        for k in range(1, peers):
            route(b, k).wait_send()
            reply(b, k).wait_send()
        for k in range(1, n_tensor):
            to_units(b, k).wait_send()
            share(b, k).wait_send()

    def gather(s):
        own, other, front = FAR[False], FAR[True], FAR[False]
        sent = []

        def block(stream, k):
            return (gath_q if stream == 2 else gath_p).at[s, slot_of(-k, stream == 1)]

        def go(ref, send, recv, target):
            moved = copy(ref, ref, send, recv, target)
            moved.start()
            sent.append(moved)

        def spread(stream, tree, k):
            for c in below(tree, k):
                go(block(stream, k), ag_zs.at[s, stream, c % n_z], ag_zr.at[s, stream, c % n_z], to_plane(c - k))

        def pass_on(k):
            go(block(2, k), ag_ys.at[s, k % n_z], ag_yr.at[s, k % n_z], pair)

        go(block(0, 0), ag_ys.at[s, n_z], ag_yr.at[s, n_z], pair)
        spread(2, front, 0)
        pass_on(0)
        spread(0, own, 0)
        events = [(due(front, k), 2, k) for k in front] + [(due(own, k), 0, k) for k in own]
        events += [(3.0 + due(other, k), 1, k) for k in [0] + list(other)]
        for _, stream, k in sorted(events):
            ref = block(stream, k)
            if k == 0:
                copy(ref, ref, ag_ys.at[s, n_z], ag_yr.at[s, n_z], pair).wait_recv()
            else:
                copy(ref, ref, ag_zs.at[s, stream, k % n_z], ag_zr.at[s, stream, k % n_z], pair).wait_recv()
            spread(stream, (own, other, front)[stream], k)
            if stream == 2:
                pass_on(k)
        for k in [0] + list(front):
            ref = gath_q.at[s, slot_of(-k, True)]
            copy(ref, ref, ag_ys.at[s, k % n_z], ag_yr.at[s, k % n_z], pair).wait_recv()
        return sent

    def scatter(s, hooks):
        trees = (FAR[False], FAR[True], FAR[False])
        sent = []

        def go(src, dst, send, recv, target):
            moved = copy(src, dst, send, recv, target)
            moved.start()
            sent.append(moved)

        for k in sorted(trees[2], key=lambda k: -due(trees[2], k)) + [0]:
            go(
                terms_q.at[slot_of(-k, True)],
                pair_q.at[s, k % n_z],
                rs_ys.at[s, k % n_z],
                rs_yr.at[s, k % n_z],
                pair,
            )
        deepest = max(due(trees[0], k) for k in trees[0])
        events = []
        for stream, offset in ((0, 1.0), (1, -0.1), (2, 3.0)):
            events += [(offset + deepest - due(trees[stream], k), stream, k) for k in [0] + list(trees[stream])]
        ends = {}
        for number, (_, stream, k) in enumerate(sorted(events)):
            if number in (0, len(events) // 2):
                hooks.pop(0)()
            tree = trees[stream]
            terms = terms_q if stream == 2 else terms_p
            slot = slot_of(-k, stream == 1)

            def landing(c):
                return tree_q.at[s, c % n_z] if stream == 2 else tree_p.at[s, stream, c % n_z]

            total = None
            children = below(tree, k)
            if stream == 2 or children or k == 0:
                total = terms[slot].astype(F32)
            if stream == 2:
                ref = pair_q.at[s, k % n_z]
                copy(ref, ref, rs_ys.at[s, k % n_z], rs_yr.at[s, k % n_z], pair).wait_recv()
                total = total + pair_q[s, k % n_z].astype(F32)
            for c in children:
                ref = landing(c)
                copy(ref, ref, rs_zs.at[s, stream, c % n_z], rs_zr.at[s, stream, c % n_z], pair).wait_recv()
                total = total + ref[...].astype(F32)
            if k:
                if total is not None:
                    terms[slot] = total.astype(BF16)
                go(
                    terms.at[slot],
                    landing(k),
                    rs_zs.at[s, stream, k % n_z],
                    rs_zr.at[s, stream, k % n_z],
                    to_plane(tree[k] - k),
                )
            elif stream == 1:
                terms[slot] = total.astype(BF16)
                go(terms.at[slot], pair_p.at[s], rs_ys.at[s, n_z], rs_yr.at[s, n_z], pair)
            else:
                ends[stream] = total
        ref = pair_p.at[s]
        copy(ref, ref, rs_ys.at[s, n_z], rs_yr.at[s, n_z], pair).wait_recv()
        first = ends[0] + pair_p[s].astype(F32)
        both = jnp.concatenate([first, ends[2]], axis=1)
        return jnp.concatenate([both[:rollouts], both[rollouts:]], axis=1), sent

    def embed_actions(s):
        at_step = lax.broadcasted_iota(jnp.int32, actions_ref.shape, 0) == s
        picked = jnp.sum(jnp.where(at_step, actions_ref[...], 0), axis=0, keepdims=True)
        code = lax.broadcasted_iota(jnp.int32, (table_ref.shape[0], rollouts), 0) == picked
        embed[...] = lax.dot_general(
            code.astype(F32).astype(BF16), table_ref[...], tn, preferred_element_type=F32
        )

    def step(s, carry):
        inputs = (state[...] + embed[...]).astype(BF16).astype(F32)
        state[...] = inputs
        normed = folded(rms_rows(inputs) * gain_ref[...]).astype(BF16)
        gath_p[s, tensor] = normed[:, :cut]
        gath_q[s, tensor] = normed[:, cut:]
        gathered = gather(s)

        @pl.when(s == 0)
        def _():
            for load in loads:
                load.wait()

        first = gath_p[s].reshape(n_tensor * 16, cut)
        second = gath_q[s].reshape(n_tensor * 16, half - cut)
        query = (fold_dot(first, second, wq_ref) * HD ** (-0.5)).astype(BF16)
        keyval = fold_dot(first, second, wkv_ref).astype(BF16)
        n_query = query.shape[1]
        qkv[s, :, :n_query] = jnp.dot(by_rollout, query, preferred_element_type=F32).astype(BF16)
        qkv[s, :, n_query:] = jnp.dot(by_rollout, keyval, preferred_element_type=F32).astype(BF16)
        part_rows = n_rows // PARTS

        def parted(n):
            return pl.ds(n * part_rows, part_rows)

        swaps = [
            copy(qkv.at[s, parted(n)], qkv_in.at[s, parted(n)], q_send.at[s, n], q_recv.at[s, n], pair)
            for n in range(PARTS)
        ]
        for swap in swaps:
            swap.start()

        heads = n_query // HD
        per = heads * tokens

        def grouped(source, r):
            rows = slice(r * tokens, (r + 1) * tokens)
            return jnp.concatenate([source[s, rows, h * HD : (h + 1) * HD] for h in range(heads)], axis=0)

        def band(r):
            return slice(r * per, (r + 1) * per)

        def score_cached(group, source, r):
            scores[group, band(r), :cached] = lax.dot_general(
                grouped(source, r), cache_ref[r, 0, :, :HD], nt, preferred_element_type=F32
            )

        def score_new(group, source, r):
            scores[group, band(r), cached:] = lax.dot_general(
                grouped(source, r), keys[r], nt, preferred_element_type=F32
            )

        for r in range(rollouts):
            score_cached(0, qkv, r)

        @pl.when(s > 0)
        def _():
            spread_start(s - 1)

        for moved in gathered:
            moved.wait_send()
        place = pl.ds(pl.multiple_of(s * tokens, tokens), tokens)

        def soften(group, low, high):
            fresh = scores[group, low:high, cached:]
            key_pos = lax.broadcasted_iota(jnp.int32, fresh.shape, 1)
            query_pos = lax.rem(lax.broadcasted_iota(jnp.int32, fresh.shape, 0), tokens)
            allowed = (key_pos <= s * tokens + query_pos) & (yh == 0)
            fresh = jnp.where(allowed, fresh, -jnp.inf)
            old = scores[group, low:high, :cached]
            top = jnp.maximum(jnp.max(old, axis=1, keepdims=True), jnp.max(fresh, axis=1, keepdims=True))
            old = jnp.exp(old - top)
            fresh = jnp.exp(fresh - top)
            total = jnp.sum(old, axis=1, keepdims=True) + jnp.sum(fresh, axis=1, keepdims=True)
            weights[group, low:high, :cached] = old.astype(BF16)
            weights[group, low:high, cached:] = fresh.astype(BF16)
            return top, total, 1.0 / total

        def attend(group, r, inverse):
            summed = jnp.dot(weights[group, band(r), :cached], cache_ref[r, 0, :, HD:], preferred_element_type=F32)
            summed = summed + jnp.dot(weights[group, band(r), cached:], vals[r], preferred_element_type=F32)
            return summed * inverse

        lane = lax.broadcasted_iota(jnp.int32, (tokens, HD), 1)
        sums = [
            copy(out_o.at[s, parted(n)], in_o.at[s, parted(n)], o_send.at[s, n], o_recv.at[s, n], pair)
            for n in range(PARTS)
        ]
        per_part = rollouts // PARTS
        for n in range(PARTS):
            swaps[n].wait_recv()
            here = slice(n * part_rows, (n + 1) * part_rows)
            own_kv = qkv[s, here, n_query:].astype(F32)
            other_kv = qkv_in[s, here, n_query:].astype(F32)
            new_key = jnp.where(yh == 0, own_kv, other_kv).astype(BF16)
            new_val = jnp.where(yh == 0, other_kv, own_kv).astype(BF16)
            for i in range(per_part):
                r = n * per_part + i
                rows = slice(i * tokens, (i + 1) * tokens)
                keys[r, place, :] = new_key[rows]
                vals[r, place, :] = new_val[rows]
                score_cached(1, qkv_in, r)
                score_new(1, qkv_in, r)
            far_top, far_total, inverse = soften(1, n * per_part * per, (n + 1) * per_part * per)
            for i in range(per_part):
                r = n * per_part + i
                rows = slice(r * tokens, (r + 1) * tokens)
                summed = attend(1, r, inverse[band(i)])
                stats = jnp.zeros((tokens, HD), F32)
                for h in range(heads):
                    at = slice(h * tokens, (h + 1) * tokens)
                    out_o[s, rows, h * HD : (h + 1) * HD] = summed[at].astype(BF16)
                    for first, column in ((8 * h, far_top), (8 * h + 3, far_total)):
                        left = column[band(i)][at]
                        for piece in range(3):
                            term = left.astype(BF16).astype(F32)
                            left = left - term
                            stats = jnp.where(lane == first + piece, term, stats)
                out_o[s, rows, n_query:] = stats.astype(BF16)
            sums[n].start()

        for r in range(rollouts):
            score_new(0, qkv, r)
        top, total, inverse = soften(0, 0, rollouts * per)
        for r in range(rollouts):
            rows = slice(r * tokens, (r + 1) * tokens)
            summed = attend(0, r, inverse[band(r)])
            for h in range(heads):
                own_o[rows, h * HD : (h + 1) * HD] = summed[h * tokens : (h + 1) * tokens]

        embed_actions(s + 1)
        for swap in swaps:
            swap.wait_send()
        for swap in sums:
            swap.wait()

        stats = in_o[s, :, n_query:].astype(F32)
        top4 = top.reshape(rollouts, heads, tokens, 1)
        total4 = total.reshape(rollouts, heads, tokens, 1)
        joined = []
        for h in range(heads):
            pick = [stats[:, 8 * h + i : 8 * h + i + 1] for i in range(6)]
            far_top = pick[0] + pick[1] + pick[2]
            far_total = pick[3] + pick[4] + pick[5]
            near_top = top4[:, h].reshape(n_rows, 1)
            near_total = total4[:, h].reshape(n_rows, 1)
            peak = jnp.maximum(near_top, far_top)
            near = near_total * jnp.exp(near_top - peak)
            far = far_total * jnp.exp(far_top - peak)
            both = 1.0 / (near + far)
            cols = slice(h * HD, (h + 1) * HD)
            joined.append(own_o[:, cols] * (near * both) + in_o[s, :, cols].astype(F32) * (far * both))
        attended = jnp.concatenate(joined, axis=1).astype(BF16)
        attended = jnp.dot(by_token, attended, preferred_element_type=F32).astype(BF16)

        tile = 512 if half % 512 == 0 else HD
        for j in range(half // tile):
            at = slice(j * tile, (j + 1) * tile)
            also = slice(half + j * tile, half + (j + 1) * tile)
            left = jnp.dot(attended, wo_ref[:, at], preferred_element_type=F32).reshape(tokens, rollouts, tile)
            right = jnp.dot(attended, wo_ref[:, also], preferred_element_type=F32).reshape(tokens, rollouts, tile)
            part = jnp.concatenate([left, right], axis=1).astype(BF16)
            if j * tile < cut:
                terms_p[:, :, at] = part
            else:
                terms_q[:, :, j * tile - cut : (j + 1) * tile - cut] = part

        def spread_hook():
            @pl.when(s > 0)
            def _():
                spread_on(s - 1)

        def route_hook():
            @pl.when(s > 0)
            def _():
                spread_end(s - 1)

            @pl.when(s == STEPS - 1)
            def _():
                route_start(batches[0])

        reduced, sent = scatter(s, [spread_hook, route_hook])
        updated = (state[...] + reduced).astype(BF16).astype(F32)
        state[...] = updated

        @pl.when(tensor == last)
        def _():
            latent_rows[s] = folded(rms_rows(updated)).astype(BF16)

        for moved in sent:
            moved.wait_send()
        return carry

    embed_actions(0)
    lax.fori_loop(0, STEPS, step, 0)
    final = STEPS - 1
    spread_start(final)
    inner_start(batches[0])
    spread_on(final)
    hidden_start(batches[0])
    spread_end(final)
    route_start(batches[1])
    heads_start(batches[0])
    latents_ref[...] = state[...].astype(BF16)
    inner_start(batches[1])
    for q in range(STEPS):
        spread_sent(q)
    hidden_start(batches[1])
    replies_wait(batches[0])
    heads_start(batches[1])
    for b in batches:
        batch_sent(b)
    replies_wait(batches[1])
    i = lax.broadcasted_iota(jnp.int32, (rollouts, spots), 1)
    mine = (i // 16 == owner) & (lax.rem(i, CAP).astype(F32) == place_of) & (lax.rem(i // CAP, eighths) == row)
    mine = mine.astype(F32)
    lane = lax.broadcasted_iota(jnp.int32, (rollouts, STEPS), 1)
    all_values = jnp.zeros((rollouts, STEPS), F32)
    n_actions = head_ref.shape[0]
    for q, b, n in [(q, b, n) for b in batches for n, q in enumerate(b.steps)]:
        now = jnp.dot(
            mine,
            b.returned[:, n * 16 : (n + 1) * 16, :].reshape(spots, 128),
            preferred_element_type=F32,
            precision=lax.Precision.HIGHEST,
        )
        logp_ref[:, q, :] = now[:, :n_actions]
        all_values = jnp.where(lane == q, now[:, n_actions : n_actions + 1], all_values)
    value_ref[...] = all_values


def shards(
    frame,
    cache,
    actions,
    owners,
    attn_gain,
    w_query,
    w_keyval,
    w_out,
    action_table,
    policy_in,
    policy_mid,
    policy_head,
    policy_value,
):
    n_tensor = lax.axis_size("tp")
    peers = lax.axis_size("row")
    n_z = n_tensor // 2
    rollouts, _, width = frame.shape
    half = width // 2
    n_rows = n_tensor * rollouts
    n_query = w_query.shape[1]
    wide = n_query + w_keyval.shape[1]
    cached = cache.shape[2]
    bands = n_rows * (n_query // HD)
    units = policy_mid.shape[2] // n_tensor
    cut = PAIR_COLUMNS
    vmem = pl.BlockSpec(memory_space=pltpu.VMEM)
    dma = pltpu.SemaphoreType.DMA

    def batch_scratch(count):
        tall = count * 16
        return (
            [pltpu.VMEM((peers, tall, half // 4), BF16)] * 2
            + [pltpu.VMEM((n_tensor, tall, units), BF16)] * 3
            + [pltpu.VMEM((tall, 128), F32), pltpu.VMEM((peers, tall, 128), F32)]
            + [dma((peers,))] * 2
            + [dma((n_tensor,))] * 4
            + [dma((peers,))] * 2
        )

    latents, log_probs, values = pl.pallas_call(
        functools.partial(kernel, n_z, peers),
        out_shape=(
            jax.ShapeDtypeStruct((rollouts, width), BF16),
            jax.ShapeDtypeStruct((rollouts, STEPS, policy_head.shape[2]), F32),
            jax.ShapeDtypeStruct((rollouts, STEPS), F32),
        ),
        in_specs=[vmem] * 5 + [pl.BlockSpec(memory_space=pl.ANY)] * 6 + [vmem] * 2,
        out_specs=(vmem,) * 3,
        scratch_shapes=[
            pltpu.VMEM(big.shape, BF16)
            for big in (cache, w_query, w_keyval, w_out, policy_in, policy_mid)
        ]
        + [
            pltpu.VMEM((rollouts, width), F32),
            pltpu.VMEM((rollouts, width), F32),
            pltpu.VMEM((STEPS, n_tensor, 16, cut), BF16),
            pltpu.VMEM((STEPS, n_tensor, 16, half - cut), BF16),
            pltpu.VMEM((STEPS, n_rows, wide), BF16),
            pltpu.VMEM((STEPS, n_rows, wide), BF16),
            pltpu.VMEM((rollouts, 128, HD), BF16),
            pltpu.VMEM((rollouts, 128, HD), BF16),
            pltpu.VMEM((2, bands, cached + 128), F32),
            pltpu.VMEM((2, bands, cached + 128), BF16),
            pltpu.VMEM((n_rows, n_query), F32),
            pltpu.VMEM((STEPS, n_rows, wide), BF16),
            pltpu.VMEM((STEPS, n_rows, wide), BF16),
            pltpu.VMEM((n_tensor, 16, cut), BF16),
            pltpu.VMEM((n_tensor, 16, half - cut), BF16),
            pltpu.VMEM((STEPS, 2, n_z, 16, cut), BF16),
            pltpu.VMEM((STEPS, n_z, 16, half - cut), BF16),
            pltpu.VMEM((STEPS, 16, cut), BF16),
            pltpu.VMEM((STEPS, n_z, 16, half - cut), BF16),
            pltpu.VMEM((STEPS, 16, half), BF16),
        ]
        + [dma((STEPS, 3, n_z))] * 2
        + [dma((STEPS, n_z + 1))] * 2
        + [dma((STEPS, 3, n_z))] * 2
        + [dma((STEPS, n_z + 1))] * 2
        + [dma((STEPS, PARTS))] * 4
        + [dma((STEPS, n_z)), dma((STEPS, 2))]
        + [dma((6,))]
        + [ref for steps in BATCHES for ref in batch_scratch(len(steps))],
        compiler_params=pltpu.CompilerParams(
            collective_id=0, has_side_effects=True, vmem_limit_bytes=VMEM_LIMIT
        ),
        name="imagine",
    )(
        frame.reshape(rollouts, width),
        actions.T,
        owners.T,
        attn_gain.reshape(1, width),
        action_table,
        cache,
        w_query,
        w_keyval,
        w_out,
        policy_in,
        policy_mid,
        policy_head.reshape(policy_head.shape[1:]).T,
        policy_value,
    )
    return (latents.reshape(frame.shape), log_probs, values)


def solution(mesh):
    placed = (
        P(("grp", "row"), "tp", None),
        P(("grp", "row"), "tp", None, None),
        P(("grp", "row"), None),
        P(("grp", "row"), None),
        P(),
        P(None, "tp"),
        P(None, "tp"),
        P("tp", None),
        P(),
        P("row", None, "tp"),
        P("row", "tp", None),
        P("row", None, None),
        P("row", None),
    )
    return jax.shard_map(
        shards,
        mesh=mesh,
        in_specs=placed,
        out_specs=(
            P(("grp", "row"), "tp", None),
            P(("grp", "row"), None, None),
            P(("grp", "row"), None),
        ),
        check_vma=False,
    )
```

```python
import functools
import typing

import jax
import jax.numpy as jnp
from jax import lax
from jax.experimental import pallas as pl
from jax.experimental.pallas import tpu as pltpu
from jax.sharding import PartitionSpec as P

HD = 128
STEPS = 4
CAP = 2
EPS = 1e-05
MESH = pl.DeviceIdType.MESH
F32 = jnp.float32
BF16 = jnp.bfloat16
VMEM_LIMIT = 56 << 20


def rms_rows(values):
    return values * lax.rsqrt(jnp.mean(values * values, axis=-1, keepdims=True) + EPS)


def folded(rows):
    half = rows.shape[1] // 2
    return jnp.concatenate([rows[:, :half], rows[:, half:]], axis=0)


PAIR_COLUMNS = 512
PARTS = 2
FAR = {False: {1: 0, -1: 0, 2: 0, -2: 0, 3: 2, -3: -2, 4: 2}, True: {1: 0, -1: 0, 2: 0, -2: 0, 3: 2, -3: -2, -4: -2}}


BATCHES = ((0, 1, 2), (3,))


class Batch(typing.NamedTuple):
    steps: tuple
    outgoing: typing.Any
    arrived: typing.Any
    partial: typing.Any
    partial_in: typing.Any
    hidden: typing.Any
    answers: typing.Any
    returned: typing.Any
    a_send: typing.Any
    a_recv: typing.Any
    h_send: typing.Any
    h_recv: typing.Any
    g_send: typing.Any
    g_recv: typing.Any
    b_send: typing.Any
    b_recv: typing.Any


def due(tree, k):
    return 0.0 if k == 0 else due(tree, tree[k]) + 2.0 + 0.8 * abs(k - tree[k])


def below(tree, k):
    return sorted([c for c in tree if tree[c] == k], key=lambda c: abs(c - k))


def halves(product, half, width):
    return product.reshape(-1, 2, 8, width)[:, half].reshape(-1, width)


def fold_dot(first, second, weight):
    half = weight.shape[0] // 2
    columns = weight.shape[1]
    cut = first.shape[1]
    left = jnp.dot(first, weight[:cut], preferred_element_type=F32)
    left = left + jnp.dot(second, weight[cut:half], preferred_element_type=F32)
    right = jnp.dot(first, weight[half : half + cut], preferred_element_type=F32)
    right = right + jnp.dot(second, weight[half + cut :], preferred_element_type=F32)
    return halves(left, 0, columns) + halves(right, 1, columns)


def silu(values):
    return values / (1.0 + jnp.exp(-values))


def kernel(
    n_z,
    peers,
    frame_ref,
    actions_ref,
    owners_ref,
    gain_ref,
    table_ref,
    cache_hbm,
    wq_hbm,
    wkv_hbm,
    wo_hbm,
    pin_hbm,
    pmid_hbm,
    head_ref,
    critic_ref,
    latents_ref,
    logp_ref,
    value_ref,
    cache_ref,
    wq_ref,
    wkv_ref,
    wo_ref,
    pin_ref,
    pmid_ref,
    embed,
    state,
    gath_p,
    gath_q,
    qkv,
    qkv_in,
    keys,
    vals,
    scores,
    weights,
    own_o,
    out_o,
    in_o,
    terms_p,
    terms_q,
    tree_p,
    tree_q,
    pair_p,
    pair_q,
    latent_rows,
    ag_zs,
    ag_zr,
    ag_ys,
    ag_yr,
    rs_zs,
    rs_zr,
    rs_ys,
    rs_yr,
    q_send,
    q_recv,
    o_send,
    o_recv,
    l_send,
    l_recv,
    loaded,
    *batch_refs,
):
    batches = [Batch(steps, *batch_refs[i * 15 : (i + 1) * 15]) for i, steps in enumerate(BATCHES)]
    loads = [
        pltpu.make_async_copy(src, dst, loaded.at[i])
        for i, (src, dst) in enumerate(
            (
                (wq_hbm, wq_ref),
                (wkv_hbm, wkv_ref),
                (cache_hbm, cache_ref),
                (wo_hbm, wo_ref),
                (pin_hbm, pin_ref),
                (pmid_hbm, pmid_ref),
            )
        )
    ]
    for load in loads:
        load.start()
    tensor = lax.axis_index("tp")
    row = lax.axis_index("row")
    z = tensor // 2
    yh = lax.rem(tensor, 2)
    pair = {"tp": tensor + 1 - 2 * yh}
    rollouts, width = state.shape
    n_tensor = 2 * n_z
    tokens = n_tensor
    n_rows = tokens * rollouts
    cached = cache_ref.shape[2]
    last = n_tensor - 1
    cut = gath_p.shape[3]
    half = width // 2

    def plane(k):
        return lax.rem(z + k + 2 * n_z, n_z)

    def to_plane(k):
        return {"tp": plane(k) * 2 + yh}

    def slot_of(k, other):
        return plane(k) * 2 + (1 - yh if other else yh)

    def to_row(k):
        return {"row": lax.rem(row + k, peers)}

    def to_tensor(k):
        return {"tp": lax.rem(tensor + k, n_tensor)}

    barrier = pltpu.get_barrier_semaphore()
    for k in range(1, n_tensor):
        pl.semaphore_signal(barrier, inc=1, device_id=to_tensor(k), device_id_type=MESH)
    for k in range(1, peers):
        pl.semaphore_signal(barrier, inc=1, device_id=to_row(k), device_id_type=MESH)

    def copy(src, dst, send, recv, target):
        return pltpu.make_async_remote_copy(
            src_ref=src, dst_ref=dst, send_sem=send, recv_sem=recv, device_id=target, device_id_type=MESH
        )

    state[...] = frame_ref[...].astype(F32)
    keys[...] = jnp.zeros_like(keys)
    vals[...] = jnp.zeros_like(vals)
    iota_r = lax.broadcasted_iota(jnp.int32, (n_rows, n_rows), 0)
    iota_c = lax.broadcasted_iota(jnp.int32, (n_rows, n_rows), 1)
    by_rollout = (lax.rem(iota_r, tokens) * rollouts + iota_r // tokens == iota_c).astype(F32).astype(BF16)
    by_token = (lax.rem(iota_c, tokens) * rollouts + iota_c // tokens == iota_r).astype(F32).astype(BF16)

    eye = lax.broadcasted_iota(jnp.int32, (rollouts, rollouts), 0) == lax.broadcasted_iota(
        jnp.int32, (rollouts, rollouts), 1
    )
    owner = jnp.sum(jnp.where(eye, owners_ref[...], 0), axis=1, keepdims=True)
    hit = (lax.broadcasted_iota(jnp.int32, (rollouts, 128), 1) == owner).astype(F32)
    later = (
        lax.broadcasted_iota(jnp.int32, (rollouts, rollouts), 0)
        > lax.broadcasted_iota(jnp.int32, (rollouts, rollouts), 1)
    ).astype(F32)
    before = jnp.zeros((rollouts, 128), F32)
    for r in range(rollouts):
        before = before + later[:, r : r + 1] * hit[r : r + 1, :]
    place_of = jnp.sum(before * hit, axis=1, keepdims=True)
    eighths = 16 // CAP
    spots = peers * 16
    tn = (((0,), (0,)), ((), ()))
    nt = (((1,), (1,)), ((), ()))
    pl.semaphore_wait(barrier, peers + n_tensor - 2)

    def spread_across(q, piece, k):
        mine = latent_rows.at[q, piece]
        return copy(mine, mine, l_send.at[q, piece, k], l_recv.at[q, piece, 0], to_plane(k))

    def spread_pair(q, piece):
        mine = latent_rows.at[q, piece]
        return copy(mine, mine, l_send.at[q, piece, 0], l_recv.at[q, piece, 1], pair)

    far_first = sorted(range(1, n_z), key=lambda k: -min(k, n_z - k))
    pieces = range(latent_rows.shape[1])

    def spread_start(q):
        @pl.when(tensor == last)
        def _():
            for piece in pieces:
                for k in far_first:
                    spread_across(q, piece, k).start()
                spread_pair(q, piece).start()

    def spread_on(q):
        @pl.when((yh == 1) & (tensor != last))
        def _():
            for piece in pieces:
                spread_across(q, piece, 1).wait_recv()
                spread_pair(q, piece).start()

    def spread_end(q):
        @pl.when(yh == 0)
        def _():
            for piece in pieces:
                spread_pair(q, piece).wait_recv()

    def spread_sent(q):
        @pl.when(yh == 1)
        def _():
            for piece in pieces:
                spread_pair(q, piece).wait_send()

        @pl.when(tensor == last)
        def _():
            for piece in pieces:
                for k in far_first:
                    spread_across(q, piece, k).wait_send()

    def route(b, k):
        return copy(b.outgoing.at[lax.rem(row + k, peers)], b.arrived.at[row], b.a_send.at[k], b.a_recv.at[k], to_row(k))

    def route_build(b, numbers):
        wide = half // 4
        i = lax.broadcasted_iota(jnp.int32, (16, spots), 1)
        j = lax.broadcasted_iota(jnp.int32, (16, spots), 0)
        owner2 = jnp.concatenate([owner, owner], axis=0)
        place2 = jnp.concatenate([place_of, place_of], axis=0)
        chosen = (i // 16 == owner2) & (lax.rem(i, CAP).astype(F32) == place2)
        eighth = lax.rem(i // CAP, eighths)
        hots = [
            (chosen & (eighth == (j // rollouts) * 4 + quarter)).astype(F32).astype(BF16) for quarter in range(4)
        ]
        for n in numbers:
            q = b.steps[n]
            built = jnp.zeros((spots, wide), F32)
            for quarter in range(4):
                built = built + lax.dot_general(
                    hots[quarter],
                    latent_rows[q, quarter // 2, :, quarter % 2 * wide : (quarter % 2 + 1) * wide],
                    tn,
                    preferred_element_type=F32,
                )
            b.outgoing[:, n * 16 : (n + 1) * 16, :] = built.astype(BF16).reshape(peers, 16, wide)

    def route_start(b):
        for k in range(1, peers):
            route(b, k).start()
        b.arrived[row] = b.outgoing[row]

    def to_units(b, k):
        return copy(
            b.partial.at[lax.rem(tensor + k, n_tensor)], b.partial_in.at[k], b.h_send.at[k], b.h_recv.at[k], to_tensor(k)
        )

    def inner_start(b):
        for k in range(1, peers):
            origin = b.arrived.at[lax.rem(row + peers - k, peers)]
            copy(origin, origin, b.a_send.at[k], b.a_recv.at[k], to_row(k)).wait_recv()
        wide = half // 4
        tall = len(b.steps) * 16
        rows = b.arrived[...].reshape(peers * tall, wide)
        n_inner = pin_ref.shape[2]
        at_row = lax.rem(lax.broadcasted_iota(jnp.int32, (peers * tall, n_inner), 0) // CAP, eighths)
        picked = jnp.zeros((peers * tall, n_inner), F32)
        for e in range(eighths):
            product = jnp.dot(rows, pin_ref[0, e * wide : (e + 1) * wide, :], preferred_element_type=F32)
            picked = picked + jnp.where(at_row == e, product, 0.0)
        i = lax.broadcasted_iota(jnp.int32, (tall, peers * tall), 1)
        j = lax.broadcasted_iota(jnp.int32, (tall, peers * tall), 0)
        collect = (i // tall == lax.rem(j, 16) // CAP) & (lax.rem(i, tall) // 16 == j // 16)
        collect = (collect & (lax.rem(i, CAP) == lax.rem(j, CAP))).astype(F32)
        before_silu = jnp.dot(collect, picked, preferred_element_type=F32, precision=lax.Precision.HIGHEST)
        inner = silu(before_silu).astype(BF16)
        units = b.partial.shape[2]
        product = jnp.dot(inner, pmid_ref[0], preferred_element_type=F32).astype(BF16)
        for t in range(n_tensor):
            b.partial[t] = product[:, t * units : (t + 1) * units]
        for k in range(1, n_tensor):
            to_units(b, k).start()

    def share(b, k):
        mine = b.hidden.at[tensor]
        return copy(mine, mine, b.g_send.at[k], b.g_recv.at[k], to_tensor(k))

    def hidden_start(b):
        summed = b.partial[tensor].astype(F32)
        for k in range(1, n_tensor):
            to_units(b, k).wait_recv()
            summed = summed + b.partial_in[k].astype(F32)
        b.hidden[tensor] = silu(summed).astype(BF16)
        for k in range(1, n_tensor):
            share(b, k).start()

    def reply(b, k):
        return copy(b.answers, b.returned.at[row], b.b_send.at[k], b.b_recv.at[k], to_row(k))

    def heads_start(b):
        for k in range(1, n_tensor):
            origin = b.hidden.at[lax.rem(tensor + n_tensor - k, n_tensor)]
            copy(origin, origin, b.g_send.at[k], b.g_recv.at[k], to_tensor(k)).wait_recv()
        whole = jnp.concatenate([b.hidden[t] for t in range(n_tensor)], axis=1)
        logits = lax.dot_general(whole, head_ref[...], nt, preferred_element_type=F32)
        value = jnp.sum(whole.astype(F32) * critic_ref[...].astype(F32), axis=1, keepdims=True)
        peak = jnp.max(logits, axis=1, keepdims=True)
        logp = logits - (peak + jnp.log(jnp.sum(jnp.exp(logits - peak), axis=1, keepdims=True)))
        blank = jnp.zeros((logits.shape[0], 128 - logits.shape[1] - 1), F32)
        b.answers[...] = jnp.concatenate([logp, value, blank], axis=1)
        for k in range(1, peers):
            reply(b, k).start()
        b.returned[row] = b.answers[...]

    def replies_wait(b):
        for k in range(1, peers):
            origin = b.returned.at[lax.rem(row + peers - k, peers)]
            copy(origin, origin, b.b_send.at[k], b.b_recv.at[k], to_row(k)).wait_recv()

    def batch_sent(b):
        for k in range(1, peers):
            route(b, k).wait_send()
            reply(b, k).wait_send()
        for k in range(1, n_tensor):
            to_units(b, k).wait_send()
            share(b, k).wait_send()

    def gather(s):
        own, other, front = FAR[False], FAR[True], FAR[False]
        sent = []

        def block(stream, k):
            return (gath_q if stream == 2 else gath_p).at[s, slot_of(-k, stream == 1)]

        def go(ref, send, recv, target):
            moved = copy(ref, ref, send, recv, target)
            moved.start()
            sent.append(moved)

        def spread(stream, tree, k):
            for c in below(tree, k):
                go(block(stream, k), ag_zs.at[s, stream, c % n_z], ag_zr.at[s, stream, c % n_z], to_plane(c - k))

        def pass_on(k):
            go(block(2, k), ag_ys.at[s, k % n_z], ag_yr.at[s, k % n_z], pair)

        go(block(0, 0), ag_ys.at[s, n_z], ag_yr.at[s, n_z], pair)
        spread(2, front, 0)
        pass_on(0)
        spread(0, own, 0)
        events = [(due(front, k), 2, k) for k in front] + [(due(own, k), 0, k) for k in own]
        events += [(3.0 + due(other, k), 1, k) for k in [0] + list(other)]
        for _, stream, k in sorted(events):
            ref = block(stream, k)
            if k == 0:
                copy(ref, ref, ag_ys.at[s, n_z], ag_yr.at[s, n_z], pair).wait_recv()
            else:
                copy(ref, ref, ag_zs.at[s, stream, k % n_z], ag_zr.at[s, stream, k % n_z], pair).wait_recv()
            spread(stream, (own, other, front)[stream], k)
            if stream == 2:
                pass_on(k)
        for k in [0] + list(front):
            ref = gath_q.at[s, slot_of(-k, True)]
            copy(ref, ref, ag_ys.at[s, k % n_z], ag_yr.at[s, k % n_z], pair).wait_recv()
        return sent

    def scatter(s, hooks):
        trees = (FAR[False], FAR[True], FAR[False])
        sent = []

        def go(src, dst, send, recv, target):
            moved = copy(src, dst, send, recv, target)
            moved.start()
            sent.append(moved)

        for k in sorted(trees[2], key=lambda k: -due(trees[2], k)) + [0]:
            go(
                terms_q.at[slot_of(-k, True)],
                pair_q.at[s, k % n_z],
                rs_ys.at[s, k % n_z],
                rs_yr.at[s, k % n_z],
                pair,
            )
        deepest = max(due(trees[0], k) for k in trees[0])
        events = []
        for stream, offset in ((0, 1.0), (1, -0.1), (2, 3.0)):
            events += [(offset + deepest - due(trees[stream], k), stream, k) for k in [0] + list(trees[stream])]
        ends = {}
        for number, (_, stream, k) in enumerate(sorted(events)):
            if number in (0, len(events) // 2):
                hooks.pop(0)()
            tree = trees[stream]
            terms = terms_q if stream == 2 else terms_p
            slot = slot_of(-k, stream == 1)

            def landing(c):
                return tree_q.at[s, c % n_z] if stream == 2 else tree_p.at[s, stream, c % n_z]

            total = None
            children = below(tree, k)
            if stream == 2 or children or k == 0:
                total = terms[slot].astype(F32)
            if stream == 2:
                ref = pair_q.at[s, k % n_z]
                copy(ref, ref, rs_ys.at[s, k % n_z], rs_yr.at[s, k % n_z], pair).wait_recv()
                total = total + pair_q[s, k % n_z].astype(F32)
            for c in children:
                ref = landing(c)
                copy(ref, ref, rs_zs.at[s, stream, c % n_z], rs_zr.at[s, stream, c % n_z], pair).wait_recv()
                total = total + ref[...].astype(F32)
            if k:
                if total is not None:
                    terms[slot] = total.astype(BF16)
                go(
                    terms.at[slot],
                    landing(k),
                    rs_zs.at[s, stream, k % n_z],
                    rs_zr.at[s, stream, k % n_z],
                    to_plane(tree[k] - k),
                )
            elif stream == 1:
                terms[slot] = total.astype(BF16)
                go(terms.at[slot], pair_p.at[s], rs_ys.at[s, n_z], rs_yr.at[s, n_z], pair)
            else:
                ends[stream] = total
        ref = pair_p.at[s]
        copy(ref, ref, rs_ys.at[s, n_z], rs_yr.at[s, n_z], pair).wait_recv()
        first = ends[0] + pair_p[s].astype(F32)
        both = jnp.concatenate([first, ends[2]], axis=1)
        return jnp.concatenate([both[:rollouts], both[rollouts:]], axis=1), sent

    def embed_actions(s):
        at_step = lax.broadcasted_iota(jnp.int32, actions_ref.shape, 0) == s
        picked = jnp.sum(jnp.where(at_step, actions_ref[...], 0), axis=0, keepdims=True)
        code = lax.broadcasted_iota(jnp.int32, (table_ref.shape[0], rollouts), 0) == picked
        embed[...] = lax.dot_general(
            code.astype(F32).astype(BF16), table_ref[...], tn, preferred_element_type=F32
        )

    def step(s, carry):
        inputs = (state[...] + embed[...]).astype(BF16).astype(F32)
        state[...] = inputs
        normed = folded(rms_rows(inputs) * gain_ref[...]).astype(BF16)
        gath_p[s, tensor] = normed[:, :cut]
        gath_q[s, tensor] = normed[:, cut:]
        gathered = gather(s)

        @pl.when(s == 0)
        def _():
            for load in loads:
                load.wait()

        first = gath_p[s].reshape(n_tensor * 16, cut)
        second = gath_q[s].reshape(n_tensor * 16, half - cut)
        query = (fold_dot(first, second, wq_ref) * HD ** (-0.5)).astype(BF16)
        keyval = fold_dot(first, second, wkv_ref).astype(BF16)
        n_query = query.shape[1]
        qkv[s, :, :n_query] = jnp.dot(by_rollout, query, preferred_element_type=F32).astype(BF16)
        qkv[s, :, n_query:] = jnp.dot(by_rollout, keyval, preferred_element_type=F32).astype(BF16)
        part_rows = n_rows // PARTS

        def parted(n):
            return pl.ds(n * part_rows, part_rows)

        swaps = [
            copy(qkv.at[s, parted(n)], qkv_in.at[s, parted(n)], q_send.at[s, n], q_recv.at[s, n], pair)
            for n in range(PARTS)
        ]
        for swap in swaps:
            swap.start()

        heads = n_query // HD
        per = heads * tokens

        def grouped(source, r):
            rows = slice(r * tokens, (r + 1) * tokens)
            return jnp.concatenate([source[s, rows, h * HD : (h + 1) * HD] for h in range(heads)], axis=0)

        def band(r):
            return slice(r * per, (r + 1) * per)

        def score_cached(group, source, r):
            scores[group, band(r), :cached] = lax.dot_general(
                grouped(source, r), cache_ref[r, 0, :, :HD], nt, preferred_element_type=F32
            )

        def score_new(group, source, r):
            scores[group, band(r), cached:] = lax.dot_general(
                grouped(source, r), keys[r], nt, preferred_element_type=F32
            )

        for r in range(rollouts):
            score_cached(0, qkv, r)

        @pl.when(s > 0)
        def _():
            spread_start(s - 1)

        for moved in gathered:
            moved.wait_send()
        place = pl.ds(pl.multiple_of(s * tokens, tokens), tokens)

        def soften(group, low, high):
            fresh = scores[group, low:high, cached:]
            key_pos = lax.broadcasted_iota(jnp.int32, fresh.shape, 1)
            query_pos = lax.rem(lax.broadcasted_iota(jnp.int32, fresh.shape, 0), tokens)
            allowed = (key_pos <= s * tokens + query_pos) & (yh == 0)
            fresh = jnp.where(allowed, fresh, -jnp.inf)
            old = scores[group, low:high, :cached]
            top = jnp.maximum(jnp.max(old, axis=1, keepdims=True), jnp.max(fresh, axis=1, keepdims=True))
            old = jnp.exp(old - top)
            fresh = jnp.exp(fresh - top)
            total = jnp.sum(old, axis=1, keepdims=True) + jnp.sum(fresh, axis=1, keepdims=True)
            weights[group, low:high, :cached] = old.astype(BF16)
            weights[group, low:high, cached:] = fresh.astype(BF16)
            return top, total, 1.0 / total

        def attend(group, r, inverse):
            summed = jnp.dot(weights[group, band(r), :cached], cache_ref[r, 0, :, HD:], preferred_element_type=F32)
            summed = summed + jnp.dot(weights[group, band(r), cached:], vals[r], preferred_element_type=F32)
            return summed * inverse

        lane = lax.broadcasted_iota(jnp.int32, (tokens, HD), 1)
        sums = [
            copy(out_o.at[s, parted(n)], in_o.at[s, parted(n)], o_send.at[s, n], o_recv.at[s, n], pair)
            for n in range(PARTS)
        ]
        per_part = rollouts // PARTS
        for n in range(PARTS):
            swaps[n].wait_recv()
            here = slice(n * part_rows, (n + 1) * part_rows)
            own_kv = qkv[s, here, n_query:].astype(F32)
            other_kv = qkv_in[s, here, n_query:].astype(F32)
            new_key = jnp.where(yh == 0, own_kv, other_kv).astype(BF16)
            new_val = jnp.where(yh == 0, other_kv, own_kv).astype(BF16)
            for i in range(per_part):
                r = n * per_part + i
                rows = slice(i * tokens, (i + 1) * tokens)
                keys[r, place, :] = new_key[rows]
                vals[r, place, :] = new_val[rows]
                score_cached(1, qkv_in, r)
                score_new(1, qkv_in, r)
            far_top, far_total, inverse = soften(1, n * per_part * per, (n + 1) * per_part * per)
            for i in range(per_part):
                r = n * per_part + i
                rows = slice(r * tokens, (r + 1) * tokens)
                summed = attend(1, r, inverse[band(i)])
                stats = jnp.zeros((tokens, HD), F32)
                for h in range(heads):
                    at = slice(h * tokens, (h + 1) * tokens)
                    out_o[s, rows, h * HD : (h + 1) * HD] = summed[at].astype(BF16)
                    for first, column in ((8 * h, far_top), (8 * h + 3, far_total)):
                        left = column[band(i)][at]
                        for piece in range(3):
                            term = left.astype(BF16).astype(F32)
                            left = left - term
                            stats = jnp.where(lane == first + piece, term, stats)
                out_o[s, rows, n_query:] = stats.astype(BF16)
            sums[n].start()

        for r in range(rollouts):
            score_new(0, qkv, r)
        top, total, inverse = soften(0, 0, rollouts * per)
        for r in range(rollouts):
            rows = slice(r * tokens, (r + 1) * tokens)
            summed = attend(0, r, inverse[band(r)])
            for h in range(heads):
                own_o[rows, h * HD : (h + 1) * HD] = summed[h * tokens : (h + 1) * tokens]

        for n in (0, 1):

            @pl.when(s == n + 2)
            def _():
                route_build(batches[0], [n])

        embed_actions(s + 1)
        for swap in swaps:
            swap.wait_send()
        for swap in sums:
            swap.wait()

        stats = in_o[s, :, n_query:].astype(F32)
        top4 = top.reshape(rollouts, heads, tokens, 1)
        total4 = total.reshape(rollouts, heads, tokens, 1)
        joined = []
        for h in range(heads):
            pick = [stats[:, 8 * h + i : 8 * h + i + 1] for i in range(6)]
            far_top = pick[0] + pick[1] + pick[2]
            far_total = pick[3] + pick[4] + pick[5]
            near_top = top4[:, h].reshape(n_rows, 1)
            near_total = total4[:, h].reshape(n_rows, 1)
            peak = jnp.maximum(near_top, far_top)
            near = near_total * jnp.exp(near_top - peak)
            far = far_total * jnp.exp(far_top - peak)
            both = 1.0 / (near + far)
            cols = slice(h * HD, (h + 1) * HD)
            joined.append(own_o[:, cols] * (near * both) + in_o[s, :, cols].astype(F32) * (far * both))
        attended = jnp.concatenate(joined, axis=1).astype(BF16)
        attended = jnp.dot(by_token, attended, preferred_element_type=F32).astype(BF16)

        tile = 512 if half % 512 == 0 else HD
        for j in range(half // tile):
            at = slice(j * tile, (j + 1) * tile)
            also = slice(half + j * tile, half + (j + 1) * tile)
            left = jnp.dot(attended, wo_ref[:, at], preferred_element_type=F32).reshape(tokens, rollouts, tile)
            right = jnp.dot(attended, wo_ref[:, also], preferred_element_type=F32).reshape(tokens, rollouts, tile)
            part = jnp.concatenate([left, right], axis=1).astype(BF16)
            if j * tile < cut:
                terms_p[:, :, at] = part
            else:
                terms_q[:, :, j * tile - cut : (j + 1) * tile - cut] = part

        def spread_hook():
            @pl.when(s > 0)
            def _():
                spread_on(s - 1)

        def route_hook():
            @pl.when(s > 0)
            def _():
                spread_end(s - 1)

            @pl.when(s == STEPS - 1)
            def _():
                route_build(batches[0], [2])
                route_start(batches[0])

        reduced, sent = scatter(s, [spread_hook, route_hook])
        updated = (state[...] + reduced).astype(BF16).astype(F32)
        state[...] = updated

        @pl.when(tensor == last)
        def _():
            rows = folded(rms_rows(updated)).astype(BF16)
            latent_rows[s, 0] = rows[:, : half // 2]
            latent_rows[s, 1] = rows[:, half // 2 :]

        for moved in sent:
            moved.wait_send()
        return carry

    embed_actions(0)
    lax.fori_loop(0, STEPS, step, 0)
    final = STEPS - 1
    spread_start(final)
    inner_start(batches[0])
    spread_on(final)
    hidden_start(batches[0])
    spread_end(final)
    route_build(batches[1], [0])
    route_start(batches[1])
    heads_start(batches[0])
    latents_ref[...] = state[...].astype(BF16)
    inner_start(batches[1])
    for q in range(STEPS):
        spread_sent(q)
    hidden_start(batches[1])
    replies_wait(batches[0])
    heads_start(batches[1])
    for b in batches:
        batch_sent(b)
    replies_wait(batches[1])
    i = lax.broadcasted_iota(jnp.int32, (rollouts, spots), 1)
    mine = (i // 16 == owner) & (lax.rem(i, CAP).astype(F32) == place_of) & (lax.rem(i // CAP, eighths) == row)
    mine = mine.astype(F32)
    lane = lax.broadcasted_iota(jnp.int32, (rollouts, STEPS), 1)
    all_values = jnp.zeros((rollouts, STEPS), F32)
    n_actions = head_ref.shape[0]
    for q, b, n in [(q, b, n) for b in batches for n, q in enumerate(b.steps)]:
        now = jnp.dot(
            mine,
            b.returned[:, n * 16 : (n + 1) * 16, :].reshape(spots, 128),
            preferred_element_type=F32,
            precision=lax.Precision.HIGHEST,
        )
        logp_ref[:, q, :] = now[:, :n_actions]
        all_values = jnp.where(lane == q, now[:, n_actions : n_actions + 1], all_values)
    value_ref[...] = all_values


def shards(
    frame,
    cache,
    actions,
    owners,
    attn_gain,
    w_query,
    w_keyval,
    w_out,
    action_table,
    policy_in,
    policy_mid,
    policy_head,
    policy_value,
):
    n_tensor = lax.axis_size("tp")
    peers = lax.axis_size("row")
    n_z = n_tensor // 2
    rollouts, _, width = frame.shape
    half = width // 2
    n_rows = n_tensor * rollouts
    n_query = w_query.shape[1]
    wide = n_query + w_keyval.shape[1]
    cached = cache.shape[2]
    bands = n_rows * (n_query // HD)
    units = policy_mid.shape[2] // n_tensor
    cut = PAIR_COLUMNS
    vmem = pl.BlockSpec(memory_space=pltpu.VMEM)
    dma = pltpu.SemaphoreType.DMA

    def batch_scratch(count):
        tall = count * 16
        return (
            [pltpu.VMEM((peers, tall, half // 4), BF16)] * 2
            + [pltpu.VMEM((n_tensor, tall, units), BF16)] * 3
            + [pltpu.VMEM((tall, 128), F32), pltpu.VMEM((peers, tall, 128), F32)]
            + [dma((peers,))] * 2
            + [dma((n_tensor,))] * 4
            + [dma((peers,))] * 2
        )

    latents, log_probs, values = pl.pallas_call(
        functools.partial(kernel, n_z, peers),
        out_shape=(
            jax.ShapeDtypeStruct((rollouts, width), BF16),
            jax.ShapeDtypeStruct((rollouts, STEPS, policy_head.shape[2]), F32),
            jax.ShapeDtypeStruct((rollouts, STEPS), F32),
        ),
        in_specs=[vmem] * 5 + [pl.BlockSpec(memory_space=pl.ANY)] * 6 + [vmem] * 2,
        out_specs=(vmem,) * 3,
        scratch_shapes=[
            pltpu.VMEM(big.shape, BF16)
            for big in (cache, w_query, w_keyval, w_out, policy_in, policy_mid)
        ]
        + [
            pltpu.VMEM((rollouts, width), F32),
            pltpu.VMEM((rollouts, width), F32),
            pltpu.VMEM((STEPS, n_tensor, 16, cut), BF16),
            pltpu.VMEM((STEPS, n_tensor, 16, half - cut), BF16),
            pltpu.VMEM((STEPS, n_rows, wide), BF16),
            pltpu.VMEM((STEPS, n_rows, wide), BF16),
            pltpu.VMEM((rollouts, 128, HD), BF16),
            pltpu.VMEM((rollouts, 128, HD), BF16),
            pltpu.VMEM((2, bands, cached + 128), F32),
            pltpu.VMEM((2, bands, cached + 128), BF16),
            pltpu.VMEM((n_rows, n_query), F32),
            pltpu.VMEM((STEPS, n_rows, wide), BF16),
            pltpu.VMEM((STEPS, n_rows, wide), BF16),
            pltpu.VMEM((n_tensor, 16, cut), BF16),
            pltpu.VMEM((n_tensor, 16, half - cut), BF16),
            pltpu.VMEM((STEPS, 2, n_z, 16, cut), BF16),
            pltpu.VMEM((STEPS, n_z, 16, half - cut), BF16),
            pltpu.VMEM((STEPS, 16, cut), BF16),
            pltpu.VMEM((STEPS, n_z, 16, half - cut), BF16),
            pltpu.VMEM((STEPS, 2, 16, half // 2), BF16),
        ]
        + [dma((STEPS, 3, n_z))] * 2
        + [dma((STEPS, n_z + 1))] * 2
        + [dma((STEPS, 3, n_z))] * 2
        + [dma((STEPS, n_z + 1))] * 2
        + [dma((STEPS, PARTS))] * 4
        + [dma((STEPS, 2, n_z)), dma((STEPS, 2, 2))]
        + [dma((6,))]
        + [ref for steps in BATCHES for ref in batch_scratch(len(steps))],
        compiler_params=pltpu.CompilerParams(
            collective_id=0, has_side_effects=True, vmem_limit_bytes=VMEM_LIMIT
        ),
        name="imagine",
    )(
        frame.reshape(rollouts, width),
        actions.T,
        owners.T,
        attn_gain.reshape(1, width),
        action_table,
        cache,
        w_query,
        w_keyval,
        w_out,
        policy_in,
        policy_mid,
        policy_head.reshape(policy_head.shape[1:]).T,
        policy_value,
    )
    return (latents.reshape(frame.shape), log_probs, values)


def solution(mesh):
    placed = (
        P(("grp", "row"), "tp", None),
        P(("grp", "row"), "tp", None, None),
        P(("grp", "row"), None),
        P(("grp", "row"), None),
        P(),
        P(None, "tp"),
        P(None, "tp"),
        P("tp", None),
        P(),
        P("row", None, "tp"),
        P("row", "tp", None),
        P("row", None, None),
        P("row", None),
    )
    return jax.shard_map(
        shards,
        mesh=mesh,
        in_specs=placed,
        out_specs=(
            P(("grp", "row"), "tp", None),
            P(("grp", "row"), None, None),
            P(("grp", "row"), None),
        ),
        check_vma=False,
    )
```

```python
import functools
import typing

import jax
import jax.numpy as jnp
from jax import lax
from jax.experimental import pallas as pl
from jax.experimental.pallas import tpu as pltpu
from jax.sharding import PartitionSpec as P

HD = 128
STEPS = 4
CAP = 2
EPS = 1e-05
MESH = pl.DeviceIdType.MESH
F32 = jnp.float32
BF16 = jnp.bfloat16
VMEM_LIMIT = 56 << 20


def rms_rows(values):
    return values * lax.rsqrt(jnp.mean(values * values, axis=-1, keepdims=True) + EPS)


def folded(rows):
    half = rows.shape[1] // 2
    return jnp.concatenate([rows[:, :half], rows[:, half:]], axis=0)


PAIR_COLUMNS = 512
PARTS = 2
FAR = {False: {1: 0, -1: 0, 2: 0, -2: 0, 3: 2, -3: -2, 4: 2}, True: {1: 0, -1: 0, 2: 0, -2: 0, 3: 2, -3: -2, -4: -2}}


BATCHES = ((0, 1, 2), (3,))


class Batch(typing.NamedTuple):
    steps: tuple
    outgoing: typing.Any
    arrived: typing.Any
    partial: typing.Any
    partial_in: typing.Any
    hidden: typing.Any
    answers: typing.Any
    returned: typing.Any
    a_send: typing.Any
    a_recv: typing.Any
    h_send: typing.Any
    h_recv: typing.Any
    g_send: typing.Any
    g_recv: typing.Any
    b_send: typing.Any
    b_recv: typing.Any


def due(tree, k):
    return 0.0 if k == 0 else due(tree, tree[k]) + 2.0 + 0.8 * abs(k - tree[k])


def below(tree, k):
    return sorted([c for c in tree if tree[c] == k], key=lambda c: abs(c - k))


def halves(product, half, width):
    return product.reshape(-1, 2, 8, width)[:, half].reshape(-1, width)


def fold_dot(first, second, weight):
    half = weight.shape[0] // 2
    columns = weight.shape[1]
    cut = first.shape[1]
    left = jnp.dot(first, weight[:cut], preferred_element_type=F32)
    left = left + jnp.dot(second, weight[cut:half], preferred_element_type=F32)
    right = jnp.dot(first, weight[half : half + cut], preferred_element_type=F32)
    right = right + jnp.dot(second, weight[half + cut :], preferred_element_type=F32)
    return halves(left, 0, columns) + halves(right, 1, columns)


def silu(values):
    return values / (1.0 + jnp.exp(-values))


def kernel(
    n_z,
    peers,
    frame_ref,
    actions_ref,
    owners_ref,
    gain_ref,
    table_ref,
    cache_hbm,
    wq_hbm,
    wkv_hbm,
    wo_hbm,
    pin_hbm,
    pmid_hbm,
    head_ref,
    critic_ref,
    latents_ref,
    logp_ref,
    value_ref,
    cache_ref,
    wq_ref,
    wkv_ref,
    wo_ref,
    pin_ref,
    pmid_ref,
    embed,
    state,
    gath_p,
    gath_q,
    qkv,
    qkv_in,
    keys,
    vals,
    scores,
    weights,
    own_o,
    out_o,
    in_o,
    terms_p,
    terms_q,
    tree_p,
    tree_q,
    pair_p,
    pair_q,
    latent_rows,
    ag_zs,
    ag_zr,
    ag_ys,
    ag_yr,
    rs_zs,
    rs_zr,
    rs_ys,
    rs_yr,
    q_send,
    q_recv,
    o_send,
    o_recv,
    l_send,
    l_recv,
    loaded,
    *batch_refs,
):
    batches = [Batch(steps, *batch_refs[i * 15 : (i + 1) * 15]) for i, steps in enumerate(BATCHES)]
    loads = [
        pltpu.make_async_copy(src, dst, loaded.at[i])
        for i, (src, dst) in enumerate(
            (
                (wq_hbm, wq_ref),
                (wkv_hbm, wkv_ref),
                (cache_hbm, cache_ref),
                (wo_hbm, wo_ref),
                (pin_hbm, pin_ref),
                (pmid_hbm, pmid_ref),
            )
        )
    ]
    for load in loads:
        load.start()
    tensor = lax.axis_index("tp")
    row = lax.axis_index("row")
    z = tensor // 2
    yh = lax.rem(tensor, 2)
    pair = {"tp": tensor + 1 - 2 * yh}
    rollouts, width = state.shape
    n_tensor = 2 * n_z
    tokens = n_tensor
    n_rows = tokens * rollouts
    cached = cache_ref.shape[2]
    last = n_tensor - 1
    cut = gath_p.shape[3]
    half = width // 2

    def plane(k):
        return lax.rem(z + k + 2 * n_z, n_z)

    def to_plane(k):
        return {"tp": plane(k) * 2 + yh}

    def slot_of(k, other):
        return plane(k) * 2 + (1 - yh if other else yh)

    def to_row(k):
        return {"row": lax.rem(row + k, peers)}

    def to_tensor(k):
        return {"tp": lax.rem(tensor + k, n_tensor)}

    barrier = pltpu.get_barrier_semaphore()
    for k in range(1, n_tensor):
        pl.semaphore_signal(barrier, inc=1, device_id=to_tensor(k), device_id_type=MESH)
    for k in range(1, peers):
        pl.semaphore_signal(barrier, inc=1, device_id=to_row(k), device_id_type=MESH)

    def copy(src, dst, send, recv, target):
        return pltpu.make_async_remote_copy(
            src_ref=src, dst_ref=dst, send_sem=send, recv_sem=recv, device_id=target, device_id_type=MESH
        )

    state[...] = frame_ref[...].astype(F32)
    keys[...] = jnp.zeros_like(keys)
    vals[...] = jnp.zeros_like(vals)
    iota_r = lax.broadcasted_iota(jnp.int32, (n_rows, n_rows), 0)
    iota_c = lax.broadcasted_iota(jnp.int32, (n_rows, n_rows), 1)
    by_rollout = (lax.rem(iota_r, tokens) * rollouts + iota_r // tokens == iota_c).astype(F32).astype(BF16)
    by_token = (lax.rem(iota_c, tokens) * rollouts + iota_c // tokens == iota_r).astype(F32).astype(BF16)

    eye = lax.broadcasted_iota(jnp.int32, (rollouts, rollouts), 0) == lax.broadcasted_iota(
        jnp.int32, (rollouts, rollouts), 1
    )
    owner = jnp.sum(jnp.where(eye, owners_ref[...], 0), axis=1, keepdims=True)
    hit = (lax.broadcasted_iota(jnp.int32, (rollouts, 128), 1) == owner).astype(F32)
    later = (
        lax.broadcasted_iota(jnp.int32, (rollouts, rollouts), 0)
        > lax.broadcasted_iota(jnp.int32, (rollouts, rollouts), 1)
    ).astype(F32)
    before = jnp.zeros((rollouts, 128), F32)
    for r in range(rollouts):
        before = before + later[:, r : r + 1] * hit[r : r + 1, :]
    place_of = jnp.sum(before * hit, axis=1, keepdims=True)
    eighths = 16 // CAP
    spots = peers * 16
    tn = (((0,), (0,)), ((), ()))
    nt = (((1,), (1,)), ((), ()))
    pl.semaphore_wait(barrier, peers + n_tensor - 2)

    def spread_across(q, piece, k):
        mine = latent_rows.at[q, piece]
        return copy(mine, mine, l_send.at[q, piece, k], l_recv.at[q, piece, 0], to_plane(k))

    def spread_pair(q, piece):
        mine = latent_rows.at[q, piece]
        return copy(mine, mine, l_send.at[q, piece, 0], l_recv.at[q, piece, 1], pair)

    far_first = sorted(range(1, n_z), key=lambda k: -min(k, n_z - k))
    pieces = range(latent_rows.shape[1])

    def spread_start(q):
        @pl.when(tensor == last)
        def _():
            for piece in pieces:
                for k in far_first:
                    spread_across(q, piece, k).start()
                spread_pair(q, piece).start()

    def spread_on(q):
        @pl.when((yh == 1) & (tensor != last))
        def _():
            for piece in pieces:
                spread_across(q, piece, 1).wait_recv()
                spread_pair(q, piece).start()

    def spread_end(q):
        @pl.when(yh == 0)
        def _():
            for piece in pieces:
                spread_pair(q, piece).wait_recv()

    def spread_sent(q):
        @pl.when(yh == 1)
        def _():
            for piece in pieces:
                spread_pair(q, piece).wait_send()

        @pl.when(tensor == last)
        def _():
            for piece in pieces:
                for k in far_first:
                    spread_across(q, piece, k).wait_send()

    def route(b, k):
        return copy(b.outgoing.at[lax.rem(row + k, peers)], b.arrived.at[row], b.a_send.at[k], b.a_recv.at[k], to_row(k))

    def route_build(b, numbers):
        wide = half // 4
        i = lax.broadcasted_iota(jnp.int32, (16, spots), 1)
        j = lax.broadcasted_iota(jnp.int32, (16, spots), 0)
        owner2 = jnp.concatenate([owner, owner], axis=0)
        place2 = jnp.concatenate([place_of, place_of], axis=0)
        chosen = (i // 16 == owner2) & (lax.rem(i, CAP).astype(F32) == place2)
        eighth = lax.rem(i // CAP, eighths)
        hots = [
            (chosen & (eighth == (j // rollouts) * 4 + quarter)).astype(F32).astype(BF16) for quarter in range(4)
        ]
        for n in numbers:
            q = b.steps[n]
            built = jnp.zeros((spots, wide), F32)
            for quarter in range(4):
                built = built + lax.dot_general(
                    hots[quarter],
                    latent_rows[q, 0, :, quarter * wide : (quarter + 1) * wide],
                    tn,
                    preferred_element_type=F32,
                )
            b.outgoing[:, n * 16 : (n + 1) * 16, :] = built.astype(BF16).reshape(peers, 16, wide)

    def route_start(b):
        for k in range(1, peers):
            route(b, k).start()
        b.arrived[row] = b.outgoing[row]

    def to_units(b, k):
        return copy(
            b.partial.at[lax.rem(tensor + k, n_tensor)], b.partial_in.at[k], b.h_send.at[k], b.h_recv.at[k], to_tensor(k)
        )

    def inner_start(b):
        for k in range(1, peers):
            origin = b.arrived.at[lax.rem(row + peers - k, peers)]
            copy(origin, origin, b.a_send.at[k], b.a_recv.at[k], to_row(k)).wait_recv()
        wide = half // 4
        tall = len(b.steps) * 16
        rows = b.arrived[...].reshape(peers * tall, wide)
        n_inner = pin_ref.shape[2]
        at_row = lax.rem(lax.broadcasted_iota(jnp.int32, (peers * tall, n_inner), 0) // CAP, eighths)
        picked = jnp.zeros((peers * tall, n_inner), F32)
        for e in range(eighths):
            product = jnp.dot(rows, pin_ref[0, e * wide : (e + 1) * wide, :], preferred_element_type=F32)
            picked = picked + jnp.where(at_row == e, product, 0.0)
        i = lax.broadcasted_iota(jnp.int32, (tall, peers * tall), 1)
        j = lax.broadcasted_iota(jnp.int32, (tall, peers * tall), 0)
        collect = (i // tall == lax.rem(j, 16) // CAP) & (lax.rem(i, tall) // 16 == j // 16)
        collect = (collect & (lax.rem(i, CAP) == lax.rem(j, CAP))).astype(F32)
        before_silu = jnp.dot(collect, picked, preferred_element_type=F32, precision=lax.Precision.HIGHEST)
        inner = silu(before_silu).astype(BF16)
        units = b.partial.shape[2]
        product = jnp.dot(inner, pmid_ref[0], preferred_element_type=F32).astype(BF16)
        for t in range(n_tensor):
            b.partial[t] = product[:, t * units : (t + 1) * units]
        for k in range(1, n_tensor):
            to_units(b, k).start()

    def share(b, k):
        mine = b.hidden.at[tensor]
        return copy(mine, mine, b.g_send.at[k], b.g_recv.at[k], to_tensor(k))

    def hidden_start(b):
        summed = b.partial[tensor].astype(F32)
        for k in range(1, n_tensor):
            to_units(b, k).wait_recv()
            summed = summed + b.partial_in[k].astype(F32)
        b.hidden[tensor] = silu(summed).astype(BF16)
        for k in range(1, n_tensor):
            share(b, k).start()

    def reply(b, k):
        return copy(b.answers, b.returned.at[row], b.b_send.at[k], b.b_recv.at[k], to_row(k))

    def heads_start(b):
        for k in range(1, n_tensor):
            origin = b.hidden.at[lax.rem(tensor + n_tensor - k, n_tensor)]
            copy(origin, origin, b.g_send.at[k], b.g_recv.at[k], to_tensor(k)).wait_recv()
        whole = jnp.concatenate([b.hidden[t] for t in range(n_tensor)], axis=1)
        logits = lax.dot_general(whole, head_ref[...], nt, preferred_element_type=F32)
        value = jnp.sum(whole.astype(F32) * critic_ref[...].astype(F32), axis=1, keepdims=True)
        peak = jnp.max(logits, axis=1, keepdims=True)
        logp = logits - (peak + jnp.log(jnp.sum(jnp.exp(logits - peak), axis=1, keepdims=True)))
        blank = jnp.zeros((logits.shape[0], 128 - logits.shape[1] - 1), F32)
        b.answers[...] = jnp.concatenate([logp, value, blank], axis=1)
        for k in range(1, peers):
            reply(b, k).start()
        b.returned[row] = b.answers[...]

    def replies_wait(b):
        for k in range(1, peers):
            origin = b.returned.at[lax.rem(row + peers - k, peers)]
            copy(origin, origin, b.b_send.at[k], b.b_recv.at[k], to_row(k)).wait_recv()

    def batch_sent(b):
        for k in range(1, peers):
            route(b, k).wait_send()
            reply(b, k).wait_send()
        for k in range(1, n_tensor):
            to_units(b, k).wait_send()
            share(b, k).wait_send()

    def gather(s):
        own, other, front = FAR[False], FAR[True], FAR[False]
        sent = []

        def block(stream, k):
            return (gath_q if stream == 2 else gath_p).at[s, slot_of(-k, stream == 1)]

        def go(ref, send, recv, target):
            moved = copy(ref, ref, send, recv, target)
            moved.start()
            sent.append(moved)

        def spread(stream, tree, k):
            for c in below(tree, k):
                go(block(stream, k), ag_zs.at[s, stream, c % n_z], ag_zr.at[s, stream, c % n_z], to_plane(c - k))

        def pass_on(k):
            go(block(2, k), ag_ys.at[s, k % n_z], ag_yr.at[s, k % n_z], pair)

        go(block(0, 0), ag_ys.at[s, n_z], ag_yr.at[s, n_z], pair)
        spread(2, front, 0)
        pass_on(0)
        spread(0, own, 0)
        events = [(due(front, k), 2, k) for k in front] + [(due(own, k), 0, k) for k in own]
        events += [(3.0 + due(other, k), 1, k) for k in [0] + list(other)]
        for _, stream, k in sorted(events):
            ref = block(stream, k)
            if k == 0:
                copy(ref, ref, ag_ys.at[s, n_z], ag_yr.at[s, n_z], pair).wait_recv()
            else:
                copy(ref, ref, ag_zs.at[s, stream, k % n_z], ag_zr.at[s, stream, k % n_z], pair).wait_recv()
            spread(stream, (own, other, front)[stream], k)
            if stream == 2:
                pass_on(k)
        for k in [0] + list(front):
            ref = gath_q.at[s, slot_of(-k, True)]
            copy(ref, ref, ag_ys.at[s, k % n_z], ag_yr.at[s, k % n_z], pair).wait_recv()
        return sent

    def scatter(s, hooks):
        trees = (FAR[False], FAR[True], FAR[False])
        sent = []

        def go(src, dst, send, recv, target):
            moved = copy(src, dst, send, recv, target)
            moved.start()
            sent.append(moved)

        for k in sorted(trees[2], key=lambda k: -due(trees[2], k)) + [0]:
            go(
                terms_q.at[slot_of(-k, True)],
                pair_q.at[s, k % n_z],
                rs_ys.at[s, k % n_z],
                rs_yr.at[s, k % n_z],
                pair,
            )
        deepest = max(due(trees[0], k) for k in trees[0])
        events = []
        for stream, offset in ((0, 1.0), (1, -0.1), (2, 3.0)):
            events += [(offset + deepest - due(trees[stream], k), stream, k) for k in [0] + list(trees[stream])]
        ends = {}
        for number, (_, stream, k) in enumerate(sorted(events)):
            if number in (0, len(events) // 2):
                hooks.pop(0)()
            tree = trees[stream]
            terms = terms_q if stream == 2 else terms_p
            slot = slot_of(-k, stream == 1)

            def landing(c):
                return tree_q.at[s, c % n_z] if stream == 2 else tree_p.at[s, stream, c % n_z]

            total = None
            children = below(tree, k)
            if stream == 2 or children or k == 0:
                total = terms[slot].astype(F32)
            if stream == 2:
                ref = pair_q.at[s, k % n_z]
                copy(ref, ref, rs_ys.at[s, k % n_z], rs_yr.at[s, k % n_z], pair).wait_recv()
                total = total + pair_q[s, k % n_z].astype(F32)
            for c in children:
                ref = landing(c)
                copy(ref, ref, rs_zs.at[s, stream, c % n_z], rs_zr.at[s, stream, c % n_z], pair).wait_recv()
                total = total + ref[...].astype(F32)
            if k:
                if total is not None:
                    terms[slot] = total.astype(BF16)
                go(
                    terms.at[slot],
                    landing(k),
                    rs_zs.at[s, stream, k % n_z],
                    rs_zr.at[s, stream, k % n_z],
                    to_plane(tree[k] - k),
                )
            elif stream == 1:
                terms[slot] = total.astype(BF16)
                go(terms.at[slot], pair_p.at[s], rs_ys.at[s, n_z], rs_yr.at[s, n_z], pair)
            else:
                ends[stream] = total
        ref = pair_p.at[s]
        copy(ref, ref, rs_ys.at[s, n_z], rs_yr.at[s, n_z], pair).wait_recv()
        first = ends[0] + pair_p[s].astype(F32)
        both = jnp.concatenate([first, ends[2]], axis=1)
        return jnp.concatenate([both[:rollouts], both[rollouts:]], axis=1), sent

    def embed_actions(s):
        at_step = lax.broadcasted_iota(jnp.int32, actions_ref.shape, 0) == s
        picked = jnp.sum(jnp.where(at_step, actions_ref[...], 0), axis=0, keepdims=True)
        code = lax.broadcasted_iota(jnp.int32, (table_ref.shape[0], rollouts), 0) == picked
        embed[...] = lax.dot_general(
            code.astype(F32).astype(BF16), table_ref[...], tn, preferred_element_type=F32
        )

    def step(s, carry):
        inputs = (state[...] + embed[...]).astype(BF16).astype(F32)
        state[...] = inputs
        normed = folded(rms_rows(inputs) * gain_ref[...]).astype(BF16)
        gath_p[s, tensor] = normed[:, :cut]
        gath_q[s, tensor] = normed[:, cut:]
        gathered = gather(s)

        @pl.when(s == 0)
        def _():
            for load in loads:
                load.wait()

        first = gath_p[s].reshape(n_tensor * 16, cut)
        second = gath_q[s].reshape(n_tensor * 16, half - cut)
        query = (fold_dot(first, second, wq_ref) * HD ** (-0.5)).astype(BF16)
        keyval = fold_dot(first, second, wkv_ref).astype(BF16)
        n_query = query.shape[1]
        qkv[s, :, :n_query] = jnp.dot(by_rollout, query, preferred_element_type=F32).astype(BF16)
        qkv[s, :, n_query:] = jnp.dot(by_rollout, keyval, preferred_element_type=F32).astype(BF16)
        part_rows = n_rows // PARTS

        def parted(n):
            return pl.ds(n * part_rows, part_rows)

        swaps = [
            copy(qkv.at[s, parted(n)], qkv_in.at[s, parted(n)], q_send.at[s, n], q_recv.at[s, n], pair)
            for n in range(PARTS)
        ]
        for swap in swaps:
            swap.start()

        heads = n_query // HD
        per = heads * tokens

        def grouped(source, r):
            rows = slice(r * tokens, (r + 1) * tokens)
            return jnp.concatenate([source[s, rows, h * HD : (h + 1) * HD] for h in range(heads)], axis=0)

        def band(r):
            return slice(r * per, (r + 1) * per)

        def score_cached(group, source, r):
            scores[group, band(r), :cached] = lax.dot_general(
                grouped(source, r), cache_ref[r, 0, :, :HD], nt, preferred_element_type=F32
            )

        def score_new(group, source, r):
            scores[group, band(r), cached:] = lax.dot_general(
                grouped(source, r), keys[r], nt, preferred_element_type=F32
            )

        for r in range(rollouts):
            score_cached(0, qkv, r)

        @pl.when(s > 0)
        def _():
            spread_start(s - 1)

        for moved in gathered:
            moved.wait_send()
        place = pl.ds(pl.multiple_of(s * tokens, tokens), tokens)

        def soften(group, low, high):
            fresh = scores[group, low:high, cached:]
            key_pos = lax.broadcasted_iota(jnp.int32, fresh.shape, 1)
            query_pos = lax.rem(lax.broadcasted_iota(jnp.int32, fresh.shape, 0), tokens)
            allowed = (key_pos <= s * tokens + query_pos) & (yh == 0)
            fresh = jnp.where(allowed, fresh, -jnp.inf)
            old = scores[group, low:high, :cached]
            top = jnp.maximum(jnp.max(old, axis=1, keepdims=True), jnp.max(fresh, axis=1, keepdims=True))
            old = jnp.exp(old - top)
            fresh = jnp.exp(fresh - top)
            total = jnp.sum(old, axis=1, keepdims=True) + jnp.sum(fresh, axis=1, keepdims=True)
            weights[group, low:high, :cached] = old.astype(BF16)
            weights[group, low:high, cached:] = fresh.astype(BF16)
            return top, total, 1.0 / total

        def attend(group, r, inverse):
            summed = jnp.dot(weights[group, band(r), :cached], cache_ref[r, 0, :, HD:], preferred_element_type=F32)
            summed = summed + jnp.dot(weights[group, band(r), cached:], vals[r], preferred_element_type=F32)
            return summed * inverse

        lane = lax.broadcasted_iota(jnp.int32, (tokens, HD), 1)
        sums = [
            copy(out_o.at[s, parted(n)], in_o.at[s, parted(n)], o_send.at[s, n], o_recv.at[s, n], pair)
            for n in range(PARTS)
        ]
        per_part = rollouts // PARTS
        for n in range(PARTS):
            swaps[n].wait_recv()
            here = slice(n * part_rows, (n + 1) * part_rows)
            own_kv = qkv[s, here, n_query:].astype(F32)
            other_kv = qkv_in[s, here, n_query:].astype(F32)
            new_key = jnp.where(yh == 0, own_kv, other_kv).astype(BF16)
            new_val = jnp.where(yh == 0, other_kv, own_kv).astype(BF16)
            for i in range(per_part):
                r = n * per_part + i
                rows = slice(i * tokens, (i + 1) * tokens)
                keys[r, place, :] = new_key[rows]
                vals[r, place, :] = new_val[rows]
                score_cached(1, qkv_in, r)
                score_new(1, qkv_in, r)
            far_top, far_total, inverse = soften(1, n * per_part * per, (n + 1) * per_part * per)
            for i in range(per_part):
                r = n * per_part + i
                rows = slice(r * tokens, (r + 1) * tokens)
                summed = attend(1, r, inverse[band(i)])
                stats = jnp.zeros((tokens, HD), F32)
                for h in range(heads):
                    at = slice(h * tokens, (h + 1) * tokens)
                    out_o[s, rows, h * HD : (h + 1) * HD] = summed[at].astype(BF16)
                    for first, column in ((8 * h, far_top), (8 * h + 3, far_total)):
                        left = column[band(i)][at]
                        for piece in range(3):
                            term = left.astype(BF16).astype(F32)
                            left = left - term
                            stats = jnp.where(lane == first + piece, term, stats)
                out_o[s, rows, n_query:] = stats.astype(BF16)
            sums[n].start()

        for r in range(rollouts):
            score_new(0, qkv, r)
        top, total, inverse = soften(0, 0, rollouts * per)
        for r in range(rollouts):
            rows = slice(r * tokens, (r + 1) * tokens)
            summed = attend(0, r, inverse[band(r)])
            for h in range(heads):
                own_o[rows, h * HD : (h + 1) * HD] = summed[h * tokens : (h + 1) * tokens]

        for n in (0, 1):

            @pl.when(s == n + 2)
            def _():
                route_build(batches[0], [n])

        embed_actions(s + 1)
        for swap in swaps:
            swap.wait_send()
        for swap in sums:
            swap.wait()

        stats = in_o[s, :, n_query:].astype(F32)
        top4 = top.reshape(rollouts, heads, tokens, 1)
        total4 = total.reshape(rollouts, heads, tokens, 1)
        joined = []
        for h in range(heads):
            pick = [stats[:, 8 * h + i : 8 * h + i + 1] for i in range(6)]
            far_top = pick[0] + pick[1] + pick[2]
            far_total = pick[3] + pick[4] + pick[5]
            near_top = top4[:, h].reshape(n_rows, 1)
            near_total = total4[:, h].reshape(n_rows, 1)
            peak = jnp.maximum(near_top, far_top)
            near = near_total * jnp.exp(near_top - peak)
            far = far_total * jnp.exp(far_top - peak)
            both = 1.0 / (near + far)
            cols = slice(h * HD, (h + 1) * HD)
            joined.append(own_o[:, cols] * (near * both) + in_o[s, :, cols].astype(F32) * (far * both))
        attended = jnp.concatenate(joined, axis=1).astype(BF16)
        attended = jnp.dot(by_token, attended, preferred_element_type=F32).astype(BF16)

        tile = 512 if half % 512 == 0 else HD
        for j in range(half // tile):
            at = slice(j * tile, (j + 1) * tile)
            also = slice(half + j * tile, half + (j + 1) * tile)
            left = jnp.dot(attended, wo_ref[:, at], preferred_element_type=F32).reshape(tokens, rollouts, tile)
            right = jnp.dot(attended, wo_ref[:, also], preferred_element_type=F32).reshape(tokens, rollouts, tile)
            part = jnp.concatenate([left, right], axis=1).astype(BF16)
            if j * tile < cut:
                terms_p[:, :, at] = part
            else:
                terms_q[:, :, j * tile - cut : (j + 1) * tile - cut] = part

        def spread_hook():
            @pl.when(s > 0)
            def _():
                spread_on(s - 1)

        def route_hook():
            @pl.when(s > 0)
            def _():
                spread_end(s - 1)

            @pl.when(s == STEPS - 1)
            def _():
                route_build(batches[0], [2])
                route_start(batches[0])

        reduced, sent = scatter(s, [spread_hook, route_hook])
        updated = (state[...] + reduced).astype(BF16).astype(F32)
        state[...] = updated

        @pl.when(tensor == last)
        def _():
            latent_rows[s, 0] = folded(rms_rows(updated)).astype(BF16)

        for moved in sent:
            moved.wait_send()
        return carry

    embed_actions(0)
    lax.fori_loop(0, STEPS, step, 0)
    final = STEPS - 1
    spread_start(final)
    inner_start(batches[0])
    spread_on(final)
    hidden_start(batches[0])
    spread_end(final)
    route_build(batches[1], [0])
    route_start(batches[1])
    heads_start(batches[0])
    latents_ref[...] = state[...].astype(BF16)
    inner_start(batches[1])
    for q in range(STEPS):
        spread_sent(q)
    hidden_start(batches[1])
    replies_wait(batches[0])
    heads_start(batches[1])
    for b in batches:
        batch_sent(b)
    replies_wait(batches[1])
    i = lax.broadcasted_iota(jnp.int32, (rollouts, spots), 1)
    mine = (i // 16 == owner) & (lax.rem(i, CAP).astype(F32) == place_of) & (lax.rem(i // CAP, eighths) == row)
    mine = mine.astype(F32)
    lane = lax.broadcasted_iota(jnp.int32, (rollouts, STEPS), 1)
    all_values = jnp.zeros((rollouts, STEPS), F32)
    n_actions = head_ref.shape[0]
    for q, b, n in [(q, b, n) for b in batches for n, q in enumerate(b.steps)]:
        now = jnp.dot(
            mine,
            b.returned[:, n * 16 : (n + 1) * 16, :].reshape(spots, 128),
            preferred_element_type=F32,
            precision=lax.Precision.HIGHEST,
        )
        logp_ref[:, q, :] = now[:, :n_actions]
        all_values = jnp.where(lane == q, now[:, n_actions : n_actions + 1], all_values)
    value_ref[...] = all_values


def shards(
    frame,
    cache,
    actions,
    owners,
    attn_gain,
    w_query,
    w_keyval,
    w_out,
    action_table,
    policy_in,
    policy_mid,
    policy_head,
    policy_value,
):
    n_tensor = lax.axis_size("tp")
    peers = lax.axis_size("row")
    n_z = n_tensor // 2
    rollouts, _, width = frame.shape
    half = width // 2
    n_rows = n_tensor * rollouts
    n_query = w_query.shape[1]
    wide = n_query + w_keyval.shape[1]
    cached = cache.shape[2]
    bands = n_rows * (n_query // HD)
    units = policy_mid.shape[2] // n_tensor
    cut = PAIR_COLUMNS
    vmem = pl.BlockSpec(memory_space=pltpu.VMEM)
    dma = pltpu.SemaphoreType.DMA

    def batch_scratch(count):
        tall = count * 16
        return (
            [pltpu.VMEM((peers, tall, half // 4), BF16)] * 2
            + [pltpu.VMEM((n_tensor, tall, units), BF16)] * 3
            + [pltpu.VMEM((tall, 128), F32), pltpu.VMEM((peers, tall, 128), F32)]
            + [dma((peers,))] * 2
            + [dma((n_tensor,))] * 4
            + [dma((peers,))] * 2
        )

    latents, log_probs, values = pl.pallas_call(
        functools.partial(kernel, n_z, peers),
        out_shape=(
            jax.ShapeDtypeStruct((rollouts, width), BF16),
            jax.ShapeDtypeStruct((rollouts, STEPS, policy_head.shape[2]), F32),
            jax.ShapeDtypeStruct((rollouts, STEPS), F32),
        ),
        in_specs=[vmem] * 5 + [pl.BlockSpec(memory_space=pl.ANY)] * 6 + [vmem] * 2,
        out_specs=(vmem,) * 3,
        scratch_shapes=[
            pltpu.VMEM(big.shape, BF16)
            for big in (cache, w_query, w_keyval, w_out, policy_in, policy_mid)
        ]
        + [
            pltpu.VMEM((rollouts, width), F32),
            pltpu.VMEM((rollouts, width), F32),
            pltpu.VMEM((STEPS, n_tensor, 16, cut), BF16),
            pltpu.VMEM((STEPS, n_tensor, 16, half - cut), BF16),
            pltpu.VMEM((STEPS, n_rows, wide), BF16),
            pltpu.VMEM((STEPS, n_rows, wide), BF16),
            pltpu.VMEM((rollouts, 128, HD), BF16),
            pltpu.VMEM((rollouts, 128, HD), BF16),
            pltpu.VMEM((2, bands, cached + 128), F32),
            pltpu.VMEM((2, bands, cached + 128), BF16),
            pltpu.VMEM((n_rows, n_query), F32),
            pltpu.VMEM((STEPS, n_rows, wide), BF16),
            pltpu.VMEM((STEPS, n_rows, wide), BF16),
            pltpu.VMEM((n_tensor, 16, cut), BF16),
            pltpu.VMEM((n_tensor, 16, half - cut), BF16),
            pltpu.VMEM((STEPS, 2, n_z, 16, cut), BF16),
            pltpu.VMEM((STEPS, n_z, 16, half - cut), BF16),
            pltpu.VMEM((STEPS, 16, cut), BF16),
            pltpu.VMEM((STEPS, n_z, 16, half - cut), BF16),
            pltpu.VMEM((STEPS, 1, 16, half), BF16),
        ]
        + [dma((STEPS, 3, n_z))] * 2
        + [dma((STEPS, n_z + 1))] * 2
        + [dma((STEPS, 3, n_z))] * 2
        + [dma((STEPS, n_z + 1))] * 2
        + [dma((STEPS, PARTS))] * 4
        + [dma((STEPS, 1, n_z)), dma((STEPS, 1, 2))]
        + [dma((6,))]
        + [ref for steps in BATCHES for ref in batch_scratch(len(steps))],
        compiler_params=pltpu.CompilerParams(
            collective_id=0, has_side_effects=True, vmem_limit_bytes=VMEM_LIMIT
        ),
        name="imagine",
    )(
        frame.reshape(rollouts, width),
        actions.T,
        owners.T,
        attn_gain.reshape(1, width),
        action_table,
        cache,
        w_query,
        w_keyval,
        w_out,
        policy_in,
        policy_mid,
        policy_head.reshape(policy_head.shape[1:]).T,
        policy_value,
    )
    return (latents.reshape(frame.shape), log_probs, values)


def solution(mesh):
    placed = (
        P(("grp", "row"), "tp", None),
        P(("grp", "row"), "tp", None, None),
        P(("grp", "row"), None),
        P(("grp", "row"), None),
        P(),
        P(None, "tp"),
        P(None, "tp"),
        P("tp", None),
        P(),
        P("row", None, "tp"),
        P("row", "tp", None),
        P("row", None, None),
        P("row", None),
    )
    return jax.shard_map(
        shards,
        mesh=mesh,
        in_specs=placed,
        out_specs=(
            P(("grp", "row"), "tp", None),
            P(("grp", "row"), None, None),
            P(("grp", "row"), None),
        ),
        check_vma=False,
    )
```
